32 devices in a mesh: row: 8 (over y, x, core), col: 4 (over z).
Axes of the slice: x: 2, y: 2, z: 4, core: 2. Of those that a mesh axis runs over, the one named last changes fastest.
Arguments:
- tokens: bfloat16 [128, 12288], P('col', 'row'), may hold values from -6 to 6
- cotangent: bfloat16 [128, 12288], P('col', 'row'), may hold values from -1.5 to 1.5
- w_in: bfloat16 [12288, 24576], P('row', 'col'), may hold values from -0.0546875 to 0.0546875
- w_out: bfloat16 [24576, 12288], P('col', 'row'), may hold values from -0.0390625 to 0.0390625
Outputs:
- layer_out: bfloat16 [128, 12288], P('col', 'row')
- grad_tokens: bfloat16 [128, 12288], P('col', 'row')
- grad_w_in: bfloat16 [12288, 24576], P('row', 'col')
- grad_w_out: bfloat16 [24576, 12288], P('col', 'row')
The draws below stay inside these ranges and needn't reach their ends.
All inputs are finite; a program needn't handle non-finite values.
Results may differ from the reference program's by a relative error of at most 0.034.
Values may be sent and summed in bfloat16 or wider, within the bound.
No kernel may reach another device: no remote copies, remote signals or barrier semaphores. Data moves between devices by JAX's collectives and lax.ppermute only.
A program may use at most 128 MiB of HBM per device.

```python
import jax
import jax.numpy as jnp
from jax import lax

D = 12288
FFW = 24576
TOKENS = 128
N_ROW = 8
N_COL = 4


def with_spikes(result, own_key, source, target, shards_of, factor):
    owner, partner = [(jnp.arange(result.shape[axis_at]) // (result.shape[axis_at] // shards_of)).reshape([-1 if axis == axis_at else 1 for axis in range(result.ndim)]) for axis_at in (source, target)]
    chosen = jax.random.permutation(own_key, shards_of)[partner]
    strong = (owner == chosen) | (owner == (partner + shards_of // 2) % shards_of)
    return jnp.where(strong, factor * result, result)


def shard_levels(own_key, shape, shards, low, high):
    factor_of = 1.0
    for dim, shards_of in shards:
        draws = jax.random.uniform(jax.random.fold_in(jax.random.fold_in(own_key, 6), dim), (shards_of,), jnp.float32, low / len(shards), high / len(shards))
        factor_of = factor_of * jnp.repeat(jnp.exp(draws), shape[dim] // shards_of).reshape((-1,) + (1,) * (len(shape) - 1 - dim))
    return factor_of


def noise(stream_key, dims, scale, reach, shards=(), kind=jnp.bfloat16):
    drawn = scale * jax.random.normal(stream_key, dims, jnp.float32)
    if shards:
        drawn = drawn * shard_levels(stream_key, dims, shards, -0.22, 0.18)
    return jnp.clip(drawn, -reach, reach).astype(kind)


def gaussian_with(key, extent, spread, reach, split, heavy, held_as=jnp.bfloat16):
    drawn = spread * jax.random.normal(key, extent, jnp.float32)
    if split:
        drawn = drawn * shard_levels(key, extent, split, -0.22, 0.18)
    return jnp.clip(with_spikes(drawn, jax.random.fold_in(key, 3), *heavy), -reach, reach).astype(held_as)


def setup_inputs(seed: int = 0) -> dict:
    key_of = jax.random.split(jax.random.key(seed), 5)
    return {
        "tokens": gaussian_with(key_of[0], (TOKENS, D), 1.0, 6.0, ((0, 4), (1, 8)), (1, 0, 8, 2.0)),
        "cotangent": gaussian_with(key_of[1], (TOKENS, D), 0.25, 1.5, ((0, 4), (1, 8)), (1, 0, 8, 2.0)),
        "w_in": noise(key_of[2], (D, FFW), D ** -0.5, 0.0546875, ((0, 8), (1, 4))),
        "w_out": noise(key_of[3], (FFW, D), FFW ** -0.5, 0.0390625, ((0, 4), (1, 8))),
    }


def gelu_fn(value):
    return jax.nn.gelu(value, approximate=True)

def block_sum(left, right, width, count):

    def step(total, index):
        start = (index * width).astype(jnp.int32)
        part_left = lax.dynamic_slice_in_dim(left, start, width, 1)
        part_right = lax.dynamic_slice_in_dim(right, start, width, 0)
        term = jnp.dot(part_left, part_right, preferred_element_type=jnp.float32).astype(jnp.bfloat16)
        term = lax.optimization_barrier(term)
        return (total + term.astype(jnp.float32), None)
    start_total = jnp.zeros((left.shape[0], right.shape[1]), jnp.float32)
    total, unused = lax.scan(step, start_total, jnp.arange(count, dtype=jnp.int32))
    return total

def reference(tokens, cotangent, w_in, w_out):
    width_block = D // N_ROW
    hidden_block = FFW // N_COL
    hidden = block_sum(tokens, w_in, width_block, N_ROW)
    act = gelu_fn(hidden).astype(jnp.bfloat16)
    layer_out = block_sum(act, w_out, hidden_block, N_COL).astype(jnp.bfloat16)
    grad_act = block_sum(cotangent, w_out.T, width_block, N_ROW)
    unused, pullback = jax.vjp(gelu_fn, hidden)
    grad_hidden = pullback(grad_act)[0].astype(jnp.bfloat16)
    grad_w_out = jnp.dot(act.T, cotangent, preferred_element_type=jnp.float32).astype(jnp.bfloat16)
    grad_w_in = jnp.dot(tokens.T, grad_hidden, preferred_element_type=jnp.float32).astype(jnp.bfloat16)
    grad_tokens = block_sum(grad_hidden, w_in.T, hidden_block, N_COL).astype(jnp.bfloat16)
    return (layer_out, grad_tokens, grad_w_in, grad_w_out)
```

```python
import functools

import jax
import jax.numpy as jnp
from jax import lax
from jax.experimental import pallas as pl
from jax.experimental.pallas import tpu as pltpu
from jax.sharding import PartitionSpec as P

BF16 = jnp.bfloat16
F32 = jnp.float32
MIB = 1024 * 1024
VMEM_LIMIT = 48 * MIB


def gelu_fn(value):
    return jax.nn.gelu(value, approximate=True)


def gelu_back(hidden, grad_act):
    unused, pullback = jax.vjp(gelu_fn, hidden)
    return pullback(grad_act)[0].astype(BF16)


def swap(value, axis, flip, count):
    return lax.ppermute(value, axis, [(i, i ^ flip) for i in range(count)])


def dot(left, right, left_dim, right_dim):
    return lax.dot_general(
        left, right, (((left_dim,), (right_dim,)), ((), ())), preferred_element_type=F32
    )


def whole():
    return pl.BlockSpec(memory_space=pltpu.VMEM)


def project_kernel(count, right_dim, me_ref, *refs):
    pieces, (w_ref, keep_ref, send_ref, left) = refs[:count], refs[count:]
    step = pl.program_id(0)

    @pl.when(step == 0)
    def _():
        size = pieces[0].shape[0]
        for i, piece in enumerate(pieces):
            left[i * size : (i + 1) * size, :] = piece[...]

    out = dot(left[...], w_ref[...], 1, right_dim).astype(BF16)

    @pl.when(step % 2 == 0)
    def _():
        keep_ref[0] = out

    @pl.when(step % 2 == 1)
    def _():
        send_ref[0] = out


def project(me, pieces, weight, rows, by_rows):
    tokens = len(pieces) * pieces[0].shape[0]
    width = pieces[0].shape[1]
    hidden = weight.shape[0 if by_rows else 1]
    block = hidden // rows
    if by_rows:
        w_spec = pl.BlockSpec((block, width), lambda s, me: (me[0] ^ s, 0))
    else:
        w_spec = pl.BlockSpec((width, block), lambda s, me: (0, me[0] ^ s))
    out = jax.ShapeDtypeStruct((rows // 2, tokens, block), BF16)
    out_spec = pl.BlockSpec((1, tokens, block), lambda s, me: (s // 2, 0, 0))
    return pl.pallas_call(
        functools.partial(project_kernel, len(pieces), 1 if by_rows else 0),
        grid_spec=pltpu.PrefetchScalarGridSpec(
            num_scalar_prefetch=1,
            grid=(rows,),
            in_specs=[whole()] * len(pieces) + [w_spec],
            out_specs=[out_spec, out_spec],
            scratch_shapes=[pltpu.VMEM((tokens, width), BF16)],
        ),
        out_shape=[out, out],
        compiler_params=pltpu.CompilerParams(vmem_limit_bytes=VMEM_LIMIT),
        cost_estimate=pl.CostEstimate(
            flops=2 * tokens * width * hidden,
            bytes_accessed=2 * width * hidden + 2 * tokens * (width + hidden),
            transcendentals=0,
        ),
    )(me, *pieces, weight)


def back_kernel(rows, cols, by_rows, me_ref, *refs):
    blocks, refs = refs[:rows], refs[rows:]
    others, refs = refs[:cols], refs[cols:]
    w_ref, out_ref, grad_ref, act, other, total = refs
    step = pl.program_id(0)

    @pl.when(step == 0)
    def _():
        for i, block in enumerate(blocks):
            act[i] = block[...]
        size = others[0].shape[0]
        for i, piece in enumerate(others):
            other[i * size : (i + 1) * size, :] = piece[...]
        total[...] = jnp.zeros_like(total)

    value = act[step]
    total[...] += dot(value, w_ref[...], 1, 0 if by_rows else 1)
    if by_rows:
        grad_ref[...] = dot(value, other[...], 0, 0).astype(BF16)
    else:
        grad_ref[...] = dot(other[...], value, 0, 0).astype(BF16)

    @pl.when(step == rows - 1)
    def _():
        size = others[0].shape[0]
        for i in range(cols):
            out_ref[i] = total[i * size : (i + 1) * size, :].astype(BF16)


def back(me, blocks, others, weight, by_rows):
    rows, cols = len(blocks), len(others)
    tokens, block = blocks[0].shape
    size, width = others[0].shape
    hidden = rows * block
    if by_rows:
        w_spec = pl.BlockSpec((block, width), lambda s, me: (me[0] ^ s, 0))
    else:
        w_spec = pl.BlockSpec((width, block), lambda s, me: (0, me[0] ^ s))
    return pl.pallas_call(
        functools.partial(back_kernel, rows, cols, by_rows),
        grid_spec=pltpu.PrefetchScalarGridSpec(
            num_scalar_prefetch=1,
            grid=(rows,),
            in_specs=[whole()] * (rows + cols) + [w_spec],
            out_specs=[whole(), w_spec],
            scratch_shapes=[
                pltpu.VMEM((rows, tokens, block), BF16),
                pltpu.VMEM((tokens, width), BF16),
                pltpu.VMEM((tokens, width), F32),
            ],
        ),
        out_shape=[
            jax.ShapeDtypeStruct((cols, size, width), BF16),
            jax.ShapeDtypeStruct(weight.shape, BF16),
        ],
        compiler_params=pltpu.CompilerParams(vmem_limit_bytes=VMEM_LIMIT),
        cost_estimate=pl.CostEstimate(
            flops=4 * tokens * width * hidden,
            bytes_accessed=4 * width * hidden + 2 * tokens * (2 * width + hidden),
            transcendentals=0,
        ),
    )(me, *blocks, *others, weight)


def gather_col(piece, cols):
    return [piece] + [swap(piece, "col", q, cols) for q in range(1, cols)]


def scatter_row(keep, send, rows):
    got = swap(send, "row", 1, rows)
    pair = [keep[i].astype(F32) + got[i].astype(F32) for i in range(rows // 2)]
    total = pair[0]
    for i in range(1, rows // 2):
        total = total + swap(pair[i].astype(BF16), "row", 2 * i, rows).astype(F32)
    return total


def gather_row(share, rows):
    own = [share] + [swap(share, "row", 2 * i, rows) for i in range(1, rows // 2)]
    blocks = []
    for value in own:
        blocks += [value, swap(value, "row", 1, rows)]
    return blocks


def scatter_col(parts, cols):
    total = parts[0].astype(F32)
    for q in range(1, cols):
        total = total + swap(parts[q], "col", q, cols).astype(F32)
    return total.astype(BF16)


def blocked(rows, cols, tokens, cotangent, w_in, w_out):
    me = lax.axis_index("row").astype(jnp.int32).reshape(1)
    token_pieces = gather_col(tokens, cols)
    cot_pieces = gather_col(cotangent, cols)
    hidden = scatter_row(*project(me, token_pieces, w_in, rows, False), rows)
    grad_act = scatter_row(*project(me, cot_pieces, w_out, rows, True), rows)
    act = gather_row(gelu_fn(hidden).astype(BF16), rows)
    layer_parts, grad_w_out = back(me, act, cot_pieces, w_out, True)
    grad_hidden = gather_row(gelu_back(hidden, grad_act), rows)
    token_parts, grad_w_in = back(me, grad_hidden, token_pieces, w_in, False)
    layer_out = scatter_col(layer_parts, cols)
    grad_tokens = scatter_col(token_parts, cols)
    return (layer_out, grad_tokens, grad_w_in, grad_w_out)


def collective(tokens, cotangent, w_in, w_out):
    token_full = lax.all_gather(tokens, "col", axis=0, tiled=True)
    cot_full = lax.all_gather(cotangent, "col", axis=0, tiled=True)

    def over(value, axis):
        return lax.psum_scatter(value.astype(BF16), axis, scatter_dimension=0, tiled=True)

    hidden = over(dot(token_full, w_in, 1, 0), "row").astype(F32)
    grad_act = over(dot(cot_full, w_out, 1, 1), "row").astype(F32)
    act = lax.all_gather(gelu_fn(hidden).astype(BF16), "row", axis=0, tiled=True)
    grad_hidden = lax.all_gather(gelu_back(hidden, grad_act), "row", axis=0, tiled=True)
    layer_out = over(dot(act, w_out, 1, 0), "col")
    grad_tokens = over(dot(grad_hidden, w_in, 1, 1), "col")
    grad_w_in = dot(token_full, grad_hidden, 0, 0).astype(BF16)
    grad_w_out = dot(act, cot_full, 0, 0).astype(BF16)
    return (layer_out, grad_tokens, grad_w_in, grad_w_out)


def solution(mesh):
    rows, cols = mesh.shape["row"], mesh.shape["col"]

    def shards(tokens, cotangent, w_in, w_out):
        powers = rows & (rows - 1) == 0 and cols & (cols - 1) == 0
        if powers and rows > 1 and w_in.shape[1] % (rows * 128) == 0:
            return blocked(rows, cols, tokens, cotangent, w_in, w_out)
        return collective(tokens, cotangent, w_in, w_out)

    return jax.shard_map(
        shards,
        mesh=mesh,
        in_specs=(P("col", "row"), P("col", "row"), P("row", "col"), P("col", "row")),
        out_specs=(P("col", "row"), P("col", "row"), P("row", "col"), P("col", "row")),
        check_vma=False,
    )
```

```python
import functools

import jax
import jax.numpy as jnp
from jax import lax
from jax.experimental import pallas as pl
from jax.experimental.pallas import tpu as pltpu
from jax.sharding import PartitionSpec as P

BF16 = jnp.bfloat16
F32 = jnp.float32
MIB = 1024 * 1024
VMEM_LIMIT = 14 * MIB


def gelu_fn(value):
    return jax.nn.gelu(value, approximate=True)


def gelu_back(hidden, grad_act):
    unused, pullback = jax.vjp(gelu_fn, hidden)
    return pullback(grad_act)[0].astype(BF16)


def swap(value, axis, flip, count):
    return lax.ppermute(value, axis, [(i, i ^ flip) for i in range(count)])


def dot(left, right, left_dim, right_dim):
    return lax.dot_general(
        left, right, (((left_dim,), (right_dim,)), ((), ())), preferred_element_type=F32
    )


def whole():
    return pl.BlockSpec(memory_space=pltpu.VMEM)


def project_kernel(count, by_rows, me_ref, *refs):
    pieces, (source, held, keep_ref, send_ref, left, arrived) = refs[:count], refs[count:]
    me = me_ref[0]
    half, _, block = keep_ref.shape
    size = pieces[0].shape[0]

    def part(ref, r):
        at = pl.ds(pl.multiple_of((me ^ r) * block, 128), block)
        return ref.at[at, :] if by_rows else ref.at[:, at]

    def load(r):
        return pltpu.make_async_copy(part(source, r), part(held, r), arrived.at[r])

    for r in range(2 * half):
        load(r).start()
    for i, piece in enumerate(pieces):
        left[i * size : (i + 1) * size, :] = piece[...]

    def step(i, unused):
        for odd, out_ref in ((0, keep_ref), (1, send_ref)):
            r = 2 * i + odd
            load(r).wait()
            weight = part(held, r)[...]
            out_ref[i] = dot(left[...], weight, 1, 1 if by_rows else 0).astype(BF16)

    lax.fori_loop(0, half, step, None)


def project(me, pieces, weight, rows, by_rows):
    tokens = len(pieces) * pieces[0].shape[0]
    width = pieces[0].shape[1]
    hidden = weight.shape[0 if by_rows else 1]
    out = jax.ShapeDtypeStruct((rows // 2, tokens, hidden // rows), BF16)
    return pl.pallas_call(
        functools.partial(project_kernel, len(pieces), by_rows),
        in_specs=[pl.BlockSpec(memory_space=pltpu.SMEM)]
        + [whole()] * len(pieces)
        + [pl.BlockSpec(memory_space=pl.ANY)],
        out_specs=[whole()] * 3,
        scratch_shapes=[pltpu.VMEM((tokens, width), BF16), pltpu.SemaphoreType.DMA((rows,))],
        out_shape=[pltpu.VMEM(weight.shape, BF16), out, out],
        compiler_params=pltpu.CompilerParams(vmem_limit_bytes=VMEM_LIMIT),
        cost_estimate=pl.CostEstimate(
            flops=2 * tokens * width * hidden,
            bytes_accessed=2 * width * hidden + 2 * tokens * (width + hidden),
            transcendentals=0,
        ),
    )(me, *pieces, pltpu.with_memory_space_constraint(weight, pltpu.HBM))


def back_kernel(rows, cols, by_rows, me_ref, *refs):
    blocks, refs = refs[:rows], refs[rows:]
    others, refs = refs[:cols], refs[cols:]
    w_ref, refs = refs[0], refs[1:]
    outs, (grad_ref, act, other, total) = refs[:cols], refs[cols:]
    step = pl.program_id(0)

    @pl.when(step == 0)
    def _():
        for i, block in enumerate(blocks):
            act[i] = block[...]
        size = others[0].shape[0]
        for i, piece in enumerate(others):
            other[i * size : (i + 1) * size, :] = piece[...]
        total[...] = jnp.zeros_like(total)

    value = act[step]
    block = value.shape[1]
    at = pl.multiple_of((me_ref[0] ^ step) * block, 128)
    if by_rows:
        total[...] += dot(value, w_ref[pl.ds(at, block), :], 1, 0)
    else:
        total[...] += dot(value, w_ref[:, pl.ds(at, block)], 1, 1)
    if by_rows:
        grad_ref[...] = dot(value, other[...], 0, 0).astype(BF16)
    else:
        grad_ref[...] = dot(other[...], value, 0, 0).astype(BF16)

    @pl.when(step == rows - 1)
    def _():
        size = others[0].shape[0]
        for i, out_ref in enumerate(outs):
            out_ref[...] = total[i * size : (i + 1) * size, :].astype(BF16)


def back(me, blocks, others, weight, by_rows):
    rows, cols = len(blocks), len(others)
    tokens, block = blocks[0].shape
    size, width = others[0].shape
    hidden = rows * block
    if by_rows:
        w_spec = pl.BlockSpec((block, width), lambda s, me: (me[0] ^ s, 0))
    else:
        w_spec = pl.BlockSpec((width, block), lambda s, me: (0, me[0] ^ s))
    return pl.pallas_call(
        functools.partial(back_kernel, rows, cols, by_rows),
        grid_spec=pltpu.PrefetchScalarGridSpec(
            num_scalar_prefetch=1,
            grid=(rows,),
            in_specs=[whole()] * (rows + cols + 1),
            out_specs=[whole()] * cols + [w_spec],
            scratch_shapes=[
                pltpu.VMEM((rows, tokens, block), BF16),
                pltpu.VMEM((tokens, width), BF16),
                pltpu.VMEM((tokens, width), F32),
            ],
        ),
        out_shape=[jax.ShapeDtypeStruct((size, width), BF16)] * cols
        + [jax.ShapeDtypeStruct(weight.shape, BF16)],
        compiler_params=pltpu.CompilerParams(vmem_limit_bytes=VMEM_LIMIT),
        cost_estimate=pl.CostEstimate(
            flops=4 * tokens * width * hidden,
            bytes_accessed=4 * width * hidden + 2 * tokens * (2 * width + hidden),
            transcendentals=0,
        ),
    )(me, *blocks, *others, pltpu.with_memory_space_constraint(weight, pltpu.VMEM))


def gather_col(piece, cols):
    return [piece] + [swap(piece, "col", q, cols) for q in range(1, cols)]


def scatter_row(keep, send, rows):
    got = swap(send, "row", 1, rows)
    pair = [keep[i].astype(F32) + got[i].astype(F32) for i in range(rows // 2)]
    total = pair[0]
    for i in range(1, rows // 2):
        total = total + swap(pair[i].astype(BF16), "row", 2 * i, rows).astype(F32)
    return total


def gather_row(share, rows):
    own = [share] + [swap(share, "row", 2 * i, rows) for i in range(1, rows // 2)]
    blocks = []
    for value in own:
        blocks += [value, swap(value, "row", 1, rows)]
    return blocks


def scatter_col(parts, cols):
    total = parts[0].astype(F32)
    for q in range(1, cols):
        total = total + swap(parts[q], "col", q, cols).astype(F32)
    return total.astype(BF16)


def blocked(rows, cols, tokens, cotangent, w_in, w_out):
    me = lax.axis_index("row").astype(jnp.int32).reshape(1)
    token_pieces = gather_col(tokens, cols)
    cot_pieces = gather_col(cotangent, cols)
    w_in, *shares = project(me, token_pieces, w_in, rows, False)
    hidden = scatter_row(*shares, rows)
    w_out, *shares = project(me, cot_pieces, w_out, rows, True)
    grad_act = scatter_row(*shares, rows)
    act = gelu_fn(hidden).astype(BF16)
    hidden, act = lax.optimization_barrier((hidden, act))
    act = gather_row(act, rows)
    *layer_parts, grad_w_out = back(me, act, cot_pieces, w_out, True)
    grad_hidden = gather_row(gelu_back(hidden, grad_act), rows)
    *token_parts, grad_w_in = back(me, grad_hidden, token_pieces, w_in, False)
    layer_out = scatter_col(layer_parts, cols)
    grad_tokens = scatter_col(token_parts, cols)
    return (layer_out, grad_tokens, grad_w_in, grad_w_out)


def collective(tokens, cotangent, w_in, w_out):
    token_full = lax.all_gather(tokens, "col", axis=0, tiled=True)
    cot_full = lax.all_gather(cotangent, "col", axis=0, tiled=True)

    def over(value, axis):
        return lax.psum_scatter(value.astype(BF16), axis, scatter_dimension=0, tiled=True)

    hidden = over(dot(token_full, w_in, 1, 0), "row").astype(F32)
    grad_act = over(dot(cot_full, w_out, 1, 1), "row").astype(F32)
    act = lax.all_gather(gelu_fn(hidden).astype(BF16), "row", axis=0, tiled=True)
    grad_hidden = lax.all_gather(gelu_back(hidden, grad_act), "row", axis=0, tiled=True)
    layer_out = over(dot(act, w_out, 1, 0), "col")
    grad_tokens = over(dot(grad_hidden, w_in, 1, 1), "col")
    grad_w_in = dot(token_full, grad_hidden, 0, 0).astype(BF16)
    grad_w_out = dot(act, cot_full, 0, 0).astype(BF16)
    return (layer_out, grad_tokens, grad_w_in, grad_w_out)


def solution(mesh):
    rows, cols = mesh.shape["row"], mesh.shape["col"]

    def shards(tokens, cotangent, w_in, w_out):
        powers = rows & (rows - 1) == 0 and cols & (cols - 1) == 0
        if powers and rows > 1 and w_in.shape[1] % (rows * 128) == 0:
            return blocked(rows, cols, tokens, cotangent, w_in, w_out)
        return collective(tokens, cotangent, w_in, w_out)

    return jax.shard_map(
        shards,
        mesh=mesh,
        in_specs=(P("col", "row"), P("col", "row"), P("row", "col"), P("col", "row")),
        out_specs=(P("col", "row"), P("col", "row"), P("row", "col"), P("col", "row")),
        check_vma=False,
    )
```

```python
import functools

import jax
import jax.numpy as jnp
from jax import lax
from jax.experimental import pallas as pl
from jax.experimental.pallas import tpu as pltpu
from jax.sharding import PartitionSpec as P

BF16 = jnp.bfloat16
F32 = jnp.float32
VMEM_LIMIT = 12 * 1024 * 1024


def gelu_fn(value):
    return jax.nn.gelu(value, approximate=True)


def gelu_back(hidden, grad_act):
    unused, pullback = jax.vjp(gelu_fn, hidden)
    return pullback(grad_act)[0].astype(BF16)


def swap(value, axis, flip, count):
    return lax.ppermute(value, axis, [(i, i ^ flip) for i in range(count)])


def dot(left, right, left_dim, right_dim):
    return lax.dot_general(
        left, right, (((left_dim,), (right_dim,)), ((), ())), preferred_element_type=F32
    )


def whole():
    return pl.BlockSpec(memory_space=pltpu.VMEM)


def anywhere(count):
    return [pl.BlockSpec(memory_space=pl.ANY)] * count


def cost(flops, moved):
    return pl.CostEstimate(flops=flops, bytes_accessed=moved, transcendentals=0)


def join(pieces, out):
    at = 0
    for piece in pieces:
        out[at : at + piece.shape[0], :] = piece[...]
        at += piece.shape[0]


def project_kernel(count, afters, chips, by_rows, me_ref, *refs):
    pieces, refs = refs[:count], refs[count:]
    source, refs = refs[0], refs[1 + afters :]
    held, keeps, (send, left, arrived) = refs[0], refs[1:-3], refs[-3:]
    me = me_ref[0]
    block = send.shape[2]

    def load(i, odd):
        r = 2 * chips[i] + odd
        at = pl.ds(pl.multiple_of((me ^ r) * block, 128), block)
        part = source.at[at, :] if by_rows else source.at[:, at]
        return pltpu.make_async_copy(part, held.at[2 * i + odd], arrived.at[2 * i + odd])

    order = [(i, odd) for i in range(len(chips)) for odd in (1, 0)]
    for at in order:
        load(*at).start()
    join(pieces, left)
    for i, odd in order:
        load(i, odd).wait()
        out = dot(left[...], held[2 * i + odd], 1, 1 if by_rows else 0).astype(BF16)
        if odd:
            send[i] = out
        else:
            keeps[i][...] = out


def project(me, pieces, weight, rows, chips, by_rows, after=()):
    tokens = sum(piece.shape[0] for piece in pieces)
    width = pieces[0].shape[1]
    block = weight.shape[0 if by_rows else 1] // rows
    count = 2 * len(chips)
    held = (count, block, width) if by_rows else (count, width, block)
    held, *keeps, send = pl.pallas_call(
        functools.partial(project_kernel, len(pieces), len(after), chips, by_rows),
        in_specs=[pl.BlockSpec(memory_space=pltpu.SMEM)]
        + [whole()] * len(pieces)
        + anywhere(1 + len(after)),
        out_specs=[whole()] * (len(chips) + 2),
        scratch_shapes=[pltpu.VMEM((tokens, width), BF16), pltpu.SemaphoreType.DMA((count,))],
        out_shape=[pltpu.VMEM(held, BF16)]
        + [jax.ShapeDtypeStruct((tokens, block), BF16)] * len(chips)
        + [jax.ShapeDtypeStruct((len(chips), tokens, block), BF16)],
        compiler_params=pltpu.CompilerParams(vmem_limit_bytes=VMEM_LIMIT),
        cost_estimate=cost(2 * tokens * width * block * count, 2 * width * block * count),
    )(me, *pieces, pltpu.with_memory_space_constraint(weight, pltpu.HBM), *after)
    return held, keeps, send


def sum_kernel(sizes, afters, by_rows, *refs):
    rows = sum(sizes)
    blocks, helds, refs = refs[:rows], refs[rows : rows + len(sizes)], refs[rows + len(sizes) :]
    outs, total = refs[afters:-1], refs[-1]
    r = 0
    for held, size in zip(helds, sizes):
        for i in range(size):
            part = dot(blocks[r][...], held[i], 1, 0 if by_rows else 1)
            total[...] = part if r == 0 else total[...] + part
            r += 1
    size = outs[0].shape[0]
    for i, out in enumerate(outs):
        out[...] = total[i * size : (i + 1) * size, :].astype(BF16)


def block_sum(blocks, helds, cols, by_rows, after=()):
    tokens, block = blocks[0].shape
    width = helds[0].shape[2 if by_rows else 1]
    sizes = [held.shape[0] for held in helds]
    rows = len(blocks)
    helds = [pltpu.with_memory_space_constraint(held, pltpu.VMEM) for held in helds]
    return pl.pallas_call(
        functools.partial(sum_kernel, sizes, len(after), by_rows),
        in_specs=[whole()] * (rows + len(sizes)) + anywhere(len(after)),
        out_specs=[whole()] * cols,
        scratch_shapes=[pltpu.VMEM((tokens, width), F32)],
        out_shape=[jax.ShapeDtypeStruct((tokens // cols, width), BF16)] * cols,
        compiler_params=pltpu.CompilerParams(vmem_limit_bytes=VMEM_LIMIT),
        cost_estimate=cost(2 * tokens * width * block * rows, 2 * width * block * rows),
    )(*blocks, *helds, *after)


def grad_kernel(rows, count, by_rows, me_ref, *refs):
    blocks, pieces, refs = refs[:rows], refs[rows : rows + count], refs[rows + count :]
    grad, value, other = refs[-3:]
    step = pl.program_id(0)

    @pl.when(step == 0)
    def _():
        for i, block in enumerate(blocks):
            value[i] = block[...]
        join(pieces, other)

    if by_rows:
        grad[...] = dot(value[step], other[...], 0, 0).astype(BF16)
    else:
        grad[...] = dot(other[...], value[step], 0, 0).astype(BF16)


def weight_grad(me, blocks, pieces, by_rows, after=()):
    rows = len(blocks)
    tokens, block = blocks[0].shape
    width = pieces[0].shape[1]
    if by_rows:
        shape, spec = (rows * block, width), pl.BlockSpec((block, width), lambda s, me: (me[0] ^ s, 0))
    else:
        shape, spec = (width, rows * block), pl.BlockSpec((width, block), lambda s, me: (0, me[0] ^ s))
    return pl.pallas_call(
        functools.partial(grad_kernel, rows, len(pieces), by_rows),
        grid_spec=pltpu.PrefetchScalarGridSpec(
            num_scalar_prefetch=1,
            grid=(rows,),
            in_specs=[whole()] * (rows + len(pieces)) + anywhere(len(after)),
            out_specs=spec,
            scratch_shapes=[
                pltpu.VMEM((rows, tokens, block), BF16),
                pltpu.VMEM((tokens, width), BF16),
            ],
        ),
        out_shape=jax.ShapeDtypeStruct(shape, BF16),
        compiler_params=pltpu.CompilerParams(vmem_limit_bytes=VMEM_LIMIT),
        cost_estimate=cost(2 * tokens * width * block * rows, 2 * width * block * rows),
    )(me, *blocks, *pieces, *after)


def gather_col(piece, cols):
    pieces, flip, held = [piece], cols // 2, piece
    while flip:
        held = pieces[0] if len(pieces) == 1 else jnp.concatenate(pieces)
        pieces.append(swap(held, "col", flip, cols))
        flip //= 2
    return pieces, held


def col_order(cols):
    order, flip = [0], cols // 2
    while flip:
        order += [q ^ flip for q in order]
        flip //= 2
    return order


def pair_sums(keeps, send, chips, rows):
    got = swap(send, "row", 1, rows)
    return {
        chip: keep.astype(F32) + got[i].astype(F32)
        for i, (chip, keep) in enumerate(zip(chips, keeps))
    }


def gather_row(share, rows):
    own = [share] + [swap(share, "row", 2 * i, rows) for i in range(1, rows // 2)]
    blocks = []
    for value in own:
        blocks += [value, swap(value, "row", 1, rows)]
    return blocks


def scatter_col(parts, cols):
    parts = dict(zip(col_order(cols), parts))
    total = parts[0].astype(F32)
    for q in range(cols - 1, 0, -1):
        total = total + swap(parts[q], "col", q, cols).astype(F32)
    return total.astype(BF16)


def blocked(rows, cols, tokens, cotangent, w_in, w_out):
    me = lax.axis_index("row").astype(jnp.int32).reshape(1)
    chips = list(range(rows // 2))
    far, near = chips[len(chips) // 2 :], chips[: len(chips) // 2]
    token_pieces, unused = gather_col(tokens, cols)
    cot_pieces, cot_sent = gather_col(cotangent, cols)

    held_in, held_out, sums = [], [], []
    afters = [(cot_sent,), (cot_pieces[-1],)]
    for pieces, weight, helds, by_rows in (
        (token_pieces, w_in, held_in, False),
        (cot_pieces, w_out, held_out, True),
    ):
        total = None
        pairs = {}
        for half in (far, near):
            held, keeps, send = project(me, pieces, weight, rows, half, by_rows, afters.pop(0))
            helds.insert(0, held)
            pairs.update(pair_sums(keeps, send, half, rows))
        travel = {chip: pairs[chip].astype(BF16) for chip in chips[1:]}
        afters = [tuple(travel[chip] for chip in far), ()]
        total = pairs[0]
        for chip in reversed(chips[1:]):
            total = total + swap(travel[chip], "row", 2 * chip, rows).astype(F32)
        sums.append(total)
    hidden, grad_act = sums

    act = gelu_fn(hidden).astype(BF16)
    hidden, act = lax.optimization_barrier((hidden, act))
    act = gather_row(act, rows)
    grad_hidden = gather_row(gelu_back(hidden, grad_act), rows)

    layer_parts = block_sum(act, held_out, cols, True)
    grad_w_out = weight_grad(me, act, cot_pieces, True)
    hbm_grad = pltpu.with_memory_space_constraint(grad_w_out, pltpu.HBM)
    token_parts = block_sum(grad_hidden, held_in, cols, False, (hbm_grad,))
    grad_w_in = weight_grad(me, grad_hidden, token_pieces, False, token_parts)
    layer_out = scatter_col(layer_parts, cols)
    grad_tokens = scatter_col(token_parts, cols)
    return (layer_out, grad_tokens, grad_w_in, grad_w_out)


def collective(tokens, cotangent, w_in, w_out):
    token_full = lax.all_gather(tokens, "col", axis=0, tiled=True)
    cot_full = lax.all_gather(cotangent, "col", axis=0, tiled=True)

    def over(value, axis):
        return lax.psum_scatter(value.astype(BF16), axis, scatter_dimension=0, tiled=True)

    hidden = over(dot(token_full, w_in, 1, 0), "row").astype(F32)
    grad_act = over(dot(cot_full, w_out, 1, 1), "row").astype(F32)
    act = lax.all_gather(gelu_fn(hidden).astype(BF16), "row", axis=0, tiled=True)
    grad_hidden = lax.all_gather(gelu_back(hidden, grad_act), "row", axis=0, tiled=True)
    layer_out = over(dot(act, w_out, 1, 0), "col")
    grad_tokens = over(dot(grad_hidden, w_in, 1, 1), "col")
    grad_w_in = dot(token_full, grad_hidden, 0, 0).astype(BF16)
    grad_w_out = dot(act, cot_full, 0, 0).astype(BF16)
    return (layer_out, grad_tokens, grad_w_in, grad_w_out)


def solution(mesh):
    rows, cols = mesh.shape["row"], mesh.shape["col"]

    def shards(tokens, cotangent, w_in, w_out):
        powers = rows & (rows - 1) == 0 and cols & (cols - 1) == 0
        if powers and rows > 2 and w_in.shape[1] % (rows * 128) == 0:
            return blocked(rows, cols, tokens, cotangent, w_in, w_out)
        return collective(tokens, cotangent, w_in, w_out)

    return jax.shard_map(
        shards,
        mesh=mesh,
        in_specs=(P("col", "row"), P("col", "row"), P("row", "col"), P("col", "row")),
        out_specs=(P("col", "row"), P("col", "row"), P("row", "col"), P("col", "row")),
        check_vma=False,
    )
```

```python
import functools

import jax
import jax.numpy as jnp
from jax import lax
from jax.experimental import pallas as pl
from jax.experimental.pallas import tpu as pltpu
from jax.sharding import PartitionSpec as P

BF16 = jnp.bfloat16
F32 = jnp.float32
VMEM_LIMIT = 10 * 1024 * 1024
WRITES = 6


def gelu_fn(value):
    return jax.nn.gelu(value, approximate=True)


def gelu_back(hidden, grad_act):
    unused, pullback = jax.vjp(gelu_fn, hidden)
    return pullback(grad_act)[0].astype(BF16)


def swap(value, axis, flip, count):
    return lax.ppermute(value, axis, [(i, i ^ flip) for i in range(count)])


def dot(left, right, left_dim, right_dim):
    return lax.dot_general(
        left, right, (((left_dim,), (right_dim,)), ((), ())), preferred_element_type=F32
    )


def call(kernel, arrays, outs, flops, moved, after=(), scratch=()):
    spaces = {"smem": pltpu.SMEM, "vmem": pltpu.VMEM, "hbm": pl.ANY}
    operands = []
    for space, value in arrays:
        if space != "smem":
            value = pltpu.with_memory_space_constraint(
                value, pltpu.HBM if space == "hbm" else pltpu.VMEM
            )
        operands.append(value)
    return pl.pallas_call(
        kernel,
        in_specs=[pl.BlockSpec(memory_space=spaces[space]) for space, value in arrays]
        + [pl.BlockSpec(memory_space=pl.ANY)] * len(after),
        out_specs=[pl.BlockSpec(memory_space=spaces[space]) for space, value in outs],
        scratch_shapes=list(scratch),
        out_shape=[
            pltpu.VMEM(shape, dtype) if space == "vmem" else jax.ShapeDtypeStruct(shape, dtype)
            for space, (shape, dtype) in outs
        ],
        compiler_params=pltpu.CompilerParams(vmem_limit_bytes=VMEM_LIMIT),
        cost_estimate=pl.CostEstimate(flops=flops, bytes_accessed=moved, transcendentals=0),
    )(*operands, *after)


def in_vmem(values):
    return [("vmem", value) for value in values]


def join(pieces, out):
    at = 0
    for piece in pieces:
        out[at : at + piece.shape[0], :] = piece[...]
        at += piece.shape[0]


def place(pieces, order, out):
    size, order = pieces[0].shape[0], list(order)
    for piece in pieces:
        for at in range(0, piece.shape[0], size):
            to = order.pop(0) * size
            out[to : to + size, :] = piece[at : at + size, :]


def joined(pieces, after=()):
    rows = sum(piece.shape[0] for piece in pieces)

    def kernel(*refs):
        join(refs[: len(pieces)], refs[-1])

    return call(
        kernel, in_vmem(pieces), [("vmem", ((rows, pieces[0].shape[1]), BF16))], 0, 0, after
    )[0]


class Weight:
    def __init__(self, me, value, rows, by_rows):
        self.me, self.value, self.by_rows = me, value, by_rows
        self.block = value.shape[0 if by_rows else 1] // rows
        self.width = value.shape[1 if by_rows else 0]
        self.held = {}

    def shape(self):
        return ((2, self.block, self.width) if self.by_rows else (2, self.width, self.block), BF16)

    def part(self, ref, me, r):
        at = pl.ds(pl.multiple_of((me ^ r) * self.block, 128), self.block)
        return ref.at[at, :] if self.by_rows else ref.at[:, at]

    def copies(self, source, helds, arrived, me, chips):
        return [
            pltpu.make_async_copy(
                self.part(source, me, 2 * chip + odd), held.at[odd], arrived.at[2 * i + odd]
            )
            for i, (chip, held) in enumerate(zip(chips, helds))
            for odd in range(2)
        ]

    def moved(self, chips):
        return 4 * len(chips) * self.block * self.width


def load(weight, chips, after=()):
    def kernel(me_ref, source, *refs):
        refs = refs[len(after) :]
        copies = weight.copies(source, refs[:-1], refs[-1], me_ref[0], chips)
        for copy in copies:
            copy.start()
        for copy in copies:
            copy.wait()

    helds = call(
        kernel,
        [("smem", weight.me), ("hbm", weight.value)],
        [("vmem", weight.shape())] * len(chips),
        0,
        0,
        after,
        [pltpu.SemaphoreType.DMA((2 * len(chips),))],
    )
    weight.held.update(zip(chips, helds))


def project(weight, shards, chips, after=(), coming=None, coming_chips=()):
    pieces, order = shards
    tokens, n = sum(piece.shape[0] for piece in pieces), len(chips)
    block, by_rows = weight.block, weight.by_rows
    more = len(coming_chips)

    def kernel(me_ref, *refs):
        piece_refs, refs = refs[: len(pieces)], refs[len(pieces) :]
        parts, refs = refs[:n], refs[n:]
        copies = []
        if more:
            source, refs = refs[0], refs[1:]
        refs = refs[len(after) :]
        keeps, send, refs = refs[:n], refs[n], refs[n + 1 :]
        left = refs[more]
        if more:
            copies = coming.copies(source, refs[:more], refs[-1], me_ref[0], coming_chips)
        for copy in copies:
            copy.start()
        place(piece_refs, order, left)
        for i in range(n):
            for odd in (1, 0):
                out = dot(left[...], parts[i][odd], 1, 1 if by_rows else 0).astype(BF16)
                if odd:
                    send[i] = out
                else:
                    keeps[i][...] = out
        for copy in copies:
            copy.wait()

    outs = call(
        kernel,
        [("smem", weight.me)]
        + in_vmem(pieces)
        + in_vmem([weight.held[chip] for chip in chips])
        + ([("hbm", coming.value)] if more else []),
        [("vmem", ((tokens, block), BF16))] * n
        + [("vmem", ((n, tokens, block), BF16))]
        + ([("vmem", coming.shape())] * more if more else []),
        4 * tokens * weight.width * block * n,
        weight.moved(chips),
        after,
        [pltpu.VMEM((tokens, weight.width), BF16)]
        + ([pltpu.SemaphoreType.DMA((2 * more,))] if more else []),
    )
    if more:
        coming.held.update(zip(coming_chips, outs[n + 1 :]))
    return outs[:n], outs[n]


def block_sum(weight, stacks, odds, cols, groups, so_far=None, after=()):
    width, by_rows, block = weight.width, weight.by_rows, weight.block
    chips = len(weight.held)
    tokens = stacks[0].shape[0] // chips
    n, size = len(stacks), tokens // cols

    def kernel(*refs):
        stack_refs, parts, refs = refs[:n], refs[n : n + chips], refs[n + chips :]
        before, refs = (refs[0], refs[1:]) if so_far is not None else (None, refs)
        outs, total = refs[len(after) : -1], refs[-1]
        first = before is None
        if not first:
            total[...] = before[...]
        for i in range(chips):
            for stack, odd in zip(stack_refs, odds):
                value = stack[i * tokens : (i + 1) * tokens, :]
                term = dot(value, parts[i][odd], 1, 0 if by_rows else 1)
                total[...] = term if first else total[...] + term
                first = False
        if not groups:
            outs[0][...] = total[...]
        for group, out in zip(groups, outs):
            for i, q in enumerate(group):
                out[i * size : (i + 1) * size, :] = total[q * size : (q + 1) * size, :].astype(BF16)

    return call(
        kernel,
        in_vmem(stacks)
        + in_vmem([weight.held[chip] for chip in range(chips)])
        + in_vmem([so_far] if so_far is not None else []),
        [("vmem", ((len(group) * size, width), BF16)) for group in groups]
        or [("vmem", ((tokens, width), F32))],
        2 * tokens * width * block * chips * n,
        weight.moved(range(chips)) // 2 * n,
        after,
        [pltpu.VMEM((tokens, width), F32)],
    )


def weight_grad(weight, stacks, shards, after=()):
    pieces, order = shards
    chips, block = len(weight.held), weight.block
    rows, tokens = 2 * chips, stacks[0].shape[0] // chips
    width, by_rows = weight.width, weight.by_rows
    halves = 2
    size = (block if by_rows else width) // halves

    def kernel(me_ref, *refs):
        stack_refs, refs = refs[:2], refs[2:]
        piece_refs, refs = refs[: len(pieces)], refs[len(pieces) :]
        grad, other, ready, sent = refs[len(after) :]
        place(piece_refs, order, other)
        me = me_ref[0]

        def write(step):
            r, half = step // halves, step % halves
            to = weight.part(grad, me, r)
            to = to.at[half * size : (half + 1) * size, :]
            return pltpu.make_async_copy(ready.at[step % WRITES], to, sent.at[step % WRITES])

        steps = rows * halves
        for step in range(steps):
            r, half = step // halves, step % halves
            if step >= WRITES:
                write(step - WRITES).wait()
            stack, of = stack_refs[r % 2], slice(r // 2 * tokens, (r // 2 + 1) * tokens)
            at = slice(half * size, (half + 1) * size)
            if by_rows:
                out = dot(stack[of, at], other[...], 0, 0)
            else:
                out = dot(other[:, at], stack[of, :], 0, 0)
            ready[step % WRITES] = out.astype(BF16)
            write(step).start()
        for step in range(max(0, steps - WRITES), steps):
            write(step).wait()

    return call(
        kernel,
        [("smem", weight.me)] + in_vmem(stacks) + in_vmem(pieces),
        [("hbm", (weight.value.shape, BF16))],
        2 * tokens * width * block * rows,
        weight.moved(range(chips)),
        after,
        [
            pltpu.VMEM((tokens, width), BF16),
            pltpu.VMEM((WRITES, size, width if by_rows else block), BF16),
            pltpu.SemaphoreType.DMA((WRITES,)),
        ],
    )[0]


def activate(keep, got, travelled, after=()):
    def kernel(keep_ref, got_ref, *refs):
        total = keep_ref[...].astype(F32) + got_ref[0].astype(F32)
        for ref in refs[: len(travelled)]:
            total = total + ref[...].astype(F32)
        refs[-2][...] = total
        refs[-1][...] = gelu_fn(total).astype(BF16)

    shape = keep.shape
    return call(
        kernel,
        in_vmem([keep, got, *travelled]),
        [("vmem", (shape, F32)), ("vmem", (shape, BF16))],
        0,
        0,
        after,
    )


def activate_back(hidden, keep, got, travelled, after=()):
    def kernel(hidden_ref, keep_ref, got_ref, *refs):
        total = keep_ref[...].astype(F32) + got_ref[0].astype(F32)
        for ref in refs[: len(travelled)]:
            total = total + ref[...].astype(F32)
        refs[-1][...] = gelu_back(hidden_ref[...], total)

    return call(
        kernel, in_vmem([hidden, keep, got, *travelled]), [("vmem", (keep.shape, BF16))], 0, 0, after
    )[0]


def pair_sums(keeps, got, chips):
    return {
        chip: (keep.astype(F32) + got[i].astype(F32)).astype(BF16)
        for i, (chip, keep) in enumerate(zip(chips, keeps))
        if chip
    }


def gather_row(share, rows, after=()):
    own = [share] + [swap(share, "row", 2 * i, rows) for i in range(1, rows // 2)]
    stack = joined(own, after)
    return stack, swap(stack, "row", 1, rows)


def exchange_col(parts, cols):
    return [parts[0]] + [swap(parts[q], "col", q, cols) for q in range(cols - 1, 0, -1)]


def summed(parts):
    return sum(part.astype(F32) for part in parts).astype(BF16)


def blocked(rows, cols, tokens, cotangent, w_in, w_out):
    me = lax.axis_index("row").astype(jnp.int32).reshape(1)
    w_in, w_out = Weight(me, w_in, rows, False), Weight(me, w_out, rows, True)
    chips = list(range(rows // 2))
    far, near = chips[len(chips) // 2 :], chips[: len(chips) // 2]

    flips = [1 << bit for bit in range(cols.bit_length() - 1)]
    token_pieces, token_order = [tokens], [0]
    cot_pieces, cot_order = [cotangent], [0]
    load(w_in, far)
    token_sent, cot_sent = tokens, cotangent
    for hop in range(len(flips)):
        if hop:
            token_sent = joined(token_pieces, (cot_pieces[-1], w_in.held[far[0]]))
            cot_sent = joined(cot_pieces, (token_sent,))
        flip = flips[-1 - hop]
        token_pieces.append(swap(token_sent, "col", flip, cols))
        token_order += [q ^ flip for q in token_order]
        if hop and hop == len(flips) - 1:
            load(w_in, near, (token_sent,))
            cot_sent = joined([cot_sent], (token_pieces[-1], w_in.held[near[0]]))
        cot_pieces.append(swap(cot_sent, "col", flips[hop], cols))
        cot_order += [q ^ flips[hop] for q in cot_order]
    token_shards, cot_shards = (token_pieces, token_order), (cot_pieces, cot_order)

    def travel(pairs):
        return {chip: swap(pairs[chip], "row", 2 * chip, rows) for chip in pairs}

    far_keeps, send = project(w_in, token_shards, far, (cot_sent,), w_out, far[: len(far) // 2])
    far_got = swap(send, "row", 1, rows)
    near_keeps, send = project(w_in, token_shards, near, (send,), w_out, far[len(far) // 2 :])
    near_got = swap(send, "row", 1, rows)
    far_pairs = pair_sums(far_keeps, far_got, far)
    near_pairs = pair_sums(near_keeps, near_got, near)
    travelled = {**travel(far_pairs), **travel(near_pairs)}
    own = near_keeps[0], near_got, [travelled[chip] for chip in chips[:0:-1]]
    load(w_out, near, (*far_pairs.values(), *near_pairs.values()))

    far_keeps, send = project(
        w_out,
        cot_shards,
        far,
        (w_out.held[near[0]], *travelled.values()),
    )
    hidden, act = activate(*own, (send,))
    far_got = swap(send, "row", 1, rows)
    far_pairs = pair_sums(far_keeps, far_got, far)
    near_keeps, send = project(w_out, cot_shards, near, (act, *far_pairs.values()))
    near_got = swap(send, "row", 1, rows)
    near_pairs = pair_sums(near_keeps, near_got, near)
    travelled = {**travel(far_pairs), **travel(near_pairs)}
    back_own = near_keeps[0], near_got, [travelled[chip] for chip in chips[:0:-1]]

    act = gather_row(act, rows, (send,))
    even, odd = range(0, cols, 2), range(1, cols, 2)
    keep, send = block_sum(w_out, act, (0, 1), cols, (even, odd))
    grad_hidden = activate_back(hidden, *back_own, (keep,))
    got = swap(send, "col", 1, cols)
    sums = [
        half.astype(F32) + other.astype(F32)
        for half, other in zip(jnp.split(keep, len(even)), jnp.split(got, len(even)))
    ]
    layer_parts = [
        swap(part.astype(BF16), "col", q, cols) for part, q in zip(sums[:0:-1], even[:0:-1])
    ]
    grad_w_out = weight_grad(w_out, act, cot_shards, (got,))
    hbm_grad = pltpu.with_memory_space_constraint(grad_w_out, pltpu.HBM)
    grad_hidden = gather_row(grad_hidden, rows, (hbm_grad, *layer_parts))

    (so_far,) = block_sum(w_in, grad_hidden[:1], (0,), cols, ())
    token_parts = block_sum(w_in, grad_hidden[1:], (1,), cols, [[q] for q in range(cols)], so_far)
    grad_w_in = weight_grad(w_in, grad_hidden, token_shards, tuple(token_parts))
    token_parts = exchange_col(token_parts, cols)
    return (summed([sums[0], *layer_parts]), summed(token_parts), grad_w_in, grad_w_out)


def collective(tokens, cotangent, w_in, w_out):
    token_full = lax.all_gather(tokens, "col", axis=0, tiled=True)
    cot_full = lax.all_gather(cotangent, "col", axis=0, tiled=True)

    def over(value, axis):
        return lax.psum_scatter(value.astype(BF16), axis, scatter_dimension=0, tiled=True)

    hidden = over(dot(token_full, w_in, 1, 0), "row").astype(F32)
    grad_act = over(dot(cot_full, w_out, 1, 1), "row").astype(F32)
    act = lax.all_gather(gelu_fn(hidden).astype(BF16), "row", axis=0, tiled=True)
    grad_hidden = lax.all_gather(gelu_back(hidden, grad_act), "row", axis=0, tiled=True)
    layer_out = over(dot(act, w_out, 1, 0), "col")
    grad_tokens = over(dot(grad_hidden, w_in, 1, 1), "col")
    grad_w_in = dot(token_full, grad_hidden, 0, 0).astype(BF16)
    grad_w_out = dot(act, cot_full, 0, 0).astype(BF16)
    return (layer_out, grad_tokens, grad_w_in, grad_w_out)


def solution(mesh):
    rows, cols = mesh.shape["row"], mesh.shape["col"]

    def shards(tokens, cotangent, w_in, w_out):
        powers = rows & (rows - 1) == 0 and cols & (cols - 1) == 0
        if powers and rows > 2 and cols > 1 and w_in.shape[1] % (rows * 128) == 0:
            return blocked(rows, cols, tokens, cotangent, w_in, w_out)
        return collective(tokens, cotangent, w_in, w_out)

    return jax.shard_map(
        shards,
        mesh=mesh,
        in_specs=(P("col", "row"), P("col", "row"), P("row", "col"), P("col", "row")),
        out_specs=(P("col", "row"), P("col", "row"), P("row", "col"), P("col", "row")),
        check_vma=False,
    )
```

```python
import functools

import jax
import jax.numpy as jnp
from jax import lax
from jax.experimental import pallas as pl
from jax.experimental.pallas import tpu as pltpu
from jax.sharding import PartitionSpec as P

BF16 = jnp.bfloat16
F32 = jnp.float32
VMEM_LIMIT = 10 * 1024 * 1024
WRITES = 6
READ_CUTS, WRITE_CUTS = 4, 3


def gelu_fn(value):
    return jax.nn.gelu(value, approximate=True)


def gelu_back(hidden, grad_act):
    unused, pullback = jax.vjp(gelu_fn, hidden)
    return pullback(grad_act)[0].astype(BF16)


def swap(value, axis, flip, count):
    return lax.ppermute(value, axis, [(i, i ^ flip) for i in range(count)])


def reverse(p, bits):
    return sum(((p >> j) & 1) << (bits - 1 - j) for j in range(bits))


def across(value, step, rows):
    bits = rows.bit_length() - 2
    flips = [2 << (bits - 1 - step if i & 1 else step) for i in range(rows)]
    return lax.ppermute(value, "row", [(i, i ^ flips[i]) for i in range(rows)])


def dot(left, right, left_dim, right_dim):
    return lax.dot_general(
        left, right, (((left_dim,), (right_dim,)), ((), ())), preferred_element_type=F32
    )


def call(kernel, arrays, outs, flops, moved, after=(), scratch=()):
    spaces = {"smem": pltpu.SMEM, "vmem": pltpu.VMEM, "hbm": pl.ANY}
    operands = []
    for space, value in arrays:
        if space != "smem":
            value = pltpu.with_memory_space_constraint(
                value, pltpu.HBM if space == "hbm" else pltpu.VMEM
            )
        operands.append(value)
    return pl.pallas_call(
        kernel,
        in_specs=[pl.BlockSpec(memory_space=spaces[space]) for space, value in arrays]
        + [pl.BlockSpec(memory_space=pl.ANY)] * len(after),
        out_specs=[pl.BlockSpec(memory_space=spaces[space]) for space, value in outs],
        scratch_shapes=list(scratch),
        out_shape=[
            pltpu.VMEM(shape, dtype) if space == "vmem" else jax.ShapeDtypeStruct(shape, dtype)
            for space, (shape, dtype) in outs
        ],
        compiler_params=pltpu.CompilerParams(vmem_limit_bytes=VMEM_LIMIT),
        cost_estimate=pl.CostEstimate(flops=flops, bytes_accessed=moved, transcendentals=0),
    )(*operands, *after)


def in_vmem(values):
    return [("vmem", value) for value in values]


def join(pieces, out):
    at = 0
    for piece in pieces:
        out[at : at + piece.shape[0], :] = piece[...]
        at += piece.shape[0]


def place(pieces, order, out):
    size, order = pieces[0].shape[0], list(order)
    for piece in pieces:
        for at in range(0, piece.shape[0], size):
            to = order.pop(0) * size
            out[to : to + size, :] = piece[at : at + size, :]


def joined(pieces, after=()):
    rows = sum(piece.shape[0] for piece in pieces)

    def kernel(*refs):
        join(refs[: len(pieces)], refs[-1])

    return call(
        kernel, in_vmem(pieces), [("vmem", ((rows, pieces[0].shape[1]), BF16))], 0, 0, after
    )[0]


class Weight:
    def __init__(self, me, value, rows, by_rows):
        self.me, self.value, self.by_rows = me, value, by_rows
        self.bits = rows.bit_length() - 2
        self.block = value.shape[0 if by_rows else 1] // rows
        self.width = value.shape[1 if by_rows else 0]
        self.shape = (self.block, self.width) if by_rows else (self.width, self.block)
        self.held = {}

    def part(self, ref, me, key):
        p, odd = key
        chip = p + (me & 1) * (reverse(p, self.bits) - p)
        at = (me ^ (2 * chip + odd)) * self.block
        at = pl.ds(pl.multiple_of(at, 128), self.block)
        return ref.at[at, :] if self.by_rows else ref.at[:, at]


def cut(ref, i, cuts):
    size = ref.shape[0] // cuts
    return ref.at[i * size : (i + 1) * size, :]


class Coming:
    def __init__(self, blocks):
        self.blocks = blocks
        self.weights = list(dict.fromkeys(weight for weight, key in blocks))
        self.count = len(blocks) * READ_CUTS
        self.inputs = [("hbm", weight.value) for weight in self.weights]
        self.outs = [("vmem", (weight.shape, BF16)) for weight, key in blocks]
        self.scratch = [pltpu.SemaphoreType.DMA((self.count,))] if blocks else []

    def copies(self, sources, helds, arrived, me):
        return [
            pltpu.make_async_copy(
                cut(weight.part(sources[self.weights.index(weight)], me, key), i, READ_CUTS),
                cut(held, i, READ_CUTS),
                arrived.at[n * READ_CUTS + i],
            )
            for n, ((weight, key), held) in enumerate(zip(self.blocks, helds))
            for i in range(READ_CUTS)
        ]

    def arrive(self, helds):
        for (weight, key), held in zip(self.blocks, helds):
            weight.held[key] = held


def load(blocks, after=()):
    coming = Coming(blocks)
    n = len(coming.inputs)

    def kernel(me_ref, *refs):
        copies = coming.copies(refs[:n], refs[n + len(after) : -1], refs[-1], me_ref[0])
        for copy in copies:
            copy.start()
        for copy in copies:
            copy.wait()

    me = blocks[0][0].me
    coming.arrive(
        call(kernel, [("smem", me), *coming.inputs], coming.outs, 0, 0, after, coming.scratch)
    )


def project(weight, shards, positions, blocks, after=()):
    pieces, order = shards
    coming = Coming(blocks)
    tokens, n = sum(piece.shape[0] for piece in pieces), len(positions)
    block, by_rows = weight.block, weight.by_rows
    keys = [(reverse(p, weight.bits), 1) for p in positions] + [(p, 0) for p in positions]

    def kernel(me_ref, *refs):
        piece_refs, refs = refs[: len(pieces)], refs[len(pieces) :]
        parts, refs = refs[: 2 * n], refs[2 * n :]
        sources, refs = refs[: len(coming.inputs)], refs[len(coming.inputs) + len(after) :]
        keep, send, refs = refs[0], refs[1], refs[2:]
        left, copies = refs[len(blocks)], []
        if blocks:
            copies = coming.copies(sources, refs[: len(blocks)], refs[-1], me_ref[0])
        for copy in copies:
            copy.start()
        place(piece_refs, order, left)
        for i, part in enumerate(parts):
            out = dot(left[...], part[...], 1, 1 if by_rows else 0).astype(BF16)
            (send if i < n else keep)[i % n] = out
        for copy in copies:
            copy.wait()

    keep, send, *helds = call(
        kernel,
        [("smem", weight.me)]
        + in_vmem(pieces)
        + in_vmem([weight.held[key] for key in keys])
        + coming.inputs,
        [("vmem", ((n, tokens, block), BF16))] * 2 + coming.outs,
        4 * tokens * weight.width * block * n,
        0,
        after,
        [pltpu.VMEM((tokens, weight.width), BF16)] + coming.scratch,
    )
    coming.arrive(helds)
    return keep, send


def block_sum(weight, stacks, odds, cols, groups, so_far=None, after=()):
    width, by_rows, block = weight.width, weight.by_rows, weight.block
    chips = len(weight.held) // 2
    tokens = stacks[0].shape[0] // chips
    n, size = len(stacks), tokens // cols
    parts = [
        weight.held[(reverse(p, weight.bits) if odd else p, odd)]
        for odd in odds
        for p in range(chips)
    ]

    def kernel(*refs):
        stack_refs, part_refs, refs = refs[:n], refs[n : n + len(parts)], refs[n + len(parts) :]
        before, refs = (refs[0], refs[1:]) if so_far is not None else (None, refs)
        outs, total = refs[len(after) : -1], refs[-1]
        if before is not None:
            total[...] = before[...]
        for i, part in enumerate(part_refs):
            p = i % chips
            value = stack_refs[i // chips][p * tokens : (p + 1) * tokens, :]
            term = dot(value, part[...], 1, 0 if by_rows else 1)
            total[...] = term if i == 0 and before is None else total[...] + term
        if not groups:
            outs[0][...] = total[...]
        for group, out in zip(groups, outs):
            for i, q in enumerate(group):
                out[i * size : (i + 1) * size, :] = total[q * size : (q + 1) * size, :].astype(BF16)

    return call(
        kernel,
        in_vmem(stacks) + in_vmem(parts) + in_vmem([so_far] if so_far is not None else []),
        [("vmem", ((len(group) * size, width), BF16)) for group in groups]
        or [("vmem", ((tokens, width), F32))],
        2 * tokens * width * block * chips * n,
        2 * width * block * chips * n,
        after,
        [pltpu.VMEM((tokens, width), F32)],
    )


def weight_grad(weight, stacks, shards, after=()):
    pieces, order = shards
    width, by_rows, block = weight.width, weight.by_rows, weight.block
    chips = len(weight.held) // 2
    tokens = stacks[0].shape[0] // chips
    halves = 2
    size = (block if by_rows else width) // halves
    keys = [
        (odd, p, (reverse(p, weight.bits) if odd else p, odd))
        for p in range(chips)
        for odd in range(2)
    ]

    def kernel(me_ref, *refs):
        stack_refs, refs = refs[:2], refs[2:]
        piece_refs, refs = refs[: len(pieces)], refs[len(pieces) :]
        grad, other, turned, ready, sent = refs[len(after) :]
        place(piece_refs, order, other)
        if not by_rows:
            turned[...] = other[...].T
        me = me_ref[0]

        def writes(step):
            to = weight.part(grad, me, keys[step // halves][2])
            at = step % halves * size
            to = to.at[at : at + size, :]
            slot = step % WRITES
            return [
                pltpu.make_async_copy(
                    cut(ready.at[slot], i, WRITE_CUTS), cut(to, i, WRITE_CUTS), sent.at[slot, i]
                )
                for i in range(WRITE_CUTS)
            ]

        steps = len(keys) * halves
        for step in range(steps):
            if step >= WRITES:
                for write in writes(step - WRITES):
                    write.wait()
            odd, p, key = keys[step // halves]
            stack, of = stack_refs[odd], slice(p * tokens, (p + 1) * tokens)
            at = slice(step % halves * size, (step % halves + 1) * size)
            if by_rows:
                out = dot(stack[of, at], other[...], 0, 0)
            else:
                out = dot(turned[at, :], stack[of, :], 1, 0)
            ready[step % WRITES] = out.astype(BF16)
            for write in writes(step):
                write.start()
        for step in range(max(0, steps - WRITES), steps):
            for write in writes(step):
                write.wait()

    return call(
        kernel,
        [("smem", weight.me)] + in_vmem(stacks) + in_vmem(pieces),
        [("hbm", (weight.value.shape, BF16))],
        4 * tokens * width * block * chips,
        4 * width * block * chips,
        after,
        [
            pltpu.VMEM((tokens, width), BF16),
            pltpu.VMEM((width, tokens), BF16),
            pltpu.VMEM((WRITES, size, width if by_rows else block), BF16),
            pltpu.SemaphoreType.DMA((WRITES, WRITE_CUTS)),
        ],
    )[0]


def folded(terms, after=()):
    shape = (terms[0].shape[0] // 2, *terms[0].shape[1:])

    def kernel(*refs):
        keep, send = refs[-2:]
        for i in range(2 * shape[0]):
            total = sum(ref[i].astype(F32) for ref in refs[: len(terms)])
            if i % 2:
                send[i // 2] = total.astype(BF16)
            else:
                keep[i // 2] = total

    return call(kernel, in_vmem(terms), [("vmem", (shape, F32)), ("vmem", (shape, BF16))], 0, 0, after)


def added(terms, after=()):
    def kernel(*refs):
        refs[-1][...] = sum(ref[...].astype(F32) for ref in refs[: len(terms)]).astype(BF16)

    return call(kernel, in_vmem(terms), [("vmem", (terms[0].shape, BF16))], 0, 0, after)[0]


def activate(terms, after=()):
    def kernel(*refs):
        total = sum(ref[0].astype(F32) for ref in refs[: len(terms)])
        refs[-2][...] = total
        refs[-1][...] = gelu_fn(total).astype(BF16)

    shape = terms[0].shape[1:]
    return call(kernel, in_vmem(terms), [("vmem", (shape, F32)), ("vmem", (shape, BF16))], 0, 0, after)


def activate_back(hidden, terms, after=()):
    def kernel(hidden_ref, *refs):
        total = sum(ref[0].astype(F32) for ref in refs[: len(terms)])
        refs[-1][...] = gelu_back(hidden_ref[...], total)

    outs = [("vmem", (hidden.shape, BF16))]
    return call(kernel, in_vmem([hidden, *terms]), outs, 0, 0, after)[0]


def exchange_col(parts, cols):
    return [parts[0]] + [swap(parts[q], "col", q, cols) for q in range(cols - 1, 0, -1)]


def summed(parts):
    return sum(part.astype(F32) for part in parts).astype(BF16)


def blocked(rows, cols, tokens, cotangent, w_in, w_out):
    me = lax.axis_index("row").astype(jnp.int32).reshape(1)
    w_in, w_out = Weight(me, w_in, rows, False), Weight(me, w_out, rows, True)
    steps = rows.bit_length() - 2
    there, here = range(1, rows // 2, 2), range(0, rows // 2, 2)

    def keys(positions):
        return [(reverse(p, steps), 1) for p in positions] + [(p, 0) for p in positions]

    wanted = [(w, key) for w in (w_in, w_out) for key in keys(there) + keys(here)]
    share = len(wanted) // 16
    loads = [wanted[: 5 * share], wanted[5 * share : 10 * share]]
    loads += [wanted[10 * share : 13 * share], wanted[13 * share :]]

    flips = [1 << bit for bit in range(cols.bit_length() - 1)]
    token_pieces, token_order = [tokens], [0]
    cot_pieces, cot_order = [cotangent], [0]
    load(loads[0])
    token_sent, cot_sent = tokens, cotangent
    for hop in range(len(flips)):
        if hop:
            token_sent = joined(token_pieces, (cot_pieces[-1], w_in.held[wanted[0][1]]))
            cot_sent = joined(cot_pieces, (token_sent,))
        flip = flips[-1 - hop]
        token_pieces.append(swap(token_sent, "col", flip, cols))
        token_order += [q ^ flip for q in token_order]
        if hop and hop == len(flips) - 1:
            load(loads[1], (token_sent,))
            cot_sent = joined([cot_sent], (token_pieces[-1], w_in.held[loads[1][0][1]]))
        cot_pieces.append(swap(cot_sent, "col", flips[hop], cols))
        cot_order += [q ^ flips[hop] for q in cot_order]
    token_shards, cot_shards = (token_pieces, token_order), (cot_pieces, cot_order)

    keep, first_sent = project(w_in, token_shards, there, loads[2], (cot_sent,))
    to_send = added([keep, swap(first_sent, "row", 1, rows)])
    keep, second_sent = project(w_in, token_shards, here, loads[3], (first_sent,))
    terms = [keep, swap(second_sent, "row", 1, rows), across(to_send, 0, rows)]

    back_keep, back_sent = project(w_out, cot_shards, there, [], (to_send,))
    back_to_send = added([back_keep, swap(back_sent, "row", 1, rows)])
    for step in range(1, steps):
        keep, send = folded(terms, (back_sent,))
        terms = [keep, across(send, step, rows)]
    back_keep, back_sent = project(w_out, cot_shards, here, [], (back_to_send, send))
    back_terms = [
        back_keep, swap(back_sent, "row", 1, rows), across(back_to_send, 0, rows)
    ]
    hidden, act = activate(terms, (back_sent,))
    for step in range(1, steps):
        back_keep, back_send = folded(back_terms, (act,))
        back_terms = [back_keep, across(back_send, step, rows)]

    stack = joined([act, across(act, 0, rows)], (back_send,))
    grad_hidden = activate_back(hidden, back_terms, (stack,))
    back_stack = joined([grad_hidden, across(grad_hidden, 0, rows)], (stack,))
    for step in range(1, steps):
        stack = joined([stack, across(stack, step, rows)], (back_stack,))
    act = stack, swap(stack, "row", 1, rows)
    even, odd = range(0, cols, 2), range(1, cols, 2)
    keep, send = block_sum(w_out, act, (0, 1), cols, (even, odd), after=(back_stack,))
    for step in range(1, steps):
        back_stack = joined([back_stack, across(back_stack, step, rows)], (keep,))
    grad_hidden = back_stack, swap(back_stack, "row", 1, rows)
    grad_w_out = weight_grad(w_out, act, cot_shards, (back_stack,))
    got = swap(send, "col", 1, cols)
    sums = [
        half.astype(F32) + other.astype(F32)
        for half, other in zip(jnp.split(keep, len(even)), jnp.split(got, len(even)))
    ]
    layer_parts = [
        swap(part.astype(BF16), "col", q, cols) for part, q in zip(sums[:0:-1], even[:0:-1])
    ]
    hbm_grad = pltpu.with_memory_space_constraint(grad_w_out, pltpu.HBM)
    (so_far,) = block_sum(w_in, grad_hidden[:1], (0,), cols, (), after=(hbm_grad, got))
    token_parts = block_sum(w_in, grad_hidden[1:], (1,), cols, [[q] for q in range(cols)], so_far)
    grad_w_in = weight_grad(w_in, grad_hidden, token_shards, tuple(token_parts))
    token_parts = exchange_col(token_parts, cols)
    return (summed([sums[0], *layer_parts]), summed(token_parts), grad_w_in, grad_w_out)


def collective(tokens, cotangent, w_in, w_out):
    token_full = lax.all_gather(tokens, "col", axis=0, tiled=True)
    cot_full = lax.all_gather(cotangent, "col", axis=0, tiled=True)

    def over(value, axis):
        return lax.psum_scatter(value.astype(BF16), axis, scatter_dimension=0, tiled=True)

    hidden = over(dot(token_full, w_in, 1, 0), "row").astype(F32)
    grad_act = over(dot(cot_full, w_out, 1, 1), "row").astype(F32)
    act = lax.all_gather(gelu_fn(hidden).astype(BF16), "row", axis=0, tiled=True)
    grad_hidden = lax.all_gather(gelu_back(hidden, grad_act), "row", axis=0, tiled=True)
    layer_out = over(dot(act, w_out, 1, 0), "col")
    grad_tokens = over(dot(grad_hidden, w_in, 1, 1), "col")
    grad_w_in = dot(token_full, grad_hidden, 0, 0).astype(BF16)
    grad_w_out = dot(act, cot_full, 0, 0).astype(BF16)
    return (layer_out, grad_tokens, grad_w_in, grad_w_out)


def solution(mesh):
    rows, cols = mesh.shape["row"], mesh.shape["col"]

    def shards(tokens, cotangent, w_in, w_out):
        powers = rows & (rows - 1) == 0 and cols & (cols - 1) == 0
        if powers and rows > 4 and cols > 1 and w_in.shape[1] % (rows * 128) == 0:
            return blocked(rows, cols, tokens, cotangent, w_in, w_out)
        return collective(tokens, cotangent, w_in, w_out)

    return jax.shard_map(
        shards,
        mesh=mesh,
        in_specs=(P("col", "row"), P("col", "row"), P("row", "col"), P("col", "row")),
        out_specs=(P("col", "row"), P("col", "row"), P("row", "col"), P("col", "row")),
        check_vma=False,
    )
```

```python
import functools

import jax
import jax.numpy as jnp
from jax import lax
from jax.experimental import pallas as pl
from jax.experimental.pallas import tpu as pltpu
from jax.sharding import PartitionSpec as P

BF16 = jnp.bfloat16
F32 = jnp.float32
VMEM_LIMIT = 10 * 1024 * 1024
WRITES = 6
READ_CUTS, WRITE_CUTS = 4, 3
WEIGHTY = 6 * 10**9


def gelu_fn(value):
    return jax.nn.gelu(value, approximate=True)


def gelu_back(hidden, grad_act):
    unused, pullback = jax.vjp(gelu_fn, hidden)
    return pullback(grad_act)[0].astype(BF16)


def swap(value, axis, flip, count):
    return lax.ppermute(value, axis, [(i, i ^ flip) for i in range(count)])


def reverse(p, bits):
    return sum(((p >> j) & 1) << (bits - 1 - j) for j in range(bits))


def across(value, step, rows):
    bits = rows.bit_length() - 2
    flips = [2 << (bits - 1 - step if i & 1 else step) for i in range(rows)]
    return lax.ppermute(value, "row", [(i, i ^ flips[i]) for i in range(rows)])


def dot(left, right, left_dim, right_dim):
    return lax.dot_general(
        left, right, (((left_dim,), (right_dim,)), ((), ())), preferred_element_type=F32
    )


LAST = []


def call(kernel, arrays, outs, flops, moved, after=(), scratch=(), in_place=False):
    unread, count = [*LAST, *after], len(arrays)

    def body(*refs):
        kernel(*refs[:count], *refs[count + len(unread) :])

    specs = {
        "smem": pl.BlockSpec(memory_space=pltpu.SMEM),
        "vmem": pl.BlockSpec(memory_space=pltpu.VMEM),
        "hbm": pl.BlockSpec(memory_space=pl.ANY),
        "window": pl.BlockSpec(),
    }
    operands = []
    for space, value in arrays:
        if space != "smem":
            value = pltpu.with_memory_space_constraint(
                value, pltpu.HBM if space == "hbm" else pltpu.VMEM
            )
        operands.append(value)
    results = pl.pallas_call(
        body,
        in_specs=[specs[space] for space, value in arrays]
        + [pl.BlockSpec(memory_space=pl.ANY)] * len(unread),
        out_specs=[specs[space] for space, value in outs],
        scratch_shapes=list(scratch),
        input_output_aliases={count - 1: 0} if in_place else {},
        out_shape=[
            pltpu.VMEM(shape, dtype) if space == "vmem" else jax.ShapeDtypeStruct(shape, dtype)
            for space, (shape, dtype) in outs
        ],
        compiler_params=pltpu.CompilerParams(vmem_limit_bytes=VMEM_LIMIT),
        cost_estimate=pl.CostEstimate(flops=flops, bytes_accessed=moved, transcendentals=0),
    )(*operands, *unread)
    last = results[-1]
    if outs[-1][0] != "vmem":
        last = pltpu.with_memory_space_constraint(last, pltpu.HBM)
    LAST[:] = [last]
    return results


def in_vmem(values):
    return [("vmem", value) for value in values]


def join(pieces, out):
    at = 0
    for piece in pieces:
        out[at : at + piece.shape[0], :] = piece[...]
        at += piece.shape[0]


def place(pieces, order, out):
    size, order = pieces[0].shape[0], list(order)
    for piece in pieces:
        for at in range(0, piece.shape[0], size):
            to = order.pop(0) * size
            out[to : to + size, :] = piece[at : at + size, :]


def joined(pieces, after=()):
    rows = sum(piece.shape[0] for piece in pieces)

    def kernel(*refs):
        join(refs[: len(pieces)], refs[-1])

    return call(
        kernel, in_vmem(pieces), [("vmem", ((rows, pieces[0].shape[1]), BF16))], 0, 0, after
    )[0]


class Weight:
    def __init__(self, me, value, rows, by_rows):
        self.me, self.value, self.by_rows = me, value, by_rows
        self.bits = rows.bit_length() - 2
        self.block = value.shape[0 if by_rows else 1] // rows
        self.width = value.shape[1 if by_rows else 0]
        self.shape = (self.block, self.width) if by_rows else (self.width, self.block)
        self.held = {}

    def part(self, ref, me, key):
        p, odd = key
        chip = p + (me & 1) * (reverse(p, self.bits) - p)
        at = (me ^ (2 * chip + odd)) * self.block
        at = pl.ds(pl.multiple_of(at, 128), self.block)
        return ref.at[at, :] if self.by_rows else ref.at[:, at]


def cut(ref, i, cuts):
    size = ref.shape[0] // cuts
    return ref.at[i * size : (i + 1) * size, :]


class Coming:
    def __init__(self, blocks):
        self.blocks = blocks
        self.weights = list(dict.fromkeys(weight for weight, key in blocks))
        self.count = len(blocks) * READ_CUTS
        self.inputs = [("hbm", weight.value) for weight in self.weights]
        self.outs = [("vmem", (weight.shape, BF16)) for weight, key in blocks]
        self.scratch = [pltpu.SemaphoreType.DMA((self.count,))] if blocks else []

    def copies(self, sources, helds, arrived, me):
        return [
            pltpu.make_async_copy(
                cut(weight.part(sources[self.weights.index(weight)], me, key), i, READ_CUTS),
                cut(held, i, READ_CUTS),
                arrived.at[n * READ_CUTS + i],
            )
            for n, ((weight, key), held) in enumerate(zip(self.blocks, helds))
            for i in range(READ_CUTS)
        ]

    def arrive(self, helds):
        for (weight, key), held in zip(self.blocks, helds):
            weight.held[key] = held


def load(blocks, after=()):
    coming = Coming(blocks)
    n = len(coming.inputs)

    def kernel(me_ref, *refs):
        copies = coming.copies(refs[:n], refs[n:-1], refs[-1], me_ref[0])
        for copy in copies:
            copy.start()
        for copy in copies:
            copy.wait()

    me = blocks[0][0].me
    coming.arrive(
        call(kernel, [("smem", me), *coming.inputs], coming.outs, 0, 0, after, coming.scratch)
    )


def project(weight, shards, positions, blocks, after=()):
    pieces, order = shards
    coming = Coming(blocks)
    tokens, n = sum(piece.shape[0] for piece in pieces), len(positions)
    block, by_rows = weight.block, weight.by_rows
    keys = [(reverse(p, weight.bits), 1) for p in positions] + [(p, 0) for p in positions]

    def kernel(me_ref, *refs):
        piece_refs, refs = refs[: len(pieces)], refs[len(pieces) :]
        parts, refs = refs[: 2 * n], refs[2 * n :]
        sources, refs = refs[: len(coming.inputs)], refs[len(coming.inputs) :]
        keep, send, refs = refs[0], refs[1], refs[2:]
        left, copies = refs[len(blocks)], []
        if blocks:
            copies = coming.copies(sources, refs[: len(blocks)], refs[-1], me_ref[0])
        for copy in copies:
            copy.start()
        place(piece_refs, order, left)
        for i, part in enumerate(parts):
            out = dot(left[...], part[...], 1, 1 if by_rows else 0).astype(BF16)
            (send if i < n else keep)[i % n] = out
        for copy in copies:
            copy.wait()

    keep, send, *helds = call(
        kernel,
        [("smem", weight.me)]
        + in_vmem(pieces)
        + in_vmem([weight.held[key] for key in keys])
        + coming.inputs,
        [("vmem", ((n, tokens, block), BF16))] * 2 + coming.outs,
        4 * tokens * weight.width * block * n,
        0,
        after,
        [pltpu.VMEM((tokens, weight.width), BF16)] + coming.scratch,
    )
    coming.arrive(helds)
    return keep, send


def block_sum(weight, stacks, odds, cols, groups, so_far=None, after=()):
    width, by_rows, block = weight.width, weight.by_rows, weight.block
    chips = len(weight.held) // 2
    tokens = stacks[0].shape[0] // chips
    n, size = len(stacks), tokens // cols
    parts = [
        weight.held[(reverse(p, weight.bits) if odd else p, odd)]
        for odd in odds
        for p in range(chips)
    ]

    def kernel(*refs):
        stack_refs, part_refs, refs = refs[:n], refs[n : n + len(parts)], refs[n + len(parts) :]
        before, refs = (refs[0], refs[1:]) if so_far is not None else (None, refs)
        outs, total = refs[:-1], refs[-1]
        if before is not None:
            total[...] = before[...]
        for i, part in enumerate(part_refs):
            p = i % chips
            value = stack_refs[i // chips][p * tokens : (p + 1) * tokens, :]
            term = dot(value, part[...], 1, 0 if by_rows else 1)
            total[...] = term if i == 0 and before is None else total[...] + term
        if not groups:
            outs[0][...] = total[...]
        for group, out in zip(groups, outs):
            for i, q in enumerate(group):
                out[i * size : (i + 1) * size, :] = total[q * size : (q + 1) * size, :].astype(BF16)

    return call(
        kernel,
        in_vmem(stacks) + in_vmem(parts) + in_vmem([so_far] if so_far is not None else []),
        [("vmem", ((len(group) * size, width), BF16)) for group in groups]
        or [("vmem", ((tokens, width), F32))],
        2 * tokens * width * block * chips * n,
        2 * width * block * chips * n,
        after,
        [pltpu.VMEM((tokens, width), F32)],
    )


def weight_grad(weight, stacks, odds, shards, into=None):
    pieces, order = shards
    width, by_rows, block = weight.width, weight.by_rows, weight.block
    chips = len(weight.held) // 2
    tokens = stacks[0].shape[0] // chips
    halves = 2
    size = (block if by_rows else width) // halves
    keys = [
        (i, p, (reverse(p, weight.bits) if odd else p, odd))
        for p in range(chips)
        for i, odd in enumerate(odds)
    ]

    def kernel(me_ref, *refs):
        stack_refs, refs = refs[: len(stacks)], refs[len(stacks) :]
        piece_refs, refs = refs[: len(pieces)], refs[len(pieces) :]
        grad, other, turned, ready, sent = refs[-5:]
        place(piece_refs, order, other)
        if not by_rows:
            turned[...] = other[...].T
        me = me_ref[0]

        def writes(step):
            to = weight.part(grad, me, keys[step // halves][2])
            at = step % halves * size
            to = to.at[at : at + size, :]
            slot = step % WRITES
            return [
                pltpu.make_async_copy(
                    cut(ready.at[slot], i, WRITE_CUTS), cut(to, i, WRITE_CUTS), sent.at[slot, i]
                )
                for i in range(WRITE_CUTS)
            ]

        steps = len(keys) * halves
        for step in range(steps):
            if step >= WRITES:
                for write in writes(step - WRITES):
                    write.wait()
            i, p, key = keys[step // halves]
            stack, of = stack_refs[i], slice(p * tokens, (p + 1) * tokens)
            at = slice(step % halves * size, (step % halves + 1) * size)
            if by_rows:
                out = dot(stack[of, at], other[...], 0, 0)
            else:
                out = dot(turned[at, :], stack[of, :], 1, 0)
            ready[step % WRITES] = out.astype(BF16)
            for write in writes(step):
                write.start()
        for step in range(max(0, steps - WRITES), steps):
            for write in writes(step):
                write.wait()

    return call(
        kernel,
        [("smem", weight.me)]
        + in_vmem(stacks)
        + in_vmem(pieces)
        + ([("hbm", into)] if into is not None else []),
        [("hbm", (weight.value.shape, BF16))],
        2 * tokens * width * block * len(keys),
        2 * width * block * len(keys),
        (),
        [
            pltpu.VMEM((tokens, width), BF16),
            pltpu.VMEM((width, tokens), BF16),
            pltpu.VMEM((WRITES, size, width if by_rows else block), BF16),
            pltpu.SemaphoreType.DMA((WRITES, WRITE_CUTS)),
        ],
        into is not None,
    )[0]


def folded(terms, after=()):
    shape = (terms[0].shape[0] // 2, *terms[0].shape[1:])

    def kernel(*refs):
        keep, send = refs[-2:]
        for i in range(2 * shape[0]):
            total = sum(ref[i].astype(F32) for ref in refs[: len(terms)])
            if i % 2:
                send[i // 2] = total.astype(BF16)
            else:
                keep[i // 2] = total

    return call(kernel, in_vmem(terms), [("vmem", (shape, F32)), ("vmem", (shape, BF16))], 0, 0, after)


def summed_half(keep, got, count, after=()):
    size = keep.shape[0] // count

    def kernel(keep_ref, got_ref, *outs):
        for i, out in enumerate(outs):
            at = slice(i * size, (i + 1) * size)
            total = keep_ref[at, :].astype(F32) + got_ref[at, :].astype(F32)
            out[...] = total.astype(out.dtype)

    shape = (size, keep.shape[1])
    outs = [("vmem", (shape, F32))] + [("vmem", (shape, BF16))] * (count - 1)
    return call(kernel, in_vmem([keep, got]), outs, 0, 0, after)


def partly(terms):
    def kernel(*refs):
        refs[-1][...] = sum(ref[...].astype(F32) for ref in refs[:-1])

    return call(kernel, in_vmem(terms), [("vmem", (terms[0].shape, F32))], WEIGHTY, 0)[0]


def added(terms, space="vmem"):
    def kernel(*refs):
        refs[-1][...] = sum(ref[...].astype(F32) for ref in refs[: len(terms)]).astype(BF16)

    return call(kernel, in_vmem(terms), [(space, (terms[0].shape, BF16))], 0, 0)[0]


def activate(terms, after=()):
    def kernel(*refs):
        total = sum(ref[0].astype(F32) for ref in refs[: len(terms)])
        refs[-2][...] = total
        refs[-1][...] = gelu_fn(total).astype(BF16)

    shape = terms[0].shape[1:]
    outs = [("vmem", (shape, F32)), ("vmem", (shape, BF16))]
    return call(kernel, in_vmem(terms), outs, WEIGHTY, 0, after)


def activate_back(hidden, terms, after=()):
    def kernel(hidden_ref, *refs):
        total = sum(ref[0].astype(F32) for ref in refs[: len(terms)])
        refs[-1][...] = gelu_back(hidden_ref[...], total)

    outs = [("vmem", (hidden.shape, BF16))]
    return call(kernel, in_vmem([hidden, *terms]), outs, 0, 0, after)[0]


def exchange_col(parts, cols):
    return [parts[0]] + [swap(parts[q], "col", q, cols) for q in range(cols - 1, 0, -1)]


def summed(parts):
    return sum(part.astype(F32) for part in parts).astype(BF16)


def blocked(rows, cols, tokens, cotangent, w_in, w_out):
    LAST.clear()
    me = lax.axis_index("row").astype(jnp.int32).reshape(1)
    w_in, w_out = Weight(me, w_in, rows, False), Weight(me, w_out, rows, True)
    steps = rows.bit_length() - 2
    there, here = range(1, rows // 2, 2), range(0, rows // 2, 2)

    def keys(positions):
        return [(reverse(p, steps), 1) for p in positions] + [(p, 0) for p in positions]

    def across_all(terms):
        for step in range(1, steps):
            keep, send = folded(terms)
            terms = [keep, across(send, step, rows)]
        return terms

    def gathered(stack, first):
        for step in [0] if first else range(1, steps):
            stack = joined([stack, across(stack, step, rows)])
        return stack

    def other_core(value):
        return swap(value, "row", 1, rows)

    wanted = [(w, key) for w in (w_in, w_out) for key in keys(there) + keys(here)]
    share = len(wanted) // 16

    flips = [1 << bit for bit in range(cols.bit_length() - 1)]
    token_pieces, token_order = [tokens], [0]
    cot_pieces, cot_order = [cotangent], [0]
    load(wanted[: 5 * share])
    token_sent, cot_sent = tokens, cotangent
    for hop in range(len(flips)):
        if hop:
            token_sent = joined(token_pieces, (cot_pieces[-1],))
            cot_sent = joined(cot_pieces)
        flip = flips[-1 - hop]
        token_pieces.append(swap(token_sent, "col", flip, cols))
        token_order += [q ^ flip for q in token_order]
        if hop and hop == len(flips) - 1:
            load(wanted[5 * share : 10 * share])
            cot_sent = joined([cot_sent], (token_pieces[-1],))
        cot_pieces.append(swap(cot_sent, "col", flips[hop], cols))
        cot_order += [q ^ flips[hop] for q in cot_order]
    token_shards, cot_shards = (token_pieces, token_order), (cot_pieces, cot_order)

    keep, sent = project(w_in, token_shards, there, [])
    got = other_core(sent)
    here_keep, here_sent = project(w_in, token_shards, here, [])
    terms = [here_keep, other_core(here_sent), across(added([keep, got]), 0, rows)]
    load(wanted[10 * share :])
    terms = across_all(terms)

    keep, sent = project(w_out, cot_shards, there, [])
    got = other_core(sent)
    hidden, act = activate(terms)
    there_sum = added([keep, got])
    here_keep, here_sent = project(w_out, cot_shards, here, [])
    came, got = across(there_sum, 0, rows), other_core(here_sent)

    stack = gathered(act, True)
    back_terms = across_all([partly([here_keep, came]), got])
    grad_hidden = activate_back(hidden, back_terms)
    stack = gathered(stack, False)
    act = stack, other_core(stack)
    grad_w_out = weight_grad(w_out, act[:1], (0,), cot_shards)
    back_stack = gathered(grad_hidden, True)

    even, odd = range(0, cols, 2), range(1, cols, 2)
    keep, send = block_sum(w_out, act, (0, 1), cols, (even, odd))
    grad_w_out = weight_grad(w_out, act[1:], (1,), cot_shards, grad_w_out)
    layer_out, *sums = summed_half(keep, swap(send, "col", 1, cols), len(even))
    layer_parts = [swap(part, "col", q, cols) for part, q in zip(sums, even[1:])]
    back_stack = gathered(back_stack, False)
    grad_hidden = back_stack, other_core(back_stack)

    (so_far,) = block_sum(w_in, grad_hidden[:1], (0,), cols, ())
    token_parts = block_sum(w_in, grad_hidden[1:], (1,), cols, [[q] for q in range(cols)], so_far)
    layer_out = added([layer_out, *layer_parts], "window")
    grad_w_in = weight_grad(w_in, grad_hidden, (0, 1), token_shards)
    token_parts = exchange_col(token_parts, cols)
    return (layer_out, summed(token_parts), grad_w_in, grad_w_out)


def collective(tokens, cotangent, w_in, w_out):
    token_full = lax.all_gather(tokens, "col", axis=0, tiled=True)
    cot_full = lax.all_gather(cotangent, "col", axis=0, tiled=True)

    def over(value, axis):
        return lax.psum_scatter(value.astype(BF16), axis, scatter_dimension=0, tiled=True)

    hidden = over(dot(token_full, w_in, 1, 0), "row").astype(F32)
    grad_act = over(dot(cot_full, w_out, 1, 1), "row").astype(F32)
    act = lax.all_gather(gelu_fn(hidden).astype(BF16), "row", axis=0, tiled=True)
    grad_hidden = lax.all_gather(gelu_back(hidden, grad_act), "row", axis=0, tiled=True)
    layer_out = over(dot(act, w_out, 1, 0), "col")
    grad_tokens = over(dot(grad_hidden, w_in, 1, 1), "col")
    grad_w_in = dot(token_full, grad_hidden, 0, 0).astype(BF16)
    grad_w_out = dot(act, cot_full, 0, 0).astype(BF16)
    return (layer_out, grad_tokens, grad_w_in, grad_w_out)


def solution(mesh):
    rows, cols = mesh.shape["row"], mesh.shape["col"]

    def shards(tokens, cotangent, w_in, w_out):
        powers = rows & (rows - 1) == 0 and cols & (cols - 1) == 0
        if powers and rows > 4 and cols > 1 and w_in.shape[1] % (rows * 128) == 0:
            return blocked(rows, cols, tokens, cotangent, w_in, w_out)
        return collective(tokens, cotangent, w_in, w_out)

    return jax.shard_map(
        shards,
        mesh=mesh,
        in_specs=(P("col", "row"), P("col", "row"), P("row", "col"), P("col", "row")),
        out_specs=(P("col", "row"), P("col", "row"), P("row", "col"), P("col", "row")),
        check_vma=False,
    )
```

```python
import functools

import jax
import jax.numpy as jnp
from jax import lax
from jax.experimental import pallas as pl
from jax.experimental.pallas import tpu as pltpu
from jax.sharding import PartitionSpec as P

BF16 = jnp.bfloat16
F32 = jnp.float32
VMEM_LIMIT = 10 * 1024 * 1024
WRITES = 6
READ_CUTS, WRITE_CUTS = 4, 3
WEIGHTY = 6 * 10**9


def gelu_fn(value):
    return jax.nn.gelu(value, approximate=True)


def gelu_back(hidden, grad_act):
    unused, pullback = jax.vjp(gelu_fn, hidden)
    return pullback(grad_act)[0].astype(BF16)


def swap(value, axis, flip, count):
    return lax.ppermute(value, axis, [(i, i ^ flip) for i in range(count)])


def reverse(p, bits):
    return sum(((p >> j) & 1) << (bits - 1 - j) for j in range(bits))


def across(value, step, rows):
    bits = rows.bit_length() - 2
    flips = [2 << (bits - 1 - step if i & 1 else step) for i in range(rows)]
    return lax.ppermute(value, "row", [(i, i ^ flips[i]) for i in range(rows)])


def dot(left, right, left_dim, right_dim):
    return lax.dot_general(
        left, right, (((left_dim,), (right_dim,)), ((), ())), preferred_element_type=F32
    )


LAST = []


def call(kernel, arrays, outs, flops, moved, after=(), scratch=(), in_place=False):
    unread, count = [*LAST, *after], len(arrays)

    def body(*refs):
        kernel(*refs[:count], *refs[count + len(unread) :])

    specs = {
        "smem": pl.BlockSpec(memory_space=pltpu.SMEM),
        "vmem": pl.BlockSpec(memory_space=pltpu.VMEM),
        "hbm": pl.BlockSpec(memory_space=pl.ANY),
        "window": pl.BlockSpec(),
    }
    operands = []
    for space, value in arrays:
        if space != "smem":
            value = pltpu.with_memory_space_constraint(
                value, pltpu.HBM if space == "hbm" else pltpu.VMEM
            )
        operands.append(value)
    results = pl.pallas_call(
        body,
        in_specs=[specs[space] for space, value in arrays]
        + [pl.BlockSpec(memory_space=pl.ANY)] * len(unread),
        out_specs=[specs[space] for space, value in outs],
        scratch_shapes=list(scratch),
        input_output_aliases={count - 1: 0} if in_place else {},
        out_shape=[
            pltpu.VMEM(shape, dtype) if space == "vmem" else jax.ShapeDtypeStruct(shape, dtype)
            for space, (shape, dtype) in outs
        ],
        compiler_params=pltpu.CompilerParams(vmem_limit_bytes=VMEM_LIMIT),
        cost_estimate=pl.CostEstimate(flops=flops, bytes_accessed=moved, transcendentals=0),
    )(*operands, *unread)
    last = results[-1]
    if outs[-1][0] != "vmem":
        last = pltpu.with_memory_space_constraint(last, pltpu.HBM)
    LAST[:] = [last]
    return results


def in_vmem(values):
    return [("vmem", value) for value in values]


def join(pieces, out):
    at = 0
    for piece in pieces:
        out[at : at + piece.shape[0], :] = piece[...]
        at += piece.shape[0]


def place(pieces, order, out):
    size, order = pieces[0].shape[0], list(order)
    for piece in pieces:
        for at in range(0, piece.shape[0], size):
            to = order.pop(0) * size
            out[to : to + size, :] = piece[at : at + size, :]


def joined(pieces, after=()):
    rows = sum(piece.shape[0] for piece in pieces)

    def kernel(*refs):
        join(refs[: len(pieces)], refs[-1])

    return call(
        kernel, in_vmem(pieces), [("vmem", ((rows, pieces[0].shape[1]), BF16))], 0, 0, after
    )[0]


class Weight:
    def __init__(self, me, value, rows, by_rows):
        self.me, self.value, self.by_rows = me, value, by_rows
        self.bits = rows.bit_length() - 2
        self.block = value.shape[0 if by_rows else 1] // rows
        self.width = value.shape[1 if by_rows else 0]
        self.shape = (self.block, self.width) if by_rows else (self.width, self.block)
        self.held = {}

    def part(self, ref, me, key):
        p, odd = key
        chip = p + (me & 1) * (reverse(p, self.bits) - p)
        at = (me ^ (2 * chip + odd)) * self.block
        at = pl.ds(pl.multiple_of(at, 128), self.block)
        return ref.at[at, :] if self.by_rows else ref.at[:, at]


def cut(ref, i, cuts):
    size = ref.shape[0] // cuts
    return ref.at[i * size : (i + 1) * size, :]


class Coming:
    def __init__(self, blocks):
        self.blocks = blocks
        self.weights = list(dict.fromkeys(weight for weight, key in blocks))
        self.count = len(blocks) * READ_CUTS
        self.inputs = [("hbm", weight.value) for weight in self.weights]
        self.outs = [("vmem", (weight.shape, BF16)) for weight, key in blocks]
        self.scratch = [pltpu.SemaphoreType.DMA((self.count,))] if blocks else []

    def copies(self, sources, helds, arrived, me):
        return [
            pltpu.make_async_copy(
                cut(weight.part(sources[self.weights.index(weight)], me, key), i, READ_CUTS),
                cut(held, i, READ_CUTS),
                arrived.at[n * READ_CUTS + i],
            )
            for n, ((weight, key), held) in enumerate(zip(self.blocks, helds))
            for i in range(READ_CUTS)
        ]

    def arrive(self, helds):
        for (weight, key), held in zip(self.blocks, helds):
            weight.held[key] = held


def load(blocks, after=()):
    coming = Coming(blocks)
    n = len(coming.inputs)

    def kernel(me_ref, *refs):
        copies = coming.copies(refs[:n], refs[n:-1], refs[-1], me_ref[0])
        for copy in copies:
            copy.start()
        for copy in copies:
            copy.wait()

    me = blocks[0][0].me
    coming.arrive(
        call(kernel, [("smem", me), *coming.inputs], coming.outs, 0, 0, after, coming.scratch)
    )


def project(weight, shards, positions, blocks, after=()):
    pieces, order = shards
    coming = Coming(blocks)
    tokens, n = sum(piece.shape[0] for piece in pieces), len(positions)
    block, by_rows = weight.block, weight.by_rows
    keys = [(reverse(p, weight.bits), 1) for p in positions] + [(p, 0) for p in positions]

    def kernel(me_ref, *refs):
        piece_refs, refs = refs[: len(pieces)], refs[len(pieces) :]
        parts, refs = refs[: 2 * n], refs[2 * n :]
        sources, refs = refs[: len(coming.inputs)], refs[len(coming.inputs) :]
        keep, send, refs = refs[0], refs[1], refs[2:]
        left, copies = refs[len(blocks)], []
        if blocks:
            copies = coming.copies(sources, refs[: len(blocks)], refs[-1], me_ref[0])
        for copy in copies:
            copy.start()
        place(piece_refs, order, left)
        for i, part in enumerate(parts):
            out = dot(left[...], part[...], 1, 1 if by_rows else 0).astype(BF16)
            (send if i < n else keep)[i % n] = out
        for copy in copies:
            copy.wait()

    keep, send, *helds = call(
        kernel,
        [("smem", weight.me)]
        + in_vmem(pieces)
        + in_vmem([weight.held[key] for key in keys])
        + coming.inputs,
        [("vmem", ((n, tokens, block), BF16))] * 2 + coming.outs,
        0,
        0,
        after,
        [pltpu.VMEM((tokens, weight.width), BF16)] + coming.scratch,
    )
    coming.arrive(helds)
    return keep, send


def block_sum(weight, stacks, odds, cols, groups, after=()):
    width, by_rows, block = weight.width, weight.by_rows, weight.block
    chips = len(weight.held) // 2
    tokens = stacks[0].shape[0] // chips
    n, size = len(stacks), tokens // cols
    parts = [
        weight.held[(reverse(p, weight.bits) if odd else p, odd)]
        for odd in odds
        for p in range(chips)
    ]

    def kernel(*refs):
        stack_refs, part_refs, refs = refs[:n], refs[n : n + len(parts)], refs[n + len(parts) :]
        outs, total = refs[:-1], refs[-1]
        for i, part in enumerate(part_refs):
            p = i % chips
            value = stack_refs[i // chips][p * tokens : (p + 1) * tokens, :]
            term = dot(value, part[...], 1, 0 if by_rows else 1)
            total[...] = term if i == 0 else total[...] + term
        for group, out in zip(groups, outs):
            for i, q in enumerate(group):
                out[i * size : (i + 1) * size, :] = total[q * size : (q + 1) * size, :].astype(BF16)

    return call(
        kernel,
        in_vmem(stacks) + in_vmem(parts),
        [("vmem", ((len(group) * size, width), BF16)) for group in groups],
        2 * tokens * width * block * chips * n,
        2 * width * block * chips * n,
        after,
        [pltpu.VMEM((tokens, width), F32)],
    )


def weight_grad(weight, stacks, odds, shards, into=None):
    pieces, order = shards
    width, by_rows, block = weight.width, weight.by_rows, weight.block
    chips = len(weight.held) // 2
    tokens = stacks[0].shape[0] // chips
    halves = 2
    size = (block if by_rows else width) // halves
    keys = [
        (i, p, (reverse(p, weight.bits) if odd else p, odd))
        for p in range(chips)
        for i, odd in enumerate(odds)
    ]

    def kernel(me_ref, *refs):
        stack_refs, refs = refs[: len(stacks)], refs[len(stacks) :]
        piece_refs, refs = refs[: len(pieces)], refs[len(pieces) :]
        grad, other, turned, ready, sent = refs[-5:]
        place(piece_refs, order, other)
        if not by_rows:
            turned[...] = other[...].T
        me = me_ref[0]

        def writes(step):
            to = weight.part(grad, me, keys[step // halves][2])
            at = step % halves * size
            to = to.at[at : at + size, :]
            slot = step % WRITES
            return [
                pltpu.make_async_copy(
                    cut(ready.at[slot], i, WRITE_CUTS), cut(to, i, WRITE_CUTS), sent.at[slot, i]
                )
                for i in range(WRITE_CUTS)
            ]

        steps = len(keys) * halves
        for step in range(steps):
            if step >= WRITES:
                for write in writes(step - WRITES):
                    write.wait()
            i, p, key = keys[step // halves]
            stack, of = stack_refs[i], slice(p * tokens, (p + 1) * tokens)
            at = slice(step % halves * size, (step % halves + 1) * size)
            if by_rows:
                out = dot(stack[of, at], other[...], 0, 0)
            else:
                out = dot(turned[at, :], stack[of, :], 1, 0)
            ready[step % WRITES] = out.astype(BF16)
            for write in writes(step):
                write.start()
        for step in range(max(0, steps - WRITES), steps):
            for write in writes(step):
                write.wait()

    return call(
        kernel,
        [("smem", weight.me)]
        + in_vmem(stacks)
        + in_vmem(pieces)
        + ([("hbm", into)] if into is not None else []),
        [("hbm", (weight.value.shape, BF16))],
        2 * tokens * width * block * len(keys),
        2 * width * block * len(keys),
        (),
        [
            pltpu.VMEM((tokens, width), BF16),
            pltpu.VMEM((width, tokens), BF16),
            pltpu.VMEM((WRITES, size, width if by_rows else block), BF16),
            pltpu.SemaphoreType.DMA((WRITES, WRITE_CUTS)),
        ],
        into is not None,
    )[0]


def folded(terms, after=()):
    shape = (terms[0].shape[0] // 2, *terms[0].shape[1:])

    def kernel(*refs):
        keep, send = refs[-2:]
        for i in range(2 * shape[0]):
            total = sum(ref[i].astype(F32) for ref in refs[: len(terms)])
            if i % 2:
                send[i // 2] = total.astype(BF16)
            else:
                keep[i // 2] = total

    return call(kernel, in_vmem(terms), [("vmem", (shape, F32)), ("vmem", (shape, BF16))], 0, 0, after)


def summed_half(keep, got, count, after=()):
    size = keep.shape[0] // count

    def kernel(keep_ref, got_ref, *outs):
        for i, out in enumerate(outs):
            at = slice(i * size, (i + 1) * size)
            total = keep_ref[at, :].astype(F32) + got_ref[at, :].astype(F32)
            out[...] = total.astype(out.dtype)

    shape = (size, keep.shape[1])
    outs = [("vmem", (shape, F32))] + [("vmem", (shape, BF16))] * (count - 1)
    return call(kernel, in_vmem([keep, got]), outs, 0, 0, after)


def partly(terms):
    def kernel(*refs):
        refs[-1][...] = sum(ref[...].astype(F32) for ref in refs[:-1])

    return call(kernel, in_vmem(terms), [("vmem", (terms[0].shape, F32))], WEIGHTY, 0)[0]


def added(terms, space="vmem"):
    def kernel(*refs):
        refs[-1][...] = sum(ref[...].astype(F32) for ref in refs[: len(terms)]).astype(BF16)

    return call(kernel, in_vmem(terms), [(space, (terms[0].shape, BF16))], 0, 0)[0]


def activate(terms, after=()):
    def kernel(*refs):
        total = sum(ref[0].astype(F32) for ref in refs[: len(terms)])
        refs[-2][...] = total
        refs[-1][...] = gelu_fn(total).astype(BF16)

    shape = terms[0].shape[1:]
    outs = [("vmem", (shape, F32)), ("vmem", (shape, BF16))]
    return call(kernel, in_vmem(terms), outs, WEIGHTY, 0, after)


def activate_back(hidden, terms, after=()):
    def kernel(hidden_ref, *refs):
        total = sum(ref[0].astype(F32) for ref in refs[: len(terms)])
        refs[-1][...] = gelu_back(hidden_ref[...], total)

    outs = [("vmem", (hidden.shape, BF16))]
    return call(kernel, in_vmem([hidden, *terms]), outs, 0, 0, after)[0]


def exchange_col(parts, cols):
    return [parts[0]] + [swap(parts[q], "col", q, cols) for q in range(cols - 1, 0, -1)]


def summed(parts):
    return sum(part.astype(F32) for part in parts).astype(BF16)


def blocked(rows, cols, tokens, cotangent, w_in, w_out):
    LAST.clear()
    me = lax.axis_index("row").astype(jnp.int32).reshape(1)
    w_in, w_out = Weight(me, w_in, rows, False), Weight(me, w_out, rows, True)
    steps = rows.bit_length() - 2
    there, here = range(1, rows // 2, 2), range(0, rows // 2, 2)

    def keys(positions):
        return [(reverse(p, steps), 1) for p in positions] + [(p, 0) for p in positions]

    def across_all(terms):
        for step in range(1, steps):
            keep, send = folded(terms)
            terms = [keep, across(send, step, rows)]
        return terms

    def gathered(stack, first):
        for step in [0] if first else range(1, steps):
            stack = joined([stack, across(stack, step, rows)])
        return stack

    def other_core(value):
        return swap(value, "row", 1, rows)

    wanted = [(w, key) for w in (w_in, w_out) for key in keys(there) + keys(here)]
    share = len(wanted) // 16

    flips = [1 << bit for bit in range(cols.bit_length() - 1)][::-1]
    token_pieces, cot_pieces, order = [tokens], [cotangent], [0]
    for hop, flip in enumerate(flips):
        sent = joined(token_pieces) if hop else tokens
        token_pieces.append(swap(sent, "col", flip, cols))
        if hop:
            sent = joined(cot_pieces, (token_pieces[hop],))
            cot_pieces.append(swap(sent, "col", flips[hop - 1], cols))
        if hop < 2:
            load(wanted[5 * hop * share : 5 * (hop + 1) * share])
        order += [q ^ flip for q in order]
    sent = joined(cot_pieces, (token_pieces[-1],))
    cot_pieces.append(swap(sent, "col", flips[-1], cols))
    token_shards, cot_shards = (token_pieces, order), (cot_pieces, order)

    keep, sent = project(w_in, token_shards, there, [])
    got = other_core(sent)
    here_keep, here_sent = project(w_in, token_shards, here, [])
    terms = [here_keep, other_core(here_sent), across(added([keep, got]), 0, rows)]
    load(wanted[5 * min(2, len(flips)) * share : 12 * share])

    keep, sent = project(w_out, cot_shards, there, [])
    got = other_core(sent)
    terms = across_all(terms)
    came = across(added([keep, got]), 0, rows)
    load(wanted[12 * share :])
    hidden, act = activate(terms)
    here_keep, here_sent = project(w_out, cot_shards, here, [])
    got = other_core(here_sent)

    back_terms = across_all([partly([here_keep, came]), got])
    stack = gathered(act, True)
    grad_hidden = activate_back(hidden, back_terms)
    stack = gathered(stack, False)
    act = stack, other_core(stack)
    even, odd = range(0, cols, 2), range(1, cols, 2)
    keep, send = block_sum(w_out, act, (0, 1), cols, (even, odd))
    got = swap(send, "col", 1, cols)
    back_stack = gathered(grad_hidden, True)
    grad_w_out = weight_grad(w_out, act[:1], (0,), cot_shards)
    layer_out, *sums = summed_half(keep, got, len(even))
    layer_parts = [swap(part, "col", q, cols) for part, q in zip(sums, even[1:])]
    back_stack = gathered(back_stack, False)
    grad_hidden = back_stack, other_core(back_stack)
    grad_w_out = weight_grad(w_out, act[1:], (1,), cot_shards, grad_w_out)

    token_parts = block_sum(w_in, grad_hidden, (0, 1), cols, [[q] for q in range(cols)])
    layer_out = added([layer_out, *layer_parts], "window")
    grad_w_in = weight_grad(w_in, grad_hidden, (0, 1), token_shards)
    token_parts = exchange_col(token_parts, cols)
    return (layer_out, summed(token_parts), grad_w_in, grad_w_out)


def collective(tokens, cotangent, w_in, w_out):
    token_full = lax.all_gather(tokens, "col", axis=0, tiled=True)
    cot_full = lax.all_gather(cotangent, "col", axis=0, tiled=True)

    def over(value, axis):
        return lax.psum_scatter(value.astype(BF16), axis, scatter_dimension=0, tiled=True)

    hidden = over(dot(token_full, w_in, 1, 0), "row").astype(F32)
    grad_act = over(dot(cot_full, w_out, 1, 1), "row").astype(F32)
    act = lax.all_gather(gelu_fn(hidden).astype(BF16), "row", axis=0, tiled=True)
    grad_hidden = lax.all_gather(gelu_back(hidden, grad_act), "row", axis=0, tiled=True)
    layer_out = over(dot(act, w_out, 1, 0), "col")
    grad_tokens = over(dot(grad_hidden, w_in, 1, 1), "col")
    grad_w_in = dot(token_full, grad_hidden, 0, 0).astype(BF16)
    grad_w_out = dot(act, cot_full, 0, 0).astype(BF16)
    return (layer_out, grad_tokens, grad_w_in, grad_w_out)


def solution(mesh):
    rows, cols = mesh.shape["row"], mesh.shape["col"]

    def shards(tokens, cotangent, w_in, w_out):
        powers = rows & (rows - 1) == 0 and cols & (cols - 1) == 0
        if powers and rows > 4 and cols > 1 and w_in.shape[1] % (rows * 128) == 0:
            return blocked(rows, cols, tokens, cotangent, w_in, w_out)
        return collective(tokens, cotangent, w_in, w_out)

    return jax.shard_map(
        shards,
        mesh=mesh,
        in_specs=(P("col", "row"), P("col", "row"), P("row", "col"), P("col", "row")),
        out_specs=(P("col", "row"), P("col", "row"), P("row", "col"), P("col", "row")),
        check_vma=False,
    )
```

```python
import functools

import jax
import jax.numpy as jnp
from jax import lax
from jax.experimental import pallas as pl
from jax.experimental.pallas import tpu as pltpu
from jax.sharding import PartitionSpec as P

BF16 = jnp.bfloat16
F32 = jnp.float32
VMEM_LIMIT = 10 * 1024 * 1024
WRITES = 6
READ_CUTS, WRITE_CUTS = 4, 3
WEIGHTY = 6 * 10**9


def gelu_fn(value):
    return jax.nn.gelu(value, approximate=True)


def gelu_back(hidden, grad_act):
    unused, pullback = jax.vjp(gelu_fn, hidden)
    return pullback(grad_act)[0].astype(BF16)


def swap(value, axis, flip, count):
    return lax.ppermute(value, axis, [(i, i ^ flip) for i in range(count)])


def reverse(p, bits):
    return sum(((p >> j) & 1) << (bits - 1 - j) for j in range(bits))


def across(value, step, rows):
    bits = rows.bit_length() - 2
    flips = [2 << (bits - 1 - step if i & 1 else step) for i in range(rows)]
    return lax.ppermute(value, "row", [(i, i ^ flips[i]) for i in range(rows)])


def dot(left, right, left_dim, right_dim):
    return lax.dot_general(
        left, right, (((left_dim,), (right_dim,)), ((), ())), preferred_element_type=F32
    )


LAST = []


def call(kernel, arrays, outs, flops, moved, after=(), scratch=(), in_place=False):
    unread, count = [*LAST, *after], len(arrays)

    def body(*refs):
        kernel(*refs[:count], *refs[count + len(unread) :])

    specs = {
        "smem": pl.BlockSpec(memory_space=pltpu.SMEM),
        "vmem": pl.BlockSpec(memory_space=pltpu.VMEM),
        "hbm": pl.BlockSpec(memory_space=pl.ANY),
        "window": pl.BlockSpec(),
    }
    operands = []
    for space, value in arrays:
        if space != "smem":
            value = pltpu.with_memory_space_constraint(
                value, pltpu.HBM if space == "hbm" else pltpu.VMEM
            )
        operands.append(value)
    results = pl.pallas_call(
        body,
        in_specs=[specs[space] for space, value in arrays]
        + [pl.BlockSpec(memory_space=pl.ANY)] * len(unread),
        out_specs=[specs[space] for space, value in outs],
        scratch_shapes=list(scratch),
        input_output_aliases={count - 1: 0} if in_place else {},
        out_shape=[
            pltpu.VMEM(shape, dtype) if space == "vmem" else jax.ShapeDtypeStruct(shape, dtype)
            for space, (shape, dtype) in outs
        ],
        compiler_params=pltpu.CompilerParams(vmem_limit_bytes=VMEM_LIMIT),
        cost_estimate=pl.CostEstimate(flops=flops, bytes_accessed=moved, transcendentals=0),
    )(*operands, *unread)
    last = results[-1]
    if outs[-1][0] != "vmem":
        last = pltpu.with_memory_space_constraint(last, pltpu.HBM)
    LAST[:] = [last]
    return results


def in_vmem(values):
    return [("vmem", value) for value in values]


def join(pieces, out):
    at = 0
    for piece in pieces:
        out[at : at + piece.shape[0], :] = piece[...]
        at += piece.shape[0]


def place(pieces, order, out):
    size, order = pieces[0].shape[0], list(order)
    for piece in pieces:
        for at in range(0, piece.shape[0], size):
            to = order.pop(0) * size
            out[to : to + size, :] = piece[at : at + size, :]


def joined(pieces, after=()):
    rows = sum(piece.shape[0] for piece in pieces)

    def kernel(*refs):
        join(refs[: len(pieces)], refs[-1])

    return call(
        kernel, in_vmem(pieces), [("vmem", ((rows, pieces[0].shape[1]), BF16))], 0, 0, after
    )[0]


class Weight:
    def __init__(self, me, value, rows, by_rows):
        self.me, self.value, self.by_rows = me, value, by_rows
        self.bits = rows.bit_length() - 2
        self.block = value.shape[0 if by_rows else 1] // rows
        self.width = value.shape[1 if by_rows else 0]
        self.shape = (self.block, self.width) if by_rows else (self.width, self.block)
        self.held = {}

    def part(self, ref, me, key):
        p, odd = key
        chip = p + (me & 1) * (reverse(p, self.bits) - p)
        at = (me ^ (2 * chip + odd)) * self.block
        at = pl.ds(pl.multiple_of(at, 128), self.block)
        return ref.at[at, :] if self.by_rows else ref.at[:, at]


def cut(ref, i, cuts):
    size = ref.shape[0] // cuts
    return ref.at[i * size : (i + 1) * size, :]


class Coming:
    def __init__(self, blocks):
        self.blocks = blocks
        self.weights = list(dict.fromkeys(weight for weight, key in blocks))
        self.count = len(blocks) * READ_CUTS
        self.inputs = [("hbm", weight.value) for weight in self.weights]
        self.outs = [("vmem", (weight.shape, BF16)) for weight, key in blocks]
        self.scratch = [pltpu.SemaphoreType.DMA((self.count,))] if blocks else []

    def copies(self, sources, helds, arrived, me):
        return [
            pltpu.make_async_copy(
                cut(weight.part(sources[self.weights.index(weight)], me, key), i, READ_CUTS),
                cut(held, i, READ_CUTS),
                arrived.at[n * READ_CUTS + i],
            )
            for n, ((weight, key), held) in enumerate(zip(self.blocks, helds))
            for i in range(READ_CUTS)
        ]

    def arrive(self, helds):
        for (weight, key), held in zip(self.blocks, helds):
            weight.held[key] = held


def load(blocks, after=()):
    coming = Coming(blocks)
    n = len(coming.inputs)

    def kernel(me_ref, *refs):
        copies = coming.copies(refs[:n], refs[n:-1], refs[-1], me_ref[0])
        for copy in copies:
            copy.start()
        for copy in copies:
            copy.wait()

    me = blocks[0][0].me
    coming.arrive(
        call(kernel, [("smem", me), *coming.inputs], coming.outs, 0, 0, after, coming.scratch)
    )


def project(weight, shards, positions, blocks, after=()):
    pieces, order = shards
    coming = Coming(blocks)
    tokens, n = sum(piece.shape[0] for piece in pieces), len(positions)
    block, by_rows = weight.block, weight.by_rows
    keys = [(reverse(p, weight.bits), 1) for p in positions] + [(p, 0) for p in positions]

    def kernel(me_ref, *refs):
        piece_refs, refs = refs[: len(pieces)], refs[len(pieces) :]
        parts, refs = refs[: 2 * n], refs[2 * n :]
        sources, refs = refs[: len(coming.inputs)], refs[len(coming.inputs) :]
        keep, send, refs = refs[0], refs[1], refs[2:]
        left, copies = refs[len(blocks)], []
        if blocks:
            copies = coming.copies(sources, refs[: len(blocks)], refs[-1], me_ref[0])
        for copy in copies:
            copy.start()
        place(piece_refs, order, left)
        for i, part in enumerate(parts):
            out = dot(left[...], part[...], 1, 1 if by_rows else 0).astype(BF16)
            (send if i < n else keep)[i % n] = out
        for copy in copies:
            copy.wait()

    keep, send, *helds = call(
        kernel,
        [("smem", weight.me)]
        + in_vmem(pieces)
        + in_vmem([weight.held[key] for key in keys])
        + coming.inputs,
        [("vmem", ((n, tokens, block), BF16))] * 2 + coming.outs,
        0,
        0,
        after,
        [pltpu.VMEM((tokens, weight.width), BF16)] + coming.scratch,
    )
    coming.arrive(helds)
    return keep, send


def block_sum(weight, stacks, odds, cols, groups, after=()):
    width, by_rows, block = weight.width, weight.by_rows, weight.block
    chips = len(weight.held) // 2
    tokens = stacks[0].shape[0] // chips
    n, size = len(stacks), tokens // cols
    parts = [
        weight.held[(reverse(p, weight.bits) if odd else p, odd)]
        for odd in odds
        for p in range(chips)
    ]

    def kernel(*refs):
        stack_refs, part_refs, refs = refs[:n], refs[n : n + len(parts)], refs[n + len(parts) :]
        outs, total = refs[:-1], refs[-1]
        for i, part in enumerate(part_refs):
            p = i % chips
            value = stack_refs[i // chips][p * tokens : (p + 1) * tokens, :]
            term = dot(value, part[...], 1, 0 if by_rows else 1)
            total[...] = term if i == 0 else total[...] + term
        for group, out in zip(groups, outs):
            for i, q in enumerate(group):
                out[i * size : (i + 1) * size, :] = total[q * size : (q + 1) * size, :].astype(BF16)

    return call(
        kernel,
        in_vmem(stacks) + in_vmem(parts),
        [("vmem", ((len(group) * size, width), BF16)) for group in groups],
        2 * tokens * width * block * chips * n,
        2 * width * block * chips * n,
        after,
        [pltpu.VMEM((tokens, width), F32)],
    )


def weight_grad(weight, stacks, odds, shards, into=None):
    pieces, order = shards
    width, by_rows, block = weight.width, weight.by_rows, weight.block
    chips = len(weight.held) // 2
    tokens = stacks[0].shape[0] // chips
    halves = 2
    size = (block if by_rows else width) // halves
    keys = [
        (i, p, (reverse(p, weight.bits) if odd else p, odd))
        for p in range(chips)
        for i, odd in enumerate(odds)
    ]

    def kernel(me_ref, *refs):
        stack_refs, refs = refs[: len(stacks)], refs[len(stacks) :]
        piece_refs, refs = refs[: len(pieces)], refs[len(pieces) :]
        grad, other, turned, ready, sent = refs[-5:]
        place(piece_refs, order, other)
        if not by_rows:
            turned[...] = other[...].T
        me = me_ref[0]

        def writes(step):
            to = weight.part(grad, me, keys[step // halves][2])
            at = step % halves * size
            to = to.at[at : at + size, :]
            slot = step % WRITES
            return [
                pltpu.make_async_copy(
                    cut(ready.at[slot], i, WRITE_CUTS), cut(to, i, WRITE_CUTS), sent.at[slot, i]
                )
                for i in range(WRITE_CUTS)
            ]

        steps = len(keys) * halves
        for step in range(steps):
            if step >= WRITES:
                for write in writes(step - WRITES):
                    write.wait()
            i, p, key = keys[step // halves]
            stack, of = stack_refs[i], slice(p * tokens, (p + 1) * tokens)
            at = slice(step % halves * size, (step % halves + 1) * size)
            if by_rows:
                out = dot(stack[of, at], other[...], 0, 0)
            else:
                out = dot(turned[at, :], stack[of, :], 1, 0)
            ready[step % WRITES] = out.astype(BF16)
            for write in writes(step):
                write.start()
        for step in range(max(0, steps - WRITES), steps):
            for write in writes(step):
                write.wait()

    return call(
        kernel,
        [("smem", weight.me)]
        + in_vmem(stacks)
        + in_vmem(pieces)
        + ([("hbm", into)] if into is not None else []),
        [("hbm", (weight.value.shape, BF16))],
        2 * tokens * width * block * len(keys),
        2 * width * block * len(keys),
        (),
        [
            pltpu.VMEM((tokens, width), BF16),
            pltpu.VMEM((width, tokens), BF16),
            pltpu.VMEM((WRITES, size, width if by_rows else block), BF16),
            pltpu.SemaphoreType.DMA((WRITES, WRITE_CUTS)),
        ],
        into is not None,
    )[0]


def summed_half(keep, got, count, after=()):
    size = keep.shape[0] // count

    def kernel(keep_ref, got_ref, *outs):
        for i, out in enumerate(outs):
            at = slice(i * size, (i + 1) * size)
            total = keep_ref[at, :].astype(F32) + got_ref[at, :].astype(F32)
            out[...] = total.astype(out.dtype)

    shape = (size, keep.shape[1])
    outs = [("vmem", (shape, F32))] + [("vmem", (shape, BF16))] * (count - 1)
    return call(kernel, in_vmem([keep, got]), outs, 0, 0, after)


def added(terms, space="vmem"):
    def kernel(*refs):
        refs[-1][...] = sum(ref[...].astype(F32) for ref in refs[: len(terms)]).astype(BF16)

    return call(kernel, in_vmem(terms), [(space, (terms[0].shape, BF16))], 0, 0)[0]


def block_of(terms):
    def total(refs):
        return sum(ref[block].astype(F32) for ref, (array, block) in zip(refs, terms))

    return total


def sent_sum(terms):
    def kernel(*refs):
        refs[-1][0] = block_of(terms)(refs).astype(BF16)

    shape = (1, *terms[0][0].shape[1:])
    return call(kernel, in_vmem([array for array, block in terms]), [("vmem", (shape, BF16))], 0, 0)[0]


def activate(terms):
    def kernel(*refs):
        total = block_of(terms)(refs)
        refs[-2][...] = total
        refs[-1][...] = gelu_fn(total).astype(BF16)

    shape = terms[0][0].shape[1:]
    outs = [("vmem", (shape, F32)), ("vmem", (shape, BF16))]
    return call(kernel, in_vmem([array for array, block in terms]), outs, WEIGHTY, 0)


def activate_back(hidden, terms):
    def kernel(hidden_ref, *refs):
        refs[-1][...] = gelu_back(hidden_ref[...], block_of(terms)(refs))

    arrays = [hidden] + [array for array, block in terms]
    return call(kernel, in_vmem(arrays), [("vmem", (hidden.shape, BF16))], WEIGHTY, 0)[0]


def exchange_col(parts, cols):
    return [parts[0]] + [swap(parts[q], "col", q, cols) for q in range(cols - 1, 0, -1)]


def summed(parts):
    return sum(part.astype(F32) for part in parts).astype(BF16)


def blocked(rows, cols, tokens, cotangent, w_in, w_out):
    LAST.clear()
    me = lax.axis_index("row").astype(jnp.int32).reshape(1)
    w_in, w_out = Weight(me, w_in, rows, False), Weight(me, w_out, rows, True)
    first, second, own = [1, 3], [2], [0]

    def keys(positions):
        return [(reverse(p, 2), 1) for p in positions] + [(p, 0) for p in positions]

    def other_core(value):
        return swap(value, "row", 1, rows)

    def doubled(stack, step):
        return joined([stack, across(stack, step, rows)])

    wanted = [(w, key) for w in (w_in, w_out) for part in (first, second, own) for key in keys(part)]

    flips = [1 << bit for bit in range(cols.bit_length() - 1)][::-1]
    token_pieces, cot_pieces, order = [tokens], [cotangent], [0]
    for hop, flip in enumerate(flips):
        sent = joined(token_pieces) if hop else tokens
        token_pieces.append(swap(sent, "col", flip, cols))
        if hop:
            sent = joined(cot_pieces, (token_pieces[hop],))
            cot_pieces.append(swap(sent, "col", flips[hop - 1], cols))
        if hop < 2:
            load(wanted[5 * hop : 5 * hop + 5])
        order += [q ^ flip for q in order]
    sent = joined(cot_pieces, (token_pieces[-1],))
    cot_pieces.append(swap(sent, "col", flips[-1], cols))
    token_shards, cot_shards = (token_pieces, order), (cot_pieces, order)

    keep, sent = project(w_in, token_shards, first, [])
    got = other_core(sent)
    here, sent = project(w_in, token_shards, second + own, [])
    got_here, came = other_core(sent), across(added([keep, got]), 0, rows)
    load(wanted[5 * min(2, len(flips)) : 12])
    keep, sent = project(w_out, cot_shards, first, [])
    got = other_core(sent)
    sent = sent_sum([(here, 0), (got_here, 0), (came, 1)])
    terms = [(here, 1), (got_here, 1), (came, 0), (across(sent, 1, rows), 0)]

    came = across(added([keep, got]), 0, rows)
    load(wanted[12:14])
    keep, sent = project(w_out, cot_shards, second, [])
    got = other_core(sent)
    hidden, act = activate(terms)
    sent = sent_sum([(keep, 0), (got, 0), (came, 1)])
    last = across(sent, 1, rows)
    load(wanted[14:])
    stack = doubled(act, 0)
    keep, sent = project(w_out, cot_shards, own, [])
    got = other_core(sent)
    grad_hidden = activate_back(hidden, [(keep, 0), (came, 0), (last, 0), (got, 0)])
    stack = doubled(stack, 1)
    act = stack, other_core(stack)
    grad_w_out = weight_grad(w_out, act[:1], (0,), cot_shards)
    back_stack = doubled(grad_hidden, 0)

    even, odd = range(0, cols, 2), range(1, cols, 2)
    keep, send = block_sum(w_out, act, (0, 1), cols, (even, odd))
    got = swap(send, "col", 1, cols)
    grad_w_out = weight_grad(w_out, act[1:], (1,), cot_shards, grad_w_out)
    layer_out, *sums = summed_half(keep, got, len(even))
    layer_parts = [swap(part, "col", q, cols) for part, q in zip(sums, even[1:])]
    back_stack = doubled(back_stack, 1)
    grad_hidden = back_stack, other_core(back_stack)

    token_parts = block_sum(w_in, grad_hidden, (0, 1), cols, [[q] for q in range(cols)])
    layer_out = added([layer_out, *layer_parts], "window")
    grad_w_in = weight_grad(w_in, grad_hidden, (0, 1), token_shards)
    token_parts = exchange_col(token_parts, cols)
    return (layer_out, summed(token_parts), grad_w_in, grad_w_out)


def collective(tokens, cotangent, w_in, w_out):
    token_full = lax.all_gather(tokens, "col", axis=0, tiled=True)
    cot_full = lax.all_gather(cotangent, "col", axis=0, tiled=True)

    def over(value, axis):
        return lax.psum_scatter(value.astype(BF16), axis, scatter_dimension=0, tiled=True)

    hidden = over(dot(token_full, w_in, 1, 0), "row").astype(F32)
    grad_act = over(dot(cot_full, w_out, 1, 1), "row").astype(F32)
    act = lax.all_gather(gelu_fn(hidden).astype(BF16), "row", axis=0, tiled=True)
    grad_hidden = lax.all_gather(gelu_back(hidden, grad_act), "row", axis=0, tiled=True)
    layer_out = over(dot(act, w_out, 1, 0), "col")
    grad_tokens = over(dot(grad_hidden, w_in, 1, 1), "col")
    grad_w_in = dot(token_full, grad_hidden, 0, 0).astype(BF16)
    grad_w_out = dot(act, cot_full, 0, 0).astype(BF16)
    return (layer_out, grad_tokens, grad_w_in, grad_w_out)


def solution(mesh):
    rows, cols = mesh.shape["row"], mesh.shape["col"]

    def shards(tokens, cotangent, w_in, w_out):
        powers = rows & (rows - 1) == 0 and cols & (cols - 1) == 0
        if powers and rows == 8 and cols > 1 and w_in.shape[1] % (rows * 128) == 0:
            return blocked(rows, cols, tokens, cotangent, w_in, w_out)
        return collective(tokens, cotangent, w_in, w_out)

    return jax.shard_map(
        shards,
        mesh=mesh,
        in_specs=(P("col", "row"), P("col", "row"), P("row", "col"), P("col", "row")),
        out_specs=(P("col", "row"), P("col", "row"), P("row", "col"), P("col", "row")),
        check_vma=False,
    )
```

```python
import functools

import jax
import jax.numpy as jnp
from jax import lax
from jax.experimental import pallas as pl
from jax.experimental.pallas import tpu as pltpu
from jax.sharding import PartitionSpec as P

BF16 = jnp.bfloat16
F32 = jnp.float32
VMEM_LIMIT = 10 * 1024 * 1024
WRITES = 6
READ_CUTS, WRITE_CUTS = 4, 3
PART_COST = 10**9


def gelu_fn(value):
    return jax.nn.gelu(value, approximate=True)


def gelu_back(hidden, grad_act):
    unused, pullback = jax.vjp(gelu_fn, hidden)
    return pullback(grad_act)[0].astype(BF16)


def swap(value, axis, flip, count):
    return lax.ppermute(value, axis, [(i, i ^ flip) for i in range(count)])


def reverse(p, bits):
    return sum(((p >> j) & 1) << (bits - 1 - j) for j in range(bits))


def across(value, step, rows):
    bits = rows.bit_length() - 2
    flips = [2 << (bits - 1 - step if i & 1 else step) for i in range(rows)]
    return lax.ppermute(value, "row", [(i, i ^ flips[i]) for i in range(rows)])


def dot(left, right, left_dim, right_dim):
    return lax.dot_general(
        left, right, (((left_dim,), (right_dim,)), ((), ())), preferred_element_type=F32
    )


LAST = []


def call(kernel, arrays, outs, flops, moved, after=(), scratch=(), in_place=False):
    unread, count = [*LAST, *after], len(arrays)

    def body(*refs):
        kernel(*refs[:count], *refs[count + len(unread) :])

    specs = {
        "smem": pl.BlockSpec(memory_space=pltpu.SMEM),
        "vmem": pl.BlockSpec(memory_space=pltpu.VMEM),
        "hbm": pl.BlockSpec(memory_space=pl.ANY),
        "window": pl.BlockSpec(),
    }
    operands = []
    for space, value in arrays:
        if space != "smem":
            value = pltpu.with_memory_space_constraint(
                value, pltpu.HBM if space == "hbm" else pltpu.VMEM
            )
        operands.append(value)
    results = pl.pallas_call(
        body,
        in_specs=[specs[space] for space, value in arrays]
        + [pl.BlockSpec(memory_space=pl.ANY)] * len(unread),
        out_specs=[specs[space] for space, value in outs],
        scratch_shapes=list(scratch),
        input_output_aliases={count - 1: 0} if in_place else {},
        out_shape=[
            pltpu.VMEM(shape, dtype) if space == "vmem" else jax.ShapeDtypeStruct(shape, dtype)
            for space, (shape, dtype) in outs
        ],
        compiler_params=pltpu.CompilerParams(vmem_limit_bytes=VMEM_LIMIT),
        cost_estimate=pl.CostEstimate(flops=flops, bytes_accessed=moved, transcendentals=0),
    )(*operands, *unread)
    last = results[-1]
    if outs[-1][0] != "vmem":
        last = pltpu.with_memory_space_constraint(last, pltpu.HBM)
    LAST[:] = [last]
    return results


def in_vmem(values):
    return [("vmem", value) for value in values]


def join(pieces, out):
    at = 0
    for piece in pieces:
        out[at : at + piece.shape[0], :] = piece[...]
        at += piece.shape[0]


def place(pieces, order, out):
    size, order = pieces[0].shape[0], list(order)
    for piece in pieces:
        for at in range(0, piece.shape[0], size):
            to = order.pop(0) * size
            out[to : to + size, :] = piece[at : at + size, :]


def joined(pieces, after=()):
    rows = sum(piece.shape[0] for piece in pieces)

    def kernel(*refs):
        join(refs[: len(pieces)], refs[-1])

    return call(
        kernel, in_vmem(pieces), [("vmem", ((rows, pieces[0].shape[1]), BF16))], 0, 0, after
    )[0]


class Weight:
    def __init__(self, me, value, rows, by_rows):
        self.me, self.value, self.by_rows = me, value, by_rows
        self.bits = rows.bit_length() - 2
        self.block = value.shape[0 if by_rows else 1] // rows
        self.width = value.shape[1 if by_rows else 0]
        self.shape = (self.block, self.width) if by_rows else (self.width, self.block)
        self.held = {}

    def part(self, ref, me, key):
        p, odd = key
        chip = p + (me & 1) * (reverse(p, self.bits) - p)
        at = (me ^ (2 * chip + odd)) * self.block
        at = pl.ds(pl.multiple_of(at, 128), self.block)
        return ref.at[at, :] if self.by_rows else ref.at[:, at]


def cut(ref, i, cuts):
    size = ref.shape[0] // cuts
    return ref.at[i * size : (i + 1) * size, :]


class Coming:
    def __init__(self, blocks):
        self.blocks = blocks
        self.weights = list(dict.fromkeys(weight for weight, key in blocks))
        self.count = len(blocks) * READ_CUTS
        self.inputs = [("hbm", weight.value) for weight in self.weights]
        self.outs = [("vmem", (weight.shape, BF16)) for weight, key in blocks]
        self.scratch = [pltpu.SemaphoreType.DMA((self.count,))] if blocks else []

    def copies(self, sources, helds, arrived, me):
        return [
            pltpu.make_async_copy(
                cut(weight.part(sources[self.weights.index(weight)], me, key), i, READ_CUTS),
                cut(held, i, READ_CUTS),
                arrived.at[n * READ_CUTS + i],
            )
            for n, ((weight, key), held) in enumerate(zip(self.blocks, helds))
            for i in range(READ_CUTS)
        ]

    def arrive(self, helds):
        for (weight, key), held in zip(self.blocks, helds):
            weight.held[key] = held


def load(blocks, after=()):
    coming = Coming(blocks)
    n = len(coming.inputs)

    def kernel(me_ref, *refs):
        copies = coming.copies(refs[:n], refs[n:-1], refs[-1], me_ref[0])
        for copy in copies:
            copy.start()
        for copy in copies:
            copy.wait()

    me = blocks[0][0].me
    coming.arrive(
        call(kernel, [("smem", me), *coming.inputs], coming.outs, 0, 0, after, coming.scratch)
    )


def project(weight, shards, positions, blocks, after=()):
    pieces, order = shards
    coming = Coming(blocks)
    tokens, n = sum(piece.shape[0] for piece in pieces), len(positions)
    block, by_rows = weight.block, weight.by_rows
    keys = [(reverse(p, weight.bits), 1) for p in positions] + [(p, 0) for p in positions]

    def kernel(me_ref, *refs):
        piece_refs, refs = refs[: len(pieces)], refs[len(pieces) :]
        parts, refs = refs[: 2 * n], refs[2 * n :]
        sources, refs = refs[: len(coming.inputs)], refs[len(coming.inputs) :]
        keep, send, refs = refs[0], refs[1], refs[2:]
        left, copies = refs[len(blocks)], []
        if blocks:
            copies = coming.copies(sources, refs[: len(blocks)], refs[-1], me_ref[0])
        for copy in copies:
            copy.start()
        place(piece_refs, order, left)
        for i, part in enumerate(parts):
            out = dot(left[...], part[...], 1, 1 if by_rows else 0).astype(BF16)
            (send if i < n else keep)[i % n] = out
        for copy in copies:
            copy.wait()

    keep, send, *helds = call(
        kernel,
        [("smem", weight.me)]
        + in_vmem(pieces)
        + in_vmem([weight.held[key] for key in keys])
        + coming.inputs,
        [("vmem", ((n, tokens, block), BF16))] * 2 + coming.outs,
        0,
        0,
        after,
        [pltpu.VMEM((tokens, weight.width), BF16)] + coming.scratch,
    )
    coming.arrive(helds)
    return keep, send


def block_sum(weight, stacks, odds, cols, groups, after=()):
    width, by_rows, block = weight.width, weight.by_rows, weight.block
    chips = len(weight.held) // 2
    tokens = stacks[0].shape[0] // chips
    n, size = len(stacks), tokens // cols
    parts = [
        weight.held[(reverse(p, weight.bits) if odd else p, odd)]
        for odd in odds
        for p in range(chips)
    ]

    def kernel(*refs):
        stack_refs, part_refs, refs = refs[:n], refs[n : n + len(parts)], refs[n + len(parts) :]
        outs, total = refs[:-1], refs[-1]
        for i, part in enumerate(part_refs):
            p = i % chips
            value = stack_refs[i // chips][p * tokens : (p + 1) * tokens, :]
            term = dot(value, part[...], 1, 0 if by_rows else 1)
            total[...] = term if i == 0 else total[...] + term
        for group, out in zip(groups, outs):
            for i, q in enumerate(group):
                out[i * size : (i + 1) * size, :] = total[q * size : (q + 1) * size, :].astype(BF16)

    return call(
        kernel,
        in_vmem(stacks) + in_vmem(parts),
        [("vmem", ((len(group) * size, width), BF16)) for group in groups],
        2 * tokens * width * block * chips * n,
        2 * width * block * chips * n,
        after,
        [pltpu.VMEM((tokens, width), F32)],
    )


def weight_grad(weight, stacks, odds, shards, into=None):
    pieces, order = shards
    width, by_rows, block = weight.width, weight.by_rows, weight.block
    chips = len(weight.held) // 2
    tokens = stacks[0].shape[0] // chips
    halves = 2
    size = (block if by_rows else width) // halves
    keys = [
        (i, p, (reverse(p, weight.bits) if odd else p, odd))
        for p in range(chips)
        for i, odd in enumerate(odds)
    ]

    def kernel(me_ref, *refs):
        stack_refs, refs = refs[: len(stacks)], refs[len(stacks) :]
        piece_refs, refs = refs[: len(pieces)], refs[len(pieces) :]
        grad, other, turned, ready, sent = refs[-5:]
        place(piece_refs, order, other)
        if not by_rows:
            turned[...] = other[...].T
        me = me_ref[0]

        def writes(step):
            to = weight.part(grad, me, keys[step // halves][2])
            at = step % halves * size
            to = to.at[at : at + size, :]
            slot = step % WRITES
            return [
                pltpu.make_async_copy(
                    cut(ready.at[slot], i, WRITE_CUTS), cut(to, i, WRITE_CUTS), sent.at[slot, i]
                )
                for i in range(WRITE_CUTS)
            ]

        steps = len(keys) * halves
        for step in range(steps):
            if step >= WRITES:
                for write in writes(step - WRITES):
                    write.wait()
            i, p, key = keys[step // halves]
            stack, of = stack_refs[i], slice(p * tokens, (p + 1) * tokens)
            at = slice(step % halves * size, (step % halves + 1) * size)
            if by_rows:
                out = dot(stack[of, at], other[...], 0, 0)
            else:
                out = dot(turned[at, :], stack[of, :], 1, 0)
            ready[step % WRITES] = out.astype(BF16)
            for write in writes(step):
                write.start()
        for step in range(max(0, steps - WRITES), steps):
            for write in writes(step):
                write.wait()

    return call(
        kernel,
        [("smem", weight.me)]
        + in_vmem(stacks)
        + in_vmem(pieces)
        + ([("hbm", into)] if into is not None else []),
        [("hbm", (weight.value.shape, BF16))],
        2 * tokens * width * block * len(keys),
        2 * width * block * len(keys),
        (),
        [
            pltpu.VMEM((tokens, width), BF16),
            pltpu.VMEM((width, tokens), BF16),
            pltpu.VMEM((WRITES, size, width if by_rows else block), BF16),
            pltpu.SemaphoreType.DMA((WRITES, WRITE_CUTS)),
        ],
        into is not None,
    )[0]


def summed_half(keep, got, count, after=()):
    size = keep.shape[0] // count

    def kernel(keep_ref, got_ref, *outs):
        for i, out in enumerate(outs):
            at = slice(i * size, (i + 1) * size)
            total = keep_ref[at, :].astype(F32) + got_ref[at, :].astype(F32)
            out[...] = total.astype(out.dtype)

    shape = (size, keep.shape[1])
    outs = [("vmem", (shape, F32))] + [("vmem", (shape, BF16))] * (count - 1)
    return call(kernel, in_vmem([keep, got]), outs, 0, 0, after)


def added(terms, space="vmem"):
    def kernel(*refs):
        refs[-1][...] = sum(ref[...].astype(F32) for ref in refs[: len(terms)]).astype(BF16)

    return call(kernel, in_vmem(terms), [(space, (terms[0].shape, BF16))], 0, 0)[0]


def block_of(terms):
    def total(refs):
        return sum(ref[block].astype(F32) for ref, (array, block) in zip(refs, terms))

    return total


def one_block(terms, dtype=BF16, flops=0):
    def kernel(*refs):
        refs[-1][0] = block_of(terms)(refs).astype(dtype)

    shape = (1, *terms[0][0].shape[1:])
    arrays = in_vmem([array for array, block in terms])
    return call(kernel, arrays, [("vmem", (shape, dtype))], flops, 0)[0]


def activate(terms):
    def kernel(*refs):
        total = block_of(terms)(refs)
        refs[-2][...] = total
        refs[-1][...] = gelu_fn(total).astype(BF16)

    shape = terms[0][0].shape[1:]
    outs = [("vmem", (shape, F32)), ("vmem", (shape, BF16))]
    return call(kernel, in_vmem([array for array, block in terms]), outs, 0, 0)


def activate_back(hidden, terms):
    def kernel(hidden_ref, *refs):
        refs[-1][...] = gelu_back(hidden_ref[...], block_of(terms)(refs))

    arrays = [hidden] + [array for array, block in terms]
    return call(kernel, in_vmem(arrays), [("vmem", (hidden.shape, BF16))], 0, 0)[0]


def exchange_col(parts, cols):
    return [parts[0]] + [swap(parts[q], "col", q, cols) for q in range(cols - 1, 0, -1)]


def summed(parts):
    return sum(part.astype(F32) for part in parts).astype(BF16)


def blocked(rows, cols, tokens, cotangent, w_in, w_out):
    LAST.clear()
    me = lax.axis_index("row").astype(jnp.int32).reshape(1)
    w_in, w_out = Weight(me, w_in, rows, False), Weight(me, w_out, rows, True)
    first, second, own = [1, 3], [2], [0]

    def keys(positions):
        return [(reverse(p, 2), 1) for p in positions] + [(p, 0) for p in positions]

    def other_core(value):
        return swap(value, "row", 1, rows)

    def doubled(stack, step):
        return joined([stack, across(stack, step, rows)])

    wanted = [(w, key) for w in (w_in, w_out) for part in (first, second, own) for key in keys(part)]

    flips = [1 << bit for bit in range(cols.bit_length() - 1)][::-1]
    token_pieces, cot_pieces, order = [tokens], [cotangent], [0]
    for hop, flip in enumerate(flips):
        sent = joined(token_pieces) if hop else tokens
        token_pieces.append(swap(sent, "col", flip, cols))
        if hop:
            sent = joined(cot_pieces, (token_pieces[hop],))
            cot_pieces.append(swap(sent, "col", flips[hop - 1], cols))
        if hop < 2:
            load(wanted[5 * hop : 5 * hop + 5])
        order += [q ^ flip for q in order]
    sent = joined(cot_pieces, (token_pieces[-1],))
    cot_pieces.append(swap(sent, "col", flips[-1], cols))
    token_shards, cot_shards = (token_pieces, order), (cot_pieces, order)

    keep, sent = project(w_in, token_shards, first, [])
    got = other_core(sent)
    here, sent = project(w_in, token_shards, second + own, [])
    got_here, came = other_core(sent), across(added([keep, got]), 0, rows)
    load(wanted[5 * min(2, len(flips)) : 12])
    keep, sent = project(w_out, cot_shards, first, [])
    got = other_core(sent)
    sent = one_block([(here, 0), (got_here, 0), (came, 1)])
    terms = [(here, 1), (got_here, 1), (came, 0), (across(sent, 1, rows), 0)]

    came = across(added([keep, got]), 0, rows)
    load(wanted[12:14])
    hidden, act = activate(terms)
    keep, sent = project(w_out, cot_shards, second, [])
    got = other_core(sent)
    stack = doubled(act, 0)
    sent = one_block([(keep, 0), (got, 0), (came, 1)])
    last = across(sent, 1, rows)
    load(wanted[14:])
    keep, sent = project(w_out, cot_shards, own, [])
    got = other_core(sent)
    part = one_block([(came, 0), (last, 0)], F32, PART_COST)
    grad_hidden = activate_back(hidden, [(keep, 0), (part, 0), (got, 0)])
    stack = doubled(stack, 1)
    act = stack, other_core(stack)
    grad_w_out = weight_grad(w_out, act[:1], (0,), cot_shards)
    back_stack = doubled(grad_hidden, 0)

    even, odd = range(0, cols, 2), range(1, cols, 2)
    keep, send = block_sum(w_out, act, (0, 1), cols, (even, odd))
    got = swap(send, "col", 1, cols)
    grad_w_out = weight_grad(w_out, act[1:], (1,), cot_shards, grad_w_out)
    layer_out, *sums = summed_half(keep, got, len(even))
    layer_parts = [swap(part, "col", q, cols) for part, q in zip(sums, even[1:])]
    back_stack = doubled(back_stack, 1)
    grad_hidden = back_stack, other_core(back_stack)

    token_parts = block_sum(w_in, grad_hidden, (0, 1), cols, [[q] for q in range(cols)])
    layer_out = added([layer_out, *layer_parts], "window")
    grad_w_in = weight_grad(w_in, grad_hidden, (0, 1), token_shards)
    token_parts = exchange_col(token_parts, cols)
    return (layer_out, summed(token_parts), grad_w_in, grad_w_out)


def collective(tokens, cotangent, w_in, w_out):
    token_full = lax.all_gather(tokens, "col", axis=0, tiled=True)
    cot_full = lax.all_gather(cotangent, "col", axis=0, tiled=True)

    def over(value, axis):
        return lax.psum_scatter(value.astype(BF16), axis, scatter_dimension=0, tiled=True)

    hidden = over(dot(token_full, w_in, 1, 0), "row").astype(F32)
    grad_act = over(dot(cot_full, w_out, 1, 1), "row").astype(F32)
    act = lax.all_gather(gelu_fn(hidden).astype(BF16), "row", axis=0, tiled=True)
    grad_hidden = lax.all_gather(gelu_back(hidden, grad_act), "row", axis=0, tiled=True)
    layer_out = over(dot(act, w_out, 1, 0), "col")
    grad_tokens = over(dot(grad_hidden, w_in, 1, 1), "col")
    grad_w_in = dot(token_full, grad_hidden, 0, 0).astype(BF16)
    grad_w_out = dot(act, cot_full, 0, 0).astype(BF16)
    return (layer_out, grad_tokens, grad_w_in, grad_w_out)


def solution(mesh):
    rows, cols = mesh.shape["row"], mesh.shape["col"]

    def shards(tokens, cotangent, w_in, w_out):
        powers = rows & (rows - 1) == 0 and cols & (cols - 1) == 0
        if powers and rows == 8 and cols > 1 and w_in.shape[1] % (rows * 128) == 0:
            return blocked(rows, cols, tokens, cotangent, w_in, w_out)
        return collective(tokens, cotangent, w_in, w_out)

    return jax.shard_map(
        shards,
        mesh=mesh,
        in_specs=(P("col", "row"), P("col", "row"), P("row", "col"), P("col", "row")),
        out_specs=(P("col", "row"), P("col", "row"), P("row", "col"), P("col", "row")),
        check_vma=False,
    )
```

```python
import functools

import jax
import jax.numpy as jnp
from jax import lax
from jax.experimental import pallas as pl
from jax.experimental.pallas import tpu as pltpu
from jax.sharding import PartitionSpec as P

BF16 = jnp.bfloat16
F32 = jnp.float32
VMEM_LIMIT = 10 * 1024 * 1024
WRITES = 6
READ_CUTS, WRITE_CUTS = 4, 3
PART_COST = 6 * 10**9


def gelu_fn(value):
    return jax.nn.gelu(value, approximate=True)


def gelu_back(hidden, grad_act):
    unused, pullback = jax.vjp(gelu_fn, hidden)
    return pullback(grad_act)[0].astype(BF16)


def swap(value, axis, flip, count):
    return lax.ppermute(value, axis, [(i, i ^ flip) for i in range(count)])


def reverse(p, bits):
    return sum(((p >> j) & 1) << (bits - 1 - j) for j in range(bits))


def across(value, step, rows):
    bits = rows.bit_length() - 2
    flips = [2 << (bits - 1 - step if i & 1 else step) for i in range(rows)]
    return lax.ppermute(value, "row", [(i, i ^ flips[i]) for i in range(rows)])


def dot(left, right, left_dim, right_dim):
    return lax.dot_general(
        left, right, (((left_dim,), (right_dim,)), ((), ())), preferred_element_type=F32
    )


LAST = []


def call(kernel, arrays, outs, flops, moved, after=(), scratch=(), in_place=False):
    unread, count = [*LAST, *after], len(arrays)

    def body(*refs):
        kernel(*refs[:count], *refs[count + len(unread) :])

    specs = {
        "smem": pl.BlockSpec(memory_space=pltpu.SMEM),
        "vmem": pl.BlockSpec(memory_space=pltpu.VMEM),
        "hbm": pl.BlockSpec(memory_space=pl.ANY),
        "window": pl.BlockSpec(),
    }
    operands = []
    for space, value in arrays:
        if space != "smem":
            value = pltpu.with_memory_space_constraint(
                value, pltpu.HBM if space == "hbm" else pltpu.VMEM
            )
        operands.append(value)
    results = pl.pallas_call(
        body,
        in_specs=[specs[space] for space, value in arrays]
        + [pl.BlockSpec(memory_space=pl.ANY)] * len(unread),
        out_specs=[specs[space] for space, value in outs],
        scratch_shapes=list(scratch),
        input_output_aliases={count - 1: 0} if in_place else {},
        out_shape=[
            pltpu.VMEM(shape, dtype) if space == "vmem" else jax.ShapeDtypeStruct(shape, dtype)
            for space, (shape, dtype) in outs
        ],
        compiler_params=pltpu.CompilerParams(vmem_limit_bytes=VMEM_LIMIT),
        cost_estimate=pl.CostEstimate(flops=flops, bytes_accessed=moved, transcendentals=0),
    )(*operands, *unread)
    last = results[-1]
    if outs[-1][0] != "vmem":
        last = pltpu.with_memory_space_constraint(last, pltpu.HBM)
    LAST[:] = [last]
    return results


def in_vmem(values):
    return [("vmem", value) for value in values]


def join(pieces, out):
    at = 0
    for piece in pieces:
        out[at : at + piece.shape[0], :] = piece[...]
        at += piece.shape[0]


def place(pieces, order, out):
    size, order = pieces[0].shape[0], list(order)
    for piece in pieces:
        for at in range(0, piece.shape[0], size):
            to = order.pop(0) * size
            out[to : to + size, :] = piece[at : at + size, :]


def joined(pieces, after=(), flops=0):
    rows = sum(piece.shape[0] for piece in pieces)

    def kernel(*refs):
        join(refs[: len(pieces)], refs[-1])

    return call(
        kernel, in_vmem(pieces), [("vmem", ((rows, pieces[0].shape[1]), BF16))], flops, 0, after
    )[0]


class Weight:
    def __init__(self, me, value, rows, by_rows):
        self.me, self.value, self.by_rows = me, value, by_rows
        self.bits = rows.bit_length() - 2
        self.block = value.shape[0 if by_rows else 1] // rows
        self.width = value.shape[1 if by_rows else 0]
        self.shape = (self.block, self.width) if by_rows else (self.width, self.block)
        self.held = {}

    def part(self, ref, me, key):
        p, odd = key
        chip = p + (me & 1) * (reverse(p, self.bits) - p)
        at = (me ^ (2 * chip + odd)) * self.block
        at = pl.ds(pl.multiple_of(at, 128), self.block)
        return ref.at[at, :] if self.by_rows else ref.at[:, at]


def cut(ref, i, cuts):
    size = ref.shape[0] // cuts
    return ref.at[i * size : (i + 1) * size, :]


class Coming:
    def __init__(self, blocks):
        self.blocks = blocks
        self.weights = list(dict.fromkeys(weight for weight, key in blocks))
        self.count = len(blocks) * READ_CUTS
        self.inputs = [("hbm", weight.value) for weight in self.weights]
        self.outs = [("vmem", (weight.shape, BF16)) for weight, key in blocks]
        self.scratch = [pltpu.SemaphoreType.DMA((self.count,))] if blocks else []

    def copies(self, sources, helds, arrived, me):
        return [
            pltpu.make_async_copy(
                cut(weight.part(sources[self.weights.index(weight)], me, key), i, READ_CUTS),
                cut(held, i, READ_CUTS),
                arrived.at[n * READ_CUTS + i],
            )
            for n, ((weight, key), held) in enumerate(zip(self.blocks, helds))
            for i in range(READ_CUTS)
        ]

    def arrive(self, helds):
        for (weight, key), held in zip(self.blocks, helds):
            weight.held[key] = held


def load(blocks, after=()):
    coming = Coming(blocks)
    n = len(coming.inputs)

    def kernel(me_ref, *refs):
        copies = coming.copies(refs[:n], refs[n:-1], refs[-1], me_ref[0])
        for copy in copies:
            copy.start()
        for copy in copies:
            copy.wait()

    me = blocks[0][0].me
    coming.arrive(
        call(kernel, [("smem", me), *coming.inputs], coming.outs, 0, 0, after, coming.scratch)
    )


def project(weight, shards, positions, blocks, after=()):
    pieces, order = shards
    coming = Coming(blocks)
    tokens, n = sum(piece.shape[0] for piece in pieces), len(positions)
    block, by_rows = weight.block, weight.by_rows
    keys = [(reverse(p, weight.bits), 1) for p in positions] + [(p, 0) for p in positions]

    def kernel(me_ref, *refs):
        piece_refs, refs = refs[: len(pieces)], refs[len(pieces) :]
        parts, refs = refs[: 2 * n], refs[2 * n :]
        sources, refs = refs[: len(coming.inputs)], refs[len(coming.inputs) :]
        keep, send, refs = refs[0], refs[1], refs[2:]
        left, copies = refs[len(blocks)], []
        if blocks:
            copies = coming.copies(sources, refs[: len(blocks)], refs[-1], me_ref[0])
        for copy in copies:
            copy.start()
        place(piece_refs, order, left)
        for i, part in enumerate(parts):
            out = dot(left[...], part[...], 1, 1 if by_rows else 0).astype(BF16)
            (send if i < n else keep)[i % n] = out
        for copy in copies:
            copy.wait()

    keep, send, *helds = call(
        kernel,
        [("smem", weight.me)]
        + in_vmem(pieces)
        + in_vmem([weight.held[key] for key in keys])
        + coming.inputs,
        [("vmem", ((n, tokens, block), BF16))] * 2 + coming.outs,
        0,
        0,
        after,
        [pltpu.VMEM((tokens, weight.width), BF16)] + coming.scratch,
    )
    coming.arrive(helds)
    return keep, send


def block_sum(weight, stacks, odds, cols, groups, after=()):
    width, by_rows, block = weight.width, weight.by_rows, weight.block
    chips = len(weight.held) // 2
    tokens = stacks[0].shape[0] // chips
    n, size = len(stacks), tokens // cols
    parts = [
        weight.held[(reverse(p, weight.bits) if odd else p, odd)]
        for odd in odds
        for p in range(chips)
    ]

    def kernel(*refs):
        stack_refs, part_refs, refs = refs[:n], refs[n : n + len(parts)], refs[n + len(parts) :]
        outs, total = refs[:-1], refs[-1]
        for i, part in enumerate(part_refs):
            p = i % chips
            value = stack_refs[i // chips][p * tokens : (p + 1) * tokens, :]
            term = dot(value, part[...], 1, 0 if by_rows else 1)
            total[...] = term if i == 0 else total[...] + term
        for group, out in zip(groups, outs):
            for i, q in enumerate(group):
                out[i * size : (i + 1) * size, :] = total[q * size : (q + 1) * size, :].astype(BF16)

    return call(
        kernel,
        in_vmem(stacks) + in_vmem(parts),
        [("vmem", ((len(group) * size, width), BF16)) for group in groups],
        2 * tokens * width * block * chips * n,
        2 * width * block * chips * n,
        after,
        [pltpu.VMEM((tokens, width), F32)],
    )


def weight_grad(weight, stacks, odds, shards, into=None):
    pieces, order = shards
    width, by_rows, block = weight.width, weight.by_rows, weight.block
    chips = len(weight.held) // 2
    tokens = stacks[0].shape[0] // chips
    halves = 2
    size = (block if by_rows else width) // halves
    keys = [
        (i, p, (reverse(p, weight.bits) if odd else p, odd))
        for p in range(chips)
        for i, odd in enumerate(odds)
    ]

    def kernel(me_ref, *refs):
        stack_refs, refs = refs[: len(stacks)], refs[len(stacks) :]
        piece_refs, refs = refs[: len(pieces)], refs[len(pieces) :]
        grad, other, turned, ready, sent = refs[-5:]
        place(piece_refs, order, other)
        if not by_rows:
            turned[...] = other[...].T
        me = me_ref[0]

        def writes(step):
            to = weight.part(grad, me, keys[step // halves][2])
            at = step % halves * size
            to = to.at[at : at + size, :]
            slot = step % WRITES
            return [
                pltpu.make_async_copy(
                    cut(ready.at[slot], i, WRITE_CUTS), cut(to, i, WRITE_CUTS), sent.at[slot, i]
                )
                for i in range(WRITE_CUTS)
            ]

        steps = len(keys) * halves
        for step in range(steps):
            if step >= WRITES:
                for write in writes(step - WRITES):
                    write.wait()
            i, p, key = keys[step // halves]
            stack, of = stack_refs[i], slice(p * tokens, (p + 1) * tokens)
            at = slice(step % halves * size, (step % halves + 1) * size)
            if by_rows:
                out = dot(stack[of, at], other[...], 0, 0)
            else:
                out = dot(turned[at, :], stack[of, :], 1, 0)
            ready[step % WRITES] = out.astype(BF16)
            for write in writes(step):
                write.start()
        for step in range(max(0, steps - WRITES), steps):
            for write in writes(step):
                write.wait()

    return call(
        kernel,
        [("smem", weight.me)]
        + in_vmem(stacks)
        + in_vmem(pieces)
        + ([("hbm", into)] if into is not None else []),
        [("hbm", (weight.value.shape, BF16))],
        2 * tokens * width * block * len(keys) if 1 in odds else 0,
        2 * width * block * len(keys) if 1 in odds else 0,
        (),
        [
            pltpu.VMEM((tokens, width), BF16),
            pltpu.VMEM((width, tokens), BF16),
            pltpu.VMEM((WRITES, size, width if by_rows else block), BF16),
            pltpu.SemaphoreType.DMA((WRITES, WRITE_CUTS)),
        ],
        into is not None,
    )[0]


def summed_half(keep, got, count, after=()):
    size = keep.shape[0] // count

    def kernel(keep_ref, got_ref, *outs):
        for i, out in enumerate(outs):
            at = slice(i * size, (i + 1) * size)
            total = keep_ref[at, :].astype(F32) + got_ref[at, :].astype(F32)
            out[...] = total.astype(out.dtype)

    shape = (size, keep.shape[1])
    outs = [("vmem", (shape, F32))] + [("vmem", (shape, BF16))] * (count - 1)
    return call(kernel, in_vmem([keep, got]), outs, 0, 0, after)


def added(terms, space="vmem"):
    def kernel(*refs):
        refs[-1][...] = sum(ref[...].astype(F32) for ref in refs[: len(terms)]).astype(BF16)

    return call(kernel, in_vmem(terms), [(space, (terms[0].shape, BF16))], 0, 0)[0]


def block_of(terms):
    def total(refs):
        return sum(ref[block].astype(F32) for ref, (array, block) in zip(refs, terms))

    return total


def one_block(terms, dtype=BF16, flops=0):
    def kernel(*refs):
        refs[-1][0] = block_of(terms)(refs).astype(dtype)

    shape = (1, *terms[0][0].shape[1:])
    arrays = in_vmem([array for array, block in terms])
    return call(kernel, arrays, [("vmem", (shape, dtype))], flops, 0)[0]


def activate(terms):
    def kernel(*refs):
        total = block_of(terms)(refs)
        refs[-2][...] = total
        refs[-1][...] = gelu_fn(total).astype(BF16)

    shape = terms[0][0].shape[1:]
    outs = [("vmem", (shape, F32)), ("vmem", (shape, BF16))]
    return call(kernel, in_vmem([array for array, block in terms]), outs, PART_COST, 0)


def activate_back(hidden, terms):
    def kernel(hidden_ref, *refs):
        refs[-1][...] = gelu_back(hidden_ref[...], block_of(terms)(refs))

    arrays = [hidden] + [array for array, block in terms]
    return call(kernel, in_vmem(arrays), [("vmem", (hidden.shape, BF16))], 0, 0)[0]


def exchange_col(parts, cols):
    return [parts[0]] + [swap(parts[q], "col", q, cols) for q in range(cols - 1, 0, -1)]


def summed(parts):
    return sum(part.astype(F32) for part in parts).astype(BF16)


def blocked(rows, cols, tokens, cotangent, w_in, w_out):
    LAST.clear()
    me = lax.axis_index("row").astype(jnp.int32).reshape(1)
    w_in, w_out = Weight(me, w_in, rows, False), Weight(me, w_out, rows, True)
    first, second, own = [1, 3], [2], [0]

    def keys(positions):
        return [(reverse(p, 2), 1) for p in positions] + [(p, 0) for p in positions]

    def other_core(value):
        return swap(value, "row", 1, rows)

    def doubled(stack, step, flops=0):
        return joined([stack, across(stack, step, rows)], (), flops)

    wanted = [(w, key) for w in (w_in, w_out) for part in (first, second, own) for key in keys(part)]

    flips = [1 << bit for bit in range(cols.bit_length() - 1)][::-1]
    token_pieces, cot_pieces, order = [tokens], [cotangent], [0]
    for hop, flip in enumerate(flips):
        sent = joined(token_pieces) if hop else tokens
        token_pieces.append(swap(sent, "col", flip, cols))
        if hop:
            sent = joined(cot_pieces, (token_pieces[hop],))
            cot_pieces.append(swap(sent, "col", flips[hop - 1], cols))
        if hop < 2:
            load(wanted[5 * hop : 5 * hop + 5])
        order += [q ^ flip for q in order]
    sent = joined(cot_pieces, (token_pieces[-1],))
    cot_pieces.append(swap(sent, "col", flips[-1], cols))
    token_shards, cot_shards = (token_pieces, order), (cot_pieces, order)

    keep, sent = project(w_in, token_shards, first, [])
    got = other_core(sent)
    here, sent = project(w_in, token_shards, second + own, [])
    got_here, came = other_core(sent), across(added([keep, got]), 0, rows)
    load(wanted[5 * min(2, len(flips)) : 12])
    keep, sent = project(w_out, cot_shards, first, wanted[12:14])
    got = other_core(sent)
    sent = one_block([(here, 0), (got_here, 0), (came, 1)])
    terms = [(here, 1), (got_here, 1), (came, 0), (across(sent, 1, rows), 0)]

    came = across(added([keep, got]), 0, rows)
    keep, sent = project(w_out, cot_shards, second, wanted[14:])
    got = other_core(sent)
    hidden, act = activate(terms)
    sent = one_block([(keep, 0), (got, 0), (came, 1)])
    last = across(sent, 1, rows)
    keep, sent = project(w_out, cot_shards, own, [])
    got = other_core(sent)
    stack = doubled(act, 0)
    part = one_block([(came, 0), (last, 0)], F32, PART_COST)
    grad_hidden = activate_back(hidden, [(keep, 0), (part, 0), (got, 0)])
    stack = doubled(stack, 1)
    act = stack, other_core(stack)
    grad_w_out = weight_grad(w_out, act[:1], (0,), cot_shards)
    back_stack = doubled(grad_hidden, 0, PART_COST)

    even, odd = range(0, cols, 2), range(1, cols, 2)
    keep, send = block_sum(w_out, act, (0, 1), cols, (even, odd))
    got = swap(send, "col", 1, cols)
    grad_w_out = weight_grad(w_out, act[1:], (1,), cot_shards, grad_w_out)
    layer_out, *sums = summed_half(keep, got, len(even))
    layer_parts = [swap(part, "col", q, cols) for part, q in zip(sums, even[1:])]
    back_stack = doubled(back_stack, 1)
    grad_hidden = back_stack, other_core(back_stack)

    token_parts = block_sum(w_in, grad_hidden, (0, 1), cols, [[q] for q in range(cols)])
    layer_out = added([layer_out, *layer_parts], "window")
    grad_w_in = weight_grad(w_in, grad_hidden, (0, 1), token_shards)
    token_parts = exchange_col(token_parts, cols)
    return (layer_out, summed(token_parts), grad_w_in, grad_w_out)


def collective(tokens, cotangent, w_in, w_out):
    token_full = lax.all_gather(tokens, "col", axis=0, tiled=True)
    cot_full = lax.all_gather(cotangent, "col", axis=0, tiled=True)

    def over(value, axis):
        return lax.psum_scatter(value.astype(BF16), axis, scatter_dimension=0, tiled=True)

    hidden = over(dot(token_full, w_in, 1, 0), "row").astype(F32)
    grad_act = over(dot(cot_full, w_out, 1, 1), "row").astype(F32)
    act = lax.all_gather(gelu_fn(hidden).astype(BF16), "row", axis=0, tiled=True)
    grad_hidden = lax.all_gather(gelu_back(hidden, grad_act), "row", axis=0, tiled=True)
    layer_out = over(dot(act, w_out, 1, 0), "col")
    grad_tokens = over(dot(grad_hidden, w_in, 1, 1), "col")
    grad_w_in = dot(token_full, grad_hidden, 0, 0).astype(BF16)
    grad_w_out = dot(act, cot_full, 0, 0).astype(BF16)
    return (layer_out, grad_tokens, grad_w_in, grad_w_out)


def solution(mesh):
    rows, cols = mesh.shape["row"], mesh.shape["col"]

    def shards(tokens, cotangent, w_in, w_out):
        powers = rows & (rows - 1) == 0 and cols & (cols - 1) == 0
        if powers and rows == 8 and cols > 1 and w_in.shape[1] % (rows * 128) == 0:
            return blocked(rows, cols, tokens, cotangent, w_in, w_out)
        return collective(tokens, cotangent, w_in, w_out)

    return jax.shard_map(
        shards,
        mesh=mesh,
        in_specs=(P("col", "row"), P("col", "row"), P("row", "col"), P("col", "row")),
        out_specs=(P("col", "row"), P("col", "row"), P("row", "col"), P("col", "row")),
        check_vma=False,
    )
```

```python
import functools

import jax
import jax.numpy as jnp
from jax import lax
from jax.experimental import pallas as pl
from jax.experimental.pallas import tpu as pltpu
from jax.sharding import PartitionSpec as P

BF16 = jnp.bfloat16
F32 = jnp.float32
VMEM_LIMIT = 10 * 1024 * 1024
WRITES = 6
READ_CUTS, WRITE_CUTS = 4, 3
PART_COST = 6 * 10**9


def gelu_fn(value):
    return jax.nn.gelu(value, approximate=True)


def gelu_back(hidden, grad_act):
    unused, pullback = jax.vjp(gelu_fn, hidden)
    return pullback(grad_act)[0].astype(BF16)


def swap(value, axis, flip, count):
    return lax.ppermute(value, axis, [(i, i ^ flip) for i in range(count)])


def reverse(p, bits):
    return sum(((p >> j) & 1) << (bits - 1 - j) for j in range(bits))


def across(value, step, rows):
    bits = rows.bit_length() - 2
    flips = [2 << (bits - 1 - step if i & 1 else step) for i in range(rows)]
    return lax.ppermute(value, "row", [(i, i ^ flips[i]) for i in range(rows)])


def dot(left, right, left_dim, right_dim):
    return lax.dot_general(
        left, right, (((left_dim,), (right_dim,)), ((), ())), preferred_element_type=F32
    )


LAST = []


def call(kernel, arrays, outs, flops, moved, after=(), scratch=(), in_place=False):
    unread, count = [*LAST, *after], len(arrays)

    def body(*refs):
        kernel(*refs[:count], *refs[count + len(unread) :])

    specs = {
        "smem": pl.BlockSpec(memory_space=pltpu.SMEM),
        "vmem": pl.BlockSpec(memory_space=pltpu.VMEM),
        "hbm": pl.BlockSpec(memory_space=pl.ANY),
        "window": pl.BlockSpec(),
    }
    operands = []
    for space, value in arrays:
        if space != "smem":
            value = pltpu.with_memory_space_constraint(
                value, pltpu.HBM if space == "hbm" else pltpu.VMEM
            )
        operands.append(value)
    results = pl.pallas_call(
        body,
        in_specs=[specs[space] for space, value in arrays]
        + [pl.BlockSpec(memory_space=pl.ANY)] * len(unread),
        out_specs=[specs[space] for space, value in outs],
        scratch_shapes=list(scratch),
        input_output_aliases={count - 1: 0} if in_place else {},
        out_shape=[
            pltpu.VMEM(shape, dtype) if space == "vmem" else jax.ShapeDtypeStruct(shape, dtype)
            for space, (shape, dtype) in outs
        ],
        compiler_params=pltpu.CompilerParams(vmem_limit_bytes=VMEM_LIMIT),
        cost_estimate=pl.CostEstimate(flops=flops, bytes_accessed=moved, transcendentals=0),
    )(*operands, *unread)
    last = results[-1]
    if outs[-1][0] != "vmem":
        last = pltpu.with_memory_space_constraint(last, pltpu.HBM)
    LAST[:] = [last]
    return results


def in_vmem(values):
    return [("vmem", value) for value in values]


def join(pieces, out):
    at = 0
    for piece in pieces:
        out[at : at + piece.shape[0], :] = piece[...]
        at += piece.shape[0]


def place(pieces, order, out):
    size, order = pieces[0].shape[0], list(order)
    for piece in pieces:
        for at in range(0, piece.shape[0], size):
            to = order.pop(0) * size
            out[to : to + size, :] = piece[at : at + size, :]


def joined(pieces, after=(), flops=0):
    rows = sum(piece.shape[0] for piece in pieces)

    def kernel(*refs):
        join(refs[: len(pieces)], refs[-1])

    return call(
        kernel, in_vmem(pieces), [("vmem", ((rows, pieces[0].shape[1]), BF16))], flops, 0, after
    )[0]


class Weight:
    def __init__(self, me, value, rows, by_rows):
        self.me, self.value, self.by_rows = me, value, by_rows
        self.bits = rows.bit_length() - 2
        self.block = value.shape[0 if by_rows else 1] // rows
        self.width = value.shape[1 if by_rows else 0]
        self.shape = (self.block, self.width) if by_rows else (self.width, self.block)
        self.held = {}

    def part(self, ref, me, key):
        p, odd = key
        chip = p + (me & 1) * (reverse(p, self.bits) - p)
        at = (me ^ (2 * chip + odd)) * self.block
        at = pl.ds(pl.multiple_of(at, 128), self.block)
        return ref.at[at, :] if self.by_rows else ref.at[:, at]


def cut(ref, i, cuts):
    size = ref.shape[0] // cuts
    return ref.at[i * size : (i + 1) * size, :]


class Coming:
    def __init__(self, blocks):
        self.blocks = blocks
        self.weights = list(dict.fromkeys(weight for weight, key in blocks))
        self.count = len(blocks) * READ_CUTS
        self.inputs = [("hbm", weight.value) for weight in self.weights]
        self.outs = [("vmem", (weight.shape, BF16)) for weight, key in blocks]
        self.scratch = [pltpu.SemaphoreType.DMA((self.count,))] if blocks else []

    def copies(self, sources, helds, arrived, me):
        return [
            pltpu.make_async_copy(
                cut(weight.part(sources[self.weights.index(weight)], me, key), i, READ_CUTS),
                cut(held, i, READ_CUTS),
                arrived.at[n * READ_CUTS + i],
            )
            for n, ((weight, key), held) in enumerate(zip(self.blocks, helds))
            for i in range(READ_CUTS)
        ]

    def arrive(self, helds):
        for (weight, key), held in zip(self.blocks, helds):
            weight.held[key] = held


def load(blocks, after=()):
    coming = Coming(blocks)
    n = len(coming.inputs)

    def kernel(me_ref, *refs):
        copies = coming.copies(refs[:n], refs[n:-1], refs[-1], me_ref[0])
        for copy in copies:
            copy.start()
        for copy in copies:
            copy.wait()

    me = blocks[0][0].me
    coming.arrive(
        call(kernel, [("smem", me), *coming.inputs], coming.outs, 0, 0, after, coming.scratch)
    )


def project(weight, shards, positions, blocks, after=()):
    pieces, order = shards
    coming = Coming(blocks)
    tokens, n = sum(piece.shape[0] for piece in pieces), len(positions)
    block, by_rows = weight.block, weight.by_rows
    keys = [(reverse(p, weight.bits), 1) for p in positions] + [(p, 0) for p in positions]

    def kernel(me_ref, *refs):
        piece_refs, refs = refs[: len(pieces)], refs[len(pieces) :]
        parts, refs = refs[: 2 * n], refs[2 * n :]
        sources, refs = refs[: len(coming.inputs)], refs[len(coming.inputs) :]
        keep, send, refs = refs[0], refs[1], refs[2:]
        left, copies = refs[len(blocks)], []
        if blocks:
            copies = coming.copies(sources, refs[: len(blocks)], refs[-1], me_ref[0])
        for copy in copies:
            copy.start()

        @pl.when(me_ref[0] >= 0)
        def _():
            place(piece_refs, order, left)
            for i, part in enumerate(parts):
                out = dot(left[...], part[...], 1, 1 if by_rows else 0).astype(BF16)
                (send if i < n else keep)[i % n] = out

        for copy in copies:
            copy.wait()

    keep, send, *helds = call(
        kernel,
        [("smem", weight.me)]
        + in_vmem(pieces)
        + in_vmem([weight.held[key] for key in keys])
        + coming.inputs,
        [("vmem", ((n, tokens, block), BF16))] * 2 + coming.outs,
        0,
        0,
        after,
        [pltpu.VMEM((tokens, weight.width), BF16)] + coming.scratch,
    )
    coming.arrive(helds)
    return keep, send


def block_sum(weight, stacks, odds, cols, groups, after=()):
    width, by_rows, block = weight.width, weight.by_rows, weight.block
    chips = len(weight.held) // 2
    tokens = stacks[0].shape[0] // chips
    n, size = len(stacks), tokens // cols
    parts = [
        weight.held[(reverse(p, weight.bits) if odd else p, odd)]
        for odd in odds
        for p in range(chips)
    ]

    def kernel(*refs):
        stack_refs, part_refs, refs = refs[:n], refs[n : n + len(parts)], refs[n + len(parts) :]
        outs, total = refs[:-1], refs[-1]
        for i, part in enumerate(part_refs):
            p = i % chips
            value = stack_refs[i // chips][p * tokens : (p + 1) * tokens, :]
            term = dot(value, part[...], 1, 0 if by_rows else 1)
            total[...] = term if i == 0 else total[...] + term
        for group, out in zip(groups, outs):
            for i, q in enumerate(group):
                out[i * size : (i + 1) * size, :] = total[q * size : (q + 1) * size, :].astype(BF16)

    return call(
        kernel,
        in_vmem(stacks) + in_vmem(parts),
        [("vmem", ((len(group) * size, width), BF16)) for group in groups],
        2 * tokens * width * block * chips * n,
        2 * width * block * chips * n,
        after,
        [pltpu.VMEM((tokens, width), F32)],
    )


def weight_grad(weight, stacks, odds, shards, into=None):
    pieces, order = shards
    width, by_rows, block = weight.width, weight.by_rows, weight.block
    chips = len(weight.held) // 2
    tokens = stacks[0].shape[0] // chips
    halves = 2
    size = (block if by_rows else width) // halves
    keys = [
        (i, p, (reverse(p, weight.bits) if odd else p, odd))
        for p in range(chips)
        for i, odd in enumerate(odds)
    ]

    def kernel(me_ref, *refs):
        stack_refs, refs = refs[: len(stacks)], refs[len(stacks) :]
        piece_refs, refs = refs[: len(pieces)], refs[len(pieces) :]
        grad, other, turned, ready, sent = refs[-5:]
        place(piece_refs, order, other)
        if not by_rows:
            turned[...] = other[...].T
        me = me_ref[0]

        def writes(step):
            to = weight.part(grad, me, keys[step // halves][2])
            at = step % halves * size
            to = to.at[at : at + size, :]
            slot = step % WRITES
            return [
                pltpu.make_async_copy(
                    cut(ready.at[slot], i, WRITE_CUTS), cut(to, i, WRITE_CUTS), sent.at[slot, i]
                )
                for i in range(WRITE_CUTS)
            ]

        steps = len(keys) * halves
        for step in range(steps):
            if step >= WRITES:
                for write in writes(step - WRITES):
                    write.wait()

            @pl.when(me >= 0)
            def _():
                i, p, key = keys[step // halves]
                stack, of = stack_refs[i], slice(p * tokens, (p + 1) * tokens)
                at = slice(step % halves * size, (step % halves + 1) * size)
                if by_rows:
                    out = dot(stack[of, at], other[...], 0, 0)
                else:
                    out = dot(turned[at, :], stack[of, :], 1, 0)
                ready[step % WRITES] = out.astype(BF16)

            for write in writes(step):
                write.start()
        for step in range(max(0, steps - WRITES), steps):
            for write in writes(step):
                write.wait()

    return call(
        kernel,
        [("smem", weight.me)]
        + in_vmem(stacks)
        + in_vmem(pieces)
        + ([("hbm", into)] if into is not None else []),
        [("hbm", (weight.value.shape, BF16))],
        2 * tokens * width * block * len(keys) if 1 in odds else 0,
        2 * width * block * len(keys) if 1 in odds else 0,
        (),
        [
            pltpu.VMEM((tokens, width), BF16),
            pltpu.VMEM((width, tokens), BF16),
            pltpu.VMEM((WRITES, size, width if by_rows else block), BF16),
            pltpu.SemaphoreType.DMA((WRITES, WRITE_CUTS)),
        ],
        into is not None,
    )[0]


def summed_half(keep, got, count, after=()):
    size = keep.shape[0] // count

    def kernel(keep_ref, got_ref, *outs):
        for i, out in enumerate(outs):
            at = slice(i * size, (i + 1) * size)
            total = keep_ref[at, :].astype(F32) + got_ref[at, :].astype(F32)
            out[...] = total.astype(out.dtype)

    shape = (size, keep.shape[1])
    outs = [("vmem", (shape, F32))] + [("vmem", (shape, BF16))] * (count - 1)
    return call(kernel, in_vmem([keep, got]), outs, 0, 0, after)


def added(terms, space="vmem"):
    def kernel(*refs):
        refs[-1][...] = sum(ref[...].astype(F32) for ref in refs[: len(terms)]).astype(BF16)

    return call(kernel, in_vmem(terms), [(space, (terms[0].shape, BF16))], 0, 0)[0]


def block_of(terms):
    def total(refs):
        return sum(ref[block].astype(F32) for ref, (array, block) in zip(refs, terms))

    return total


def one_block(terms, dtype=BF16, flops=0):
    def kernel(*refs):
        refs[-1][0] = block_of(terms)(refs).astype(dtype)

    shape = (1, *terms[0][0].shape[1:])
    arrays = in_vmem([array for array, block in terms])
    return call(kernel, arrays, [("vmem", (shape, dtype))], flops, 0)[0]


def activate(terms):
    def kernel(*refs):
        total = block_of(terms)(refs)
        refs[-2][...] = total
        refs[-1][...] = gelu_fn(total).astype(BF16)

    shape = terms[0][0].shape[1:]
    outs = [("vmem", (shape, F32)), ("vmem", (shape, BF16))]
    return call(kernel, in_vmem([array for array, block in terms]), outs, PART_COST, 0)


def activate_back(hidden, terms):
    def kernel(hidden_ref, *refs):
        refs[-1][...] = gelu_back(hidden_ref[...], block_of(terms)(refs))

    arrays = [hidden] + [array for array, block in terms]
    return call(kernel, in_vmem(arrays), [("vmem", (hidden.shape, BF16))], 0, 0)[0]


def exchange_col(parts, cols):
    return [parts[0]] + [swap(parts[q], "col", q, cols) for q in range(cols - 1, 0, -1)]


def summed(parts):
    return sum(part.astype(F32) for part in parts).astype(BF16)


def blocked(rows, cols, tokens, cotangent, w_in, w_out):
    LAST.clear()
    me = lax.axis_index("row").astype(jnp.int32).reshape(1)
    w_in, w_out = Weight(me, w_in, rows, False), Weight(me, w_out, rows, True)
    first, second, own = [1, 3], [2], [0]

    def keys(positions):
        return [(reverse(p, 2), 1) for p in positions] + [(p, 0) for p in positions]

    def other_core(value):
        return swap(value, "row", 1, rows)

    def doubled(stack, step, flops=0):
        return joined([stack, across(stack, step, rows)], (), flops)

    wanted = [(w, key) for w in (w_in, w_out) for part in (first, second, own) for key in keys(part)]

    flips = [1 << bit for bit in range(cols.bit_length() - 1)][::-1]
    token_pieces, cot_pieces, order = [tokens], [cotangent], [0]
    for hop, flip in enumerate(flips):
        sent = joined(token_pieces) if hop else tokens
        token_pieces.append(swap(sent, "col", flip, cols))
        if hop:
            sent = joined(cot_pieces, (token_pieces[hop],))
            cot_pieces.append(swap(sent, "col", flips[hop - 1], cols))
        if hop < 2:
            load(wanted[5 * hop : 5 + 3 * hop])
        order += [q ^ flip for q in order]
    sent = joined(cot_pieces, (token_pieces[-1],))
    cot_pieces.append(swap(sent, "col", flips[-1], cols))
    token_shards, cot_shards = (token_pieces, order), (cot_pieces, order)

    keep, sent = project(w_in, token_shards, first, wanted[8:10])
    got = other_core(sent)
    here, sent = project(w_in, token_shards, second + own, [])
    got_here, came = other_core(sent), across(added([keep, got]), 0, rows)
    load(wanted[10:12])
    keep, sent = project(w_out, cot_shards, first, wanted[12:14])
    got = other_core(sent)
    sent = one_block([(here, 0), (got_here, 0), (came, 1)])
    terms = [(here, 1), (got_here, 1), (came, 0), (across(sent, 1, rows), 0)]

    came = across(added([keep, got]), 0, rows)
    keep, sent = project(w_out, cot_shards, second, wanted[14:])
    got = other_core(sent)
    hidden, act = activate(terms)
    sent = one_block([(keep, 0), (got, 0), (came, 1)])
    last = across(sent, 1, rows)
    keep, sent = project(w_out, cot_shards, own, [])
    got = other_core(sent)
    stack = doubled(act, 0)
    part = one_block([(came, 0), (last, 0)], F32, PART_COST)
    grad_hidden = activate_back(hidden, [(keep, 0), (part, 0), (got, 0)])
    stack = doubled(stack, 1)
    act = stack, other_core(stack)
    grad_w_out = weight_grad(w_out, act[:1], (0,), cot_shards)
    back_stack = doubled(grad_hidden, 0, PART_COST)

    even, odd = range(0, cols, 2), range(1, cols, 2)
    keep, send = block_sum(w_out, act, (0, 1), cols, (even, odd))
    got = swap(send, "col", 1, cols)
    grad_w_out = weight_grad(w_out, act[1:], (1,), cot_shards, grad_w_out)
    layer_out, *sums = summed_half(keep, got, len(even))
    layer_parts = [swap(part, "col", q, cols) for part, q in zip(sums, even[1:])]
    back_stack = doubled(back_stack, 1)
    grad_hidden = back_stack, other_core(back_stack)

    token_parts = block_sum(w_in, grad_hidden, (0, 1), cols, [[q] for q in range(cols)])
    layer_out = added([layer_out, *layer_parts], "window")
    grad_w_in = weight_grad(w_in, grad_hidden, (0, 1), token_shards)
    token_parts = exchange_col(token_parts, cols)
    return (layer_out, summed(token_parts), grad_w_in, grad_w_out)


def collective(tokens, cotangent, w_in, w_out):
    token_full = lax.all_gather(tokens, "col", axis=0, tiled=True)
    cot_full = lax.all_gather(cotangent, "col", axis=0, tiled=True)

    def over(value, axis):
        return lax.psum_scatter(value.astype(BF16), axis, scatter_dimension=0, tiled=True)

    hidden = over(dot(token_full, w_in, 1, 0), "row").astype(F32)
    grad_act = over(dot(cot_full, w_out, 1, 1), "row").astype(F32)
    act = lax.all_gather(gelu_fn(hidden).astype(BF16), "row", axis=0, tiled=True)
    grad_hidden = lax.all_gather(gelu_back(hidden, grad_act), "row", axis=0, tiled=True)
    layer_out = over(dot(act, w_out, 1, 0), "col")
    grad_tokens = over(dot(grad_hidden, w_in, 1, 1), "col")
    grad_w_in = dot(token_full, grad_hidden, 0, 0).astype(BF16)
    grad_w_out = dot(act, cot_full, 0, 0).astype(BF16)
    return (layer_out, grad_tokens, grad_w_in, grad_w_out)


def solution(mesh):
    rows, cols = mesh.shape["row"], mesh.shape["col"]

    def shards(tokens, cotangent, w_in, w_out):
        powers = rows & (rows - 1) == 0 and cols & (cols - 1) == 0
        if powers and rows == 8 and cols > 2 and w_in.shape[1] % (rows * 128) == 0:
            return blocked(rows, cols, tokens, cotangent, w_in, w_out)
        return collective(tokens, cotangent, w_in, w_out)

    return jax.shard_map(
        shards,
        mesh=mesh,
        in_specs=(P("col", "row"), P("col", "row"), P("row", "col"), P("col", "row")),
        out_specs=(P("col", "row"), P("col", "row"), P("row", "col"), P("col", "row")),
        check_vma=False,
    )
```

```python
import functools

import jax
import jax.numpy as jnp
from jax import lax
from jax.experimental import pallas as pl
from jax.experimental.pallas import tpu as pltpu
from jax.sharding import PartitionSpec as P

BF16 = jnp.bfloat16
F32 = jnp.float32
VMEM_LIMIT = 10 * 1024 * 1024
WRITES = 6
READ_CUTS, WRITE_CUTS = 4, 3
PART_COST = 6 * 10**9


def gelu_fn(value):
    return jax.nn.gelu(value, approximate=True)


def gelu_back(hidden, grad_act):
    unused, pullback = jax.vjp(gelu_fn, hidden)
    return pullback(grad_act)[0].astype(BF16)


def swap(value, axis, flip, count):
    return lax.ppermute(value, axis, [(i, i ^ flip) for i in range(count)])


def reverse(p, bits):
    return sum(((p >> j) & 1) << (bits - 1 - j) for j in range(bits))


def across(value, step, rows):
    bits = rows.bit_length() - 2
    flips = [2 << (bits - 1 - step if i & 1 else step) for i in range(rows)]
    return lax.ppermute(value, "row", [(i, i ^ flips[i]) for i in range(rows)])


def dot(left, right, left_dim, right_dim):
    return lax.dot_general(
        left, right, (((left_dim,), (right_dim,)), ((), ())), preferred_element_type=F32
    )


LAST = []


def call(kernel, arrays, outs, flops, moved, after=(), scratch=()):
    unread, count = [*LAST, *after], len(arrays)

    def body(*refs):
        kernel(*refs[:count], *refs[count + len(unread) :])

    specs = {
        "smem": pl.BlockSpec(memory_space=pltpu.SMEM),
        "vmem": pl.BlockSpec(memory_space=pltpu.VMEM),
        "hbm": pl.BlockSpec(memory_space=pl.ANY),
        "window": pl.BlockSpec(),
    }
    operands = []
    for space, value in arrays:
        if space != "smem":
            value = pltpu.with_memory_space_constraint(
                value, pltpu.HBM if space == "hbm" else pltpu.VMEM
            )
        operands.append(value)
    results = pl.pallas_call(
        body,
        in_specs=[specs[space] for space, value in arrays]
        + [pl.BlockSpec(memory_space=pl.ANY)] * len(unread),
        out_specs=[specs[space] for space, value in outs],
        scratch_shapes=list(scratch),
        out_shape=[
            pltpu.VMEM(shape, dtype) if space == "vmem" else jax.ShapeDtypeStruct(shape, dtype)
            for space, (shape, dtype) in outs
        ],
        compiler_params=pltpu.CompilerParams(vmem_limit_bytes=VMEM_LIMIT),
        cost_estimate=pl.CostEstimate(flops=flops, bytes_accessed=moved, transcendentals=0),
    )(*operands, *unread)
    last = results[-1]
    if outs[-1][0] != "vmem":
        last = pltpu.with_memory_space_constraint(last, pltpu.HBM)
    LAST[:] = [last]
    return results


def in_vmem(values):
    return [("vmem", value) for value in values]


def join(pieces, out):
    at = 0
    for piece in pieces:
        out[at : at + piece.shape[0], :] = piece[...]
        at += piece.shape[0]


def place(pieces, order, out):
    size, order = pieces[0].shape[0], list(order)
    for piece in pieces:
        for at in range(0, piece.shape[0], size):
            to = order.pop(0) * size
            out[to : to + size, :] = piece[at : at + size, :]


def joined(pieces, after=(), flops=0):
    rows = sum(piece.shape[0] for piece in pieces)

    def kernel(*refs):
        join(refs[: len(pieces)], refs[-1])

    return call(
        kernel, in_vmem(pieces), [("vmem", ((rows, pieces[0].shape[1]), BF16))], flops, 0, after
    )[0]


class Weight:
    def __init__(self, me, value, rows, by_rows):
        self.me, self.value, self.by_rows = me, value, by_rows
        self.bits = rows.bit_length() - 2
        self.block = value.shape[0 if by_rows else 1] // rows
        self.width = value.shape[1 if by_rows else 0]
        self.shape = (self.block, self.width) if by_rows else (self.width, self.block)
        self.held = {}

    def part(self, ref, me, key):
        p, odd = key
        chip = p + (me & 1) * (reverse(p, self.bits) - p)
        at = (me ^ (2 * chip + odd)) * self.block
        at = pl.ds(pl.multiple_of(at, 128), self.block)
        return ref.at[at, :] if self.by_rows else ref.at[:, at]


def cut(ref, i, cuts):
    size = ref.shape[0] // cuts
    return ref.at[i * size : (i + 1) * size, :]


class Coming:
    def __init__(self, blocks):
        self.blocks = blocks
        self.weights = list(dict.fromkeys(weight for weight, key in blocks))
        self.count = len(blocks) * READ_CUTS
        self.inputs = [("hbm", weight.value) for weight in self.weights]
        self.outs = [("vmem", (weight.shape, BF16)) for weight, key in blocks]
        self.scratch = [pltpu.SemaphoreType.DMA((self.count,))] if blocks else []

    def copies(self, sources, helds, arrived, me):
        return [
            pltpu.make_async_copy(
                cut(weight.part(sources[self.weights.index(weight)], me, key), i, READ_CUTS),
                cut(held, i, READ_CUTS),
                arrived.at[n * READ_CUTS + i],
            )
            for n, ((weight, key), held) in enumerate(zip(self.blocks, helds))
            for i in range(READ_CUTS)
        ]

    def arrive(self, helds):
        for (weight, key), held in zip(self.blocks, helds):
            weight.held[key] = held


def load(blocks, after=()):
    coming = Coming(blocks)
    n = len(coming.inputs)

    def kernel(me_ref, *refs):
        copies = coming.copies(refs[:n], refs[n:-1], refs[-1], me_ref[0])
        for copy in copies:
            copy.start()
        for copy in copies:
            copy.wait()

    me = blocks[0][0].me
    coming.arrive(
        call(kernel, [("smem", me), *coming.inputs], coming.outs, 0, 0, after, coming.scratch)
    )


def project(weight, shards, positions, blocks, after=()):
    pieces, order = shards
    coming = Coming(blocks)
    tokens, n = sum(piece.shape[0] for piece in pieces), len(positions)
    block, by_rows = weight.block, weight.by_rows
    keys = [(reverse(p, weight.bits), 1) for p in positions] + [(p, 0) for p in positions]

    def kernel(me_ref, *refs):
        piece_refs, refs = refs[: len(pieces)], refs[len(pieces) :]
        parts, refs = refs[: 2 * n], refs[2 * n :]
        sources, refs = refs[: len(coming.inputs)], refs[len(coming.inputs) :]
        keep, send, refs = refs[0], refs[1], refs[2:]
        left, copies = refs[len(blocks)], []
        if blocks:
            copies = coming.copies(sources, refs[: len(blocks)], refs[-1], me_ref[0])
        for copy in copies:
            copy.start()

        @pl.when(me_ref[0] >= 0)
        def _():
            place(piece_refs, order, left)
            for i, part in enumerate(parts):
                out = dot(left[...], part[...], 1, 1 if by_rows else 0).astype(BF16)
                (send if i < n else keep)[i % n] = out

        for copy in copies:
            copy.wait()

    keep, send, *helds = call(
        kernel,
        [("smem", weight.me)]
        + in_vmem(pieces)
        + in_vmem([weight.held[key] for key in keys])
        + coming.inputs,
        [("vmem", ((n, tokens, block), BF16))] * 2 + coming.outs,
        0,
        0,
        after,
        [pltpu.VMEM((tokens, weight.width), BF16)] + coming.scratch,
    )
    coming.arrive(helds)
    return keep, send


def block_sum(weight, stacks, odds, cols, groups, after=()):
    width, by_rows, block = weight.width, weight.by_rows, weight.block
    chips = len(weight.held) // 2
    tokens = stacks[0].shape[0] // chips
    n, size = len(stacks), tokens // cols
    parts = [
        weight.held[(reverse(p, weight.bits) if odd else p, odd)]
        for odd in odds
        for p in range(chips)
    ]

    def kernel(*refs):
        stack_refs, part_refs, refs = refs[:n], refs[n : n + len(parts)], refs[n + len(parts) :]
        outs, total = refs[:-1], refs[-1]
        for i, part in enumerate(part_refs):
            p = i % chips
            value = stack_refs[i // chips][p * tokens : (p + 1) * tokens, :]
            term = dot(value, part[...], 1, 0 if by_rows else 1)
            total[...] = term if i == 0 else total[...] + term
        for group, out in zip(groups, outs):
            for i, q in enumerate(group):
                out[i * size : (i + 1) * size, :] = total[q * size : (q + 1) * size, :].astype(BF16)

    return call(
        kernel,
        in_vmem(stacks) + in_vmem(parts),
        [("vmem", ((len(group) * size, width), BF16)) for group in groups],
        2 * tokens * width * block * chips * n,
        2 * width * block * chips * n,
        after,
        [pltpu.VMEM((tokens, width), F32)],
    )


def block_keys(weight):
    chips = len(weight.held) // 2
    return [(reverse(p, weight.bits) if odd else p, odd) for odd in range(2) for p in range(chips)]


def weight_grad(weight, stacks, shards, cols=1, groups=()):
    pieces, order = shards
    width, by_rows, block = weight.width, weight.by_rows, weight.block
    chips = len(weight.held) // 2
    tokens = stacks[0].shape[0] // chips
    halves = 2
    size = (block if by_rows else width) // halves
    keys = block_keys(weight)
    order_of = [i for p in range(chips) for i in (p, chips + p)]
    parts = [weight.held[key] for key in keys] if groups else []

    def kernel(me_ref, *refs):
        stack_refs, refs = refs[:2], refs[2:]
        piece_refs, refs = refs[: len(pieces)], refs[len(pieces) :]
        part_refs, refs = refs[: len(parts)], refs[len(parts) :]
        sums, (grad, other, turned, ready, sent, total) = refs[: len(groups)], refs[len(groups) :]
        place(piece_refs, order, other)
        if not by_rows:
            turned[...] = other[...].T
        me = me_ref[0]

        def value(i):
            return stack_refs[i // chips], slice(i % chips * tokens, (i % chips + 1) * tokens)

        def writes(step):
            to = weight.part(grad, me, keys[order_of[step // halves]])
            at = step % halves * size
            to = to.at[at : at + size, :]
            slot = step % WRITES
            return [
                pltpu.make_async_copy(
                    cut(ready.at[slot], i, WRITE_CUTS), cut(to, i, WRITE_CUTS), sent.at[slot, i]
                )
                for i in range(WRITE_CUTS)
            ]

        def product(step):
            stack, of = value(order_of[step // halves])
            at = slice(step % halves * size, (step % halves + 1) * size)
            if by_rows:
                out = dot(stack[of, at], other[...], 0, 0)
            else:
                out = dot(turned[at, :], stack[of, :], 1, 0)
            ready[step % WRITES] = out.astype(BF16)

        steps = len(keys) * halves
        for step in range(steps):
            if step >= WRITES:
                for write in writes(step - WRITES):
                    write.wait()
            if by_rows:
                product(step)
            else:
                pl.when(me >= 0)(functools.partial(product, step))
            for write in writes(step):
                write.start()

        @pl.when(me >= 0)
        def _():
            for i, part in enumerate(part_refs):
                stack, of = value(i)
                term = dot(stack[of, :], part[...], 1, 0)
                total[...] = term if i == 0 else total[...] + term
            rows = tokens // cols
            for group, out in zip(groups, sums):
                for i, q in enumerate(group):
                    out[i * rows : (i + 1) * rows, :] = total[q * rows : (q + 1) * rows, :].astype(BF16)

        for step in range(max(0, steps - WRITES), steps):
            for write in writes(step):
                write.wait()

    return call(
        kernel,
        [("smem", weight.me)] + in_vmem(stacks) + in_vmem(pieces) + in_vmem(parts),
        [("vmem", ((len(group) * tokens // cols, width), BF16)) for group in groups]
        + [("hbm", (weight.value.shape, BF16))],
        2 * tokens * width * block * len(keys),
        2 * width * block * len(keys),
        (),
        [
            pltpu.VMEM((tokens, width), BF16),
            pltpu.VMEM((width, tokens), BF16),
            pltpu.VMEM((WRITES, size, width if by_rows else block), BF16),
            pltpu.SemaphoreType.DMA((WRITES, WRITE_CUTS)),
            pltpu.VMEM((tokens, width), F32),
        ],
    )


def summed_half(keep, got, count, after=()):
    size = keep.shape[0] // count

    def kernel(keep_ref, got_ref, *outs):
        for i, out in enumerate(outs):
            at = slice(i * size, (i + 1) * size)
            total = keep_ref[at, :].astype(F32) + got_ref[at, :].astype(F32)
            out[...] = total.astype(out.dtype)

    shape = (size, keep.shape[1])
    outs = [("vmem", (shape, F32))] + [("vmem", (shape, BF16))] * (count - 1)
    return call(kernel, in_vmem([keep, got]), outs, 0, 0, after)


def added(*sums, space="vmem"):
    def kernel(*refs):
        refs, outs = refs[: -len(sums)], refs[-len(sums) :]
        for terms, out in zip(sums, outs):
            out[...] = sum(ref[...].astype(F32) for ref in refs[: len(terms)]).astype(BF16)
            refs = refs[len(terms) :]

    arrays = in_vmem([term for terms in sums for term in terms])
    return call(kernel, arrays, [(space, (terms[0].shape, BF16)) for terms in sums], 0, 0)


def block_of(terms):
    def total(refs):
        return sum(ref[block].astype(F32) for ref, (array, block) in zip(refs, terms))

    return total


def one_block(terms, dtype=BF16, flops=0):
    def kernel(*refs):
        refs[-1][0] = block_of(terms)(refs).astype(dtype)

    shape = (1, *terms[0][0].shape[1:])
    arrays = in_vmem([array for array, block in terms])
    return call(kernel, arrays, [("vmem", (shape, dtype))], flops, 0)[0]


def activate(terms):
    def kernel(*refs):
        total = block_of(terms)(refs)
        refs[-2][...] = total
        refs[-1][...] = gelu_fn(total).astype(BF16)

    shape = terms[0][0].shape[1:]
    outs = [("vmem", (shape, F32)), ("vmem", (shape, BF16))]
    return call(kernel, in_vmem([array for array, block in terms]), outs, PART_COST, 0)


def activate_back(hidden, terms):
    def kernel(hidden_ref, *refs):
        refs[-1][...] = gelu_back(hidden_ref[...], block_of(terms)(refs))

    arrays = [hidden] + [array for array, block in terms]
    return call(kernel, in_vmem(arrays), [("vmem", (hidden.shape, BF16))], 0, 0)[0]


def exchange_col(parts, cols):
    return [parts[0]] + [swap(parts[q], "col", q, cols) for q in range(cols - 1, 0, -1)]


def blocked(rows, cols, tokens, cotangent, w_in, w_out):
    LAST.clear()
    me = lax.axis_index("row").astype(jnp.int32).reshape(1)
    w_in, w_out = Weight(me, w_in, rows, False), Weight(me, w_out, rows, True)
    first, second, own = [1, 3], [2], [0]

    def keys(positions):
        return [(reverse(p, 2), 1) for p in positions] + [(p, 0) for p in positions]

    def other_core(value):
        return swap(value, "row", 1, rows)

    def doubled(stack, step, flops=0):
        return joined([stack, across(stack, step, rows)], (), flops)

    wanted = [(w, key) for w in (w_in, w_out) for part in (first, second, own) for key in keys(part)]

    flips = [1 << bit for bit in range(cols.bit_length() - 1)][::-1]
    token_pieces, cot_pieces, order = [tokens], [cotangent], [0]
    for hop, flip in enumerate(flips):
        sent = joined(token_pieces) if hop else tokens
        token_pieces.append(swap(sent, "col", flip, cols))
        if hop:
            sent = joined(cot_pieces, (token_pieces[hop],))
            cot_pieces.append(swap(sent, "col", flips[hop - 1], cols))
        if hop < 2:
            load(wanted[5 * hop : 5 + 3 * hop])
        order += [q ^ flip for q in order]
    sent = joined(cot_pieces, (token_pieces[-1],))
    cot_pieces.append(swap(sent, "col", flips[-1], cols))
    token_shards, cot_shards = (token_pieces, order), (cot_pieces, order)

    keep, sent = project(w_in, token_shards, first, wanted[8:10])
    got = other_core(sent)
    here, sent = project(w_in, token_shards, second + own, [])
    got_here, came = other_core(sent), across(added([keep, got])[0], 0, rows)
    load(wanted[10:12])
    keep, sent = project(w_out, cot_shards, first, wanted[12:14])
    got = other_core(sent)
    sent = one_block([(here, 0), (got_here, 0), (came, 1)])
    terms = [(here, 1), (got_here, 1), (came, 0), (across(sent, 1, rows), 0)]

    came = across(added([keep, got])[0], 0, rows)
    keep, sent = project(w_out, cot_shards, second, wanted[14:])
    got = other_core(sent)
    hidden, act = activate(terms)
    sent = one_block([(keep, 0), (got, 0), (came, 1)])
    last = across(sent, 1, rows)
    keep, sent = project(w_out, cot_shards, own, [])
    got = other_core(sent)
    stack = doubled(act, 0)
    part = one_block([(came, 0), (last, 0)], F32, PART_COST)
    grad_hidden = activate_back(hidden, [(keep, 0), (part, 0), (got, 0)])
    stack = doubled(stack, 1)
    act = stack, other_core(stack)
    back_stack = doubled(grad_hidden, 0, PART_COST)

    even, odd = range(0, cols, 2), range(1, cols, 2)
    keep, sent, grad_w_out = weight_grad(w_out, act, cot_shards, cols, (even, odd))
    got = swap(sent, "col", 1, cols)
    back_stack = doubled(back_stack, 1)
    grad_hidden = back_stack, other_core(back_stack)
    token_parts = block_sum(w_in, grad_hidden, (0, 1), cols, [[q] for q in range(cols)])
    layer_out, *sums = summed_half(keep, got, len(even))
    layer_parts = [swap(part, "col", q, cols) for part, q in zip(sums, even[1:])]
    token_parts = exchange_col(token_parts, cols)
    (grad_w_in,) = weight_grad(w_in, grad_hidden, token_shards)
    layer_out, grad_tokens = added([layer_out, *layer_parts], token_parts, space="window")
    return (layer_out, grad_tokens, grad_w_in, grad_w_out)


def collective(tokens, cotangent, w_in, w_out):
    token_full = lax.all_gather(tokens, "col", axis=0, tiled=True)
    cot_full = lax.all_gather(cotangent, "col", axis=0, tiled=True)

    def over(value, axis):
        return lax.psum_scatter(value.astype(BF16), axis, scatter_dimension=0, tiled=True)

    hidden = over(dot(token_full, w_in, 1, 0), "row").astype(F32)
    grad_act = over(dot(cot_full, w_out, 1, 1), "row").astype(F32)
    act = lax.all_gather(gelu_fn(hidden).astype(BF16), "row", axis=0, tiled=True)
    grad_hidden = lax.all_gather(gelu_back(hidden, grad_act), "row", axis=0, tiled=True)
    layer_out = over(dot(act, w_out, 1, 0), "col")
    grad_tokens = over(dot(grad_hidden, w_in, 1, 1), "col")
    grad_w_in = dot(token_full, grad_hidden, 0, 0).astype(BF16)
    grad_w_out = dot(act, cot_full, 0, 0).astype(BF16)
    return (layer_out, grad_tokens, grad_w_in, grad_w_out)


def solution(mesh):
    rows, cols = mesh.shape["row"], mesh.shape["col"]

    def shards(tokens, cotangent, w_in, w_out):
        powers = rows & (rows - 1) == 0 and cols & (cols - 1) == 0
        if powers and rows == 8 and cols > 2 and w_in.shape[1] % (rows * 128) == 0:
            return blocked(rows, cols, tokens, cotangent, w_in, w_out)
        return collective(tokens, cotangent, w_in, w_out)

    return jax.shard_map(
        shards,
        mesh=mesh,
        in_specs=(P("col", "row"), P("col", "row"), P("row", "col"), P("col", "row")),
        out_specs=(P("col", "row"), P("col", "row"), P("row", "col"), P("col", "row")),
        check_vma=False,
    )
```

```python
import functools

import jax
import jax.numpy as jnp
from jax import lax
from jax.experimental import pallas as pl
from jax.experimental.pallas import tpu as pltpu
from jax.sharding import PartitionSpec as P

BF16 = jnp.bfloat16
F32 = jnp.float32
VMEM_LIMIT = 10 * 1024 * 1024
WRITES = 6
READ_CUTS, WRITE_CUTS = 4, 3
PART_COST = 6 * 10**9


def gelu_fn(value):
    return jax.nn.gelu(value, approximate=True)


def gelu_back(hidden, grad_act):
    unused, pullback = jax.vjp(gelu_fn, hidden)
    return pullback(grad_act)[0].astype(BF16)


def swap(value, axis, flip, count):
    return lax.ppermute(value, axis, [(i, i ^ flip) for i in range(count)])


def reverse(p, bits):
    return sum(((p >> j) & 1) << (bits - 1 - j) for j in range(bits))


def across(value, step, rows):
    bits = rows.bit_length() - 2
    flips = [2 << (bits - 1 - step if i & 1 else step) for i in range(rows)]
    return lax.ppermute(value, "row", [(i, i ^ flips[i]) for i in range(rows)])


def dot(left, right, left_dim, right_dim):
    return lax.dot_general(
        left, right, (((left_dim,), (right_dim,)), ((), ())), preferred_element_type=F32
    )


LAST = []


def call(kernel, arrays, outs, flops, moved, after=(), scratch=(), in_place=False):
    unread, count = [*LAST, *after], len(arrays)

    def body(*refs):
        kernel(*refs[:count], *refs[count + len(unread) :])

    specs = {
        "smem": pl.BlockSpec(memory_space=pltpu.SMEM),
        "vmem": pl.BlockSpec(memory_space=pltpu.VMEM),
        "hbm": pl.BlockSpec(memory_space=pl.ANY),
        "window": pl.BlockSpec(),
    }
    operands = []
    for space, value in arrays:
        if space != "smem":
            value = pltpu.with_memory_space_constraint(
                value, pltpu.HBM if space == "hbm" else pltpu.VMEM
            )
        operands.append(value)
    results = pl.pallas_call(
        body,
        in_specs=[specs[space] for space, value in arrays]
        + [pl.BlockSpec(memory_space=pl.ANY)] * len(unread),
        out_specs=[specs[space] for space, value in outs],
        scratch_shapes=list(scratch),
        input_output_aliases={count - 1: len(outs) - 1} if in_place else {},
        out_shape=[
            pltpu.VMEM(shape, dtype) if space == "vmem" else jax.ShapeDtypeStruct(shape, dtype)
            for space, (shape, dtype) in outs
        ],
        compiler_params=pltpu.CompilerParams(vmem_limit_bytes=VMEM_LIMIT),
        cost_estimate=pl.CostEstimate(flops=flops, bytes_accessed=moved, transcendentals=0),
    )(*operands, *unread)
    last = results[-1]
    if outs[-1][0] != "vmem":
        last = pltpu.with_memory_space_constraint(last, pltpu.HBM)
    LAST[:] = [last]
    return results


def in_vmem(values):
    return [("vmem", value) for value in values]


def join(pieces, out):
    at = 0
    for piece in pieces:
        out[at : at + piece.shape[0], :] = piece[...]
        at += piece.shape[0]


def place(pieces, order, out):
    size, order = pieces[0].shape[0], list(order)
    for piece in pieces:
        for at in range(0, piece.shape[0], size):
            to = order.pop(0) * size
            out[to : to + size, :] = piece[at : at + size, :]


def joined(pieces, after=(), flops=0):
    rows = sum(piece.shape[0] for piece in pieces)

    def kernel(*refs):
        join(refs[: len(pieces)], refs[-1])

    return call(
        kernel, in_vmem(pieces), [("vmem", ((rows, pieces[0].shape[1]), BF16))], flops, 0, after
    )[0]


class Weight:
    def __init__(self, me, value, rows, by_rows):
        self.me, self.value, self.by_rows = me, value, by_rows
        self.bits = rows.bit_length() - 2
        self.block = value.shape[0 if by_rows else 1] // rows
        self.width = value.shape[1 if by_rows else 0]
        self.shape = (self.block, self.width) if by_rows else (self.width, self.block)
        self.held = {}

    def part(self, ref, me, key):
        p, odd = key
        chip = p + (me & 1) * (reverse(p, self.bits) - p)
        at = (me ^ (2 * chip + odd)) * self.block
        at = pl.ds(pl.multiple_of(at, 128), self.block)
        return ref.at[at, :] if self.by_rows else ref.at[:, at]


def cut(ref, i, cuts):
    size = ref.shape[0] // cuts
    return ref.at[i * size : (i + 1) * size, :]


class Coming:
    def __init__(self, blocks):
        self.blocks = blocks
        self.weights = list(dict.fromkeys(weight for weight, key in blocks))
        self.count = len(blocks) * READ_CUTS
        self.inputs = [("hbm", weight.value) for weight in self.weights]
        self.outs = [("vmem", (weight.shape, BF16)) for weight, key in blocks]
        self.scratch = [pltpu.SemaphoreType.DMA((self.count,))] if blocks else []

    def copies(self, sources, helds, arrived, me):
        return [
            pltpu.make_async_copy(
                cut(weight.part(sources[self.weights.index(weight)], me, key), i, READ_CUTS),
                cut(held, i, READ_CUTS),
                arrived.at[n * READ_CUTS + i],
            )
            for n, ((weight, key), held) in enumerate(zip(self.blocks, helds))
            for i in range(READ_CUTS)
        ]

    def arrive(self, helds):
        for (weight, key), held in zip(self.blocks, helds):
            weight.held[key] = held


def load(blocks, after=()):
    coming = Coming(blocks)
    n = len(coming.inputs)

    def kernel(me_ref, *refs):
        copies = coming.copies(refs[:n], refs[n:-1], refs[-1], me_ref[0])
        for copy in copies:
            copy.start()
        for copy in copies:
            copy.wait()

    me = blocks[0][0].me
    coming.arrive(
        call(kernel, [("smem", me), *coming.inputs], coming.outs, 0, 0, after, coming.scratch)
    )


def project(weight, shards, positions, blocks, after=()):
    pieces, order = shards
    coming = Coming(blocks)
    tokens, n = sum(piece.shape[0] for piece in pieces), len(positions)
    block, by_rows = weight.block, weight.by_rows
    keys = [(reverse(p, weight.bits), 1) for p in positions] + [(p, 0) for p in positions]

    def kernel(me_ref, *refs):
        piece_refs, refs = refs[: len(pieces)], refs[len(pieces) :]
        parts, refs = refs[: 2 * n], refs[2 * n :]
        sources, refs = refs[: len(coming.inputs)], refs[len(coming.inputs) :]
        keep, send, refs = refs[0], refs[1], refs[2:]
        left, copies = refs[len(blocks)], []
        if blocks:
            copies = coming.copies(sources, refs[: len(blocks)], refs[-1], me_ref[0])
        for copy in copies:
            copy.start()

        @pl.when(me_ref[0] >= 0)
        def _():
            place(piece_refs, order, left)
            for i, part in enumerate(parts):
                out = dot(left[...], part[...], 1, 1 if by_rows else 0).astype(BF16)
                (send if i < n else keep)[i % n] = out

        for copy in copies:
            copy.wait()

    keep, send, *helds = call(
        kernel,
        [("smem", weight.me)]
        + in_vmem(pieces)
        + in_vmem([weight.held[key] for key in keys])
        + coming.inputs,
        [("vmem", ((n, tokens, block), BF16))] * 2 + coming.outs,
        0,
        0,
        after,
        [pltpu.VMEM((tokens, weight.width), BF16)] + coming.scratch,
    )
    coming.arrive(helds)
    return keep, send


def block_sum(weight, stacks, odds, cols, groups, so_far=()):
    width, by_rows, block = weight.width, weight.by_rows, weight.block
    chips = len(weight.held) // 2
    tokens = stacks[0].shape[0] // chips
    n, size = len(stacks), tokens // cols
    parts = [
        weight.held[(reverse(p, weight.bits) if odd else p, odd)]
        for odd in odds
        for p in range(chips)
    ]

    def kernel(*refs):
        stack_refs, part_refs, refs = refs[:n], refs[n : n + len(parts)], refs[n + len(parts) :]
        before, outs, total = refs[: len(so_far)], refs[len(so_far) : -1], refs[-1]
        for ref in before:
            total[...] = ref[...]
        for i, part in enumerate(part_refs):
            p = i % chips
            value = stack_refs[i // chips][p * tokens : (p + 1) * tokens, :]
            term = dot(value, part[...], 1, 0 if by_rows else 1)
            total[...] = total[...] + term if i or before else term
        if not groups:
            outs[0][...] = total[...]
        for group, out in zip(groups, outs):
            for i, q in enumerate(group):
                out[i * size : (i + 1) * size, :] = total[q * size : (q + 1) * size, :].astype(BF16)

    return call(
        kernel,
        in_vmem(stacks) + in_vmem(parts) + in_vmem(so_far),
        [("vmem", ((len(group) * size, width), BF16)) for group in groups]
        or [("vmem", ((tokens, width), F32))],
        2 * tokens * width * block * chips * n,
        2 * width * block * chips * n,
        (),
        [pltpu.VMEM((tokens, width), F32)],
    )


def block_keys(weight):
    chips = len(weight.held) // 2
    return [(reverse(p, weight.bits) if odd else p, odd) for odd in range(2) for p in range(chips)]


def weight_grad(weight, stacks, shards, odds=(0, 1), cols=1, groups=(), into=None):
    pieces, order = shards
    width, by_rows, block = weight.width, weight.by_rows, weight.block
    chips, n = len(weight.held) // 2, len(stacks)
    tokens = stacks[0].shape[0] // chips
    halves = 2
    size = (block if by_rows else width) // halves
    keys = block_keys(weight)
    order_of = [odd * chips + p for p in range(chips) for odd in odds]
    parts = [weight.held[key] for key in keys] if groups else []

    def kernel(me_ref, *refs):
        stack_refs, refs = refs[:n], refs[n:]
        piece_refs, refs = refs[: len(pieces)], refs[len(pieces) :]
        part_refs, refs = refs[: len(parts)], refs[len(parts) + (into is not None) :]
        sums, (grad, other, turned, ready, sent, total) = refs[: len(groups)], refs[len(groups) :]
        place(piece_refs, order, other)
        if not by_rows:
            turned[...] = other[...].T
        me = me_ref[0]

        def value(i):
            return stack_refs[i // chips], slice(i % chips * tokens, (i % chips + 1) * tokens)

        def writes(step):
            to = weight.part(grad, me, keys[order_of[step // halves]])
            at = step % halves * size
            to = to.at[at : at + size, :]
            slot = step % WRITES
            return [
                pltpu.make_async_copy(
                    cut(ready.at[slot], i, WRITE_CUTS), cut(to, i, WRITE_CUTS), sent.at[slot, i]
                )
                for i in range(WRITE_CUTS)
            ]

        def product(step):
            stack, of = value(order_of[step // halves])
            at = slice(step % halves * size, (step % halves + 1) * size)
            if by_rows:
                out = dot(stack[of, at], other[...], 0, 0)
            else:
                out = dot(turned[at, :], stack[of, :], 1, 0)
            ready[step % WRITES] = out.astype(BF16)

        steps = len(order_of) * halves
        for step in range(steps):
            if step >= WRITES:
                for write in writes(step - WRITES):
                    write.wait()
            if by_rows:
                product(step)
            else:
                pl.when(me >= 0)(functools.partial(product, step))
            for write in writes(step):
                write.start()

        @pl.when(me >= 0)
        def _():
            for i, part in enumerate(part_refs):
                stack, of = value(i)
                term = dot(stack[of, :], part[...], 1, 0)
                total[...] = term if i == 0 else total[...] + term
            rows = tokens // cols
            for group, out in zip(groups, sums):
                for i, q in enumerate(group):
                    out[i * rows : (i + 1) * rows, :] = total[q * rows : (q + 1) * rows, :].astype(BF16)

        for step in range(max(0, steps - WRITES), steps):
            for write in writes(step):
                write.wait()

    return call(
        kernel,
        [("smem", weight.me)]
        + in_vmem(stacks)
        + in_vmem(pieces)
        + in_vmem(parts)
        + ([("hbm", into)] if into is not None else []),
        [("vmem", ((len(group) * tokens // cols, width), BF16)) for group in groups]
        + [("hbm", (weight.value.shape, BF16))],
        2 * tokens * width * block * len(order_of) if 1 in odds else 0,
        2 * width * block * len(order_of) if 1 in odds else 0,
        (),
        [
            pltpu.VMEM((tokens, width), BF16),
            pltpu.VMEM((width, tokens), BF16),
            pltpu.VMEM((WRITES, size, width if by_rows else block), BF16),
            pltpu.SemaphoreType.DMA((WRITES, WRITE_CUTS)),
            pltpu.VMEM((tokens, width), F32),
        ],
        into is not None,
    )


def summed_half(keep, got, count, after=()):
    size = keep.shape[0] // count

    def kernel(keep_ref, got_ref, *outs):
        for i, out in enumerate(outs):
            at = slice(i * size, (i + 1) * size)
            total = keep_ref[at, :].astype(F32) + got_ref[at, :].astype(F32)
            out[...] = total.astype(out.dtype)

    shape = (size, keep.shape[1])
    outs = [("vmem", (shape, F32))] + [("vmem", (shape, BF16))] * (count - 1)
    return call(kernel, in_vmem([keep, got]), outs, 0, 0, after)


def added(*sums, space="vmem"):
    def kernel(*refs):
        refs, outs = refs[: -len(sums)], refs[-len(sums) :]
        for terms, out in zip(sums, outs):
            out[...] = sum(ref[...].astype(F32) for ref in refs[: len(terms)]).astype(BF16)
            refs = refs[len(terms) :]

    arrays = in_vmem([term for terms in sums for term in terms])
    return call(kernel, arrays, [(space, (terms[0].shape, BF16)) for terms in sums], 0, 0)


def block_of(terms):
    def total(refs):
        return sum(ref[block].astype(F32) for ref, (array, block) in zip(refs, terms))

    return total


def one_block(terms, dtype=BF16, flops=0):
    def kernel(*refs):
        refs[-1][0] = block_of(terms)(refs).astype(dtype)

    shape = (1, *terms[0][0].shape[1:])
    arrays = in_vmem([array for array, block in terms])
    return call(kernel, arrays, [("vmem", (shape, dtype))], flops, 0)[0]


def activate(terms):
    def kernel(*refs):
        total = block_of(terms)(refs)
        refs[-2][...] = total
        refs[-1][...] = gelu_fn(total).astype(BF16)

    shape = terms[0][0].shape[1:]
    outs = [("vmem", (shape, F32)), ("vmem", (shape, BF16))]
    return call(kernel, in_vmem([array for array, block in terms]), outs, PART_COST, 0)


def activate_back(hidden, terms):
    def kernel(hidden_ref, *refs):
        refs[-1][...] = gelu_back(hidden_ref[...], block_of(terms)(refs))

    arrays = [hidden] + [array for array, block in terms]
    return call(kernel, in_vmem(arrays), [("vmem", (hidden.shape, BF16))], 0, 0)[0]


def exchange_col(parts, cols):
    return [parts[0]] + [swap(parts[q], "col", q, cols) for q in range(cols - 1, 0, -1)]


def blocked(rows, cols, tokens, cotangent, w_in, w_out):
    LAST.clear()
    me = lax.axis_index("row").astype(jnp.int32).reshape(1)
    w_in, w_out = Weight(me, w_in, rows, False), Weight(me, w_out, rows, True)
    first, second, own = [1, 3], [2], [0]

    def keys(positions):
        return [(reverse(p, 2), 1) for p in positions] + [(p, 0) for p in positions]

    def other_core(value):
        return swap(value, "row", 1, rows)

    def doubled(stack, step, flops=0):
        return joined([stack, across(stack, step, rows)], (), flops)

    wanted = [(w, key) for w in (w_in, w_out) for part in (first, second, own) for key in keys(part)]

    flips = [1 << bit for bit in range(cols.bit_length() - 1)][::-1]
    token_pieces, cot_pieces, order = [tokens], [cotangent], [0]
    for hop, flip in enumerate(flips):
        sent = joined(token_pieces) if hop else tokens
        token_pieces.append(swap(sent, "col", flip, cols))
        if hop:
            sent = joined(cot_pieces, (token_pieces[hop],))
            cot_pieces.append(swap(sent, "col", flips[hop - 1], cols))
        if hop < 2:
            load(wanted[5 * hop : 5 + 3 * hop])
        order += [q ^ flip for q in order]
    token_shards = token_pieces, order
    cot_sent = joined(cot_pieces, (token_pieces[-1],))

    keep, sent = project(w_in, token_shards, first, wanted[8:10])
    got = other_core(sent)
    here, sent = project(w_in, token_shards, second + own, [])
    got_here, came = other_core(sent), across(added([keep, got])[0], 0, rows)
    cot_pieces.append(swap(joined([cot_sent]), "col", flips[-1], cols))
    cot_shards = cot_pieces, order
    load(wanted[10:12])
    sent = one_block([(here, 0), (got_here, 0), (came, 1)])
    terms = [(here, 1), (got_here, 1), (came, 0), (across(sent, 1, rows), 0)]

    keep, sent = project(w_out, cot_shards, first, wanted[12:14])
    got = other_core(sent)
    hidden, act = activate(terms)
    came = across(added([keep, got])[0], 0, rows)
    keep, sent = project(w_out, cot_shards, second, wanted[14:])
    got = other_core(sent)
    stack = doubled(act, 0, PART_COST)
    sent = one_block([(keep, 0), (got, 0), (came, 1)])
    last = across(sent, 1, rows)
    keep, sent = project(w_out, cot_shards, own, [])
    got = other_core(sent)
    part = one_block([(came, 0), (last, 0)], F32, PART_COST // 6)
    grad_hidden = activate_back(hidden, [(keep, 0), (part, 0), (got, 0)])
    stack = doubled(stack, 1)
    act = stack, other_core(stack)
    (grad_w_out,) = weight_grad(w_out, act[:1], cot_shards, (0,))
    back_stack = doubled(grad_hidden, 0)

    even, odd = range(0, cols, 2), range(1, cols, 2)
    keep, sent, grad_w_out = weight_grad(
        w_out, act, cot_shards, (1,), cols, (even, odd), grad_w_out
    )
    got = swap(sent, "col", 1, cols)
    back_stack = doubled(back_stack, 1)
    grad_hidden = back_stack, other_core(back_stack)
    so_far = block_sum(w_in, grad_hidden[:1], (0,), cols, [])
    token_parts = block_sum(w_in, grad_hidden[1:], (1,), cols, [[q] for q in range(cols)], so_far)
    layer_out, *sums = summed_half(keep, got, len(even))
    layer_parts = [swap(part, "col", q, cols) for part, q in zip(sums, even[1:])]
    token_parts = exchange_col(token_parts, cols)
    (grad_w_in,) = weight_grad(w_in, grad_hidden, token_shards)
    layer_out, grad_tokens = added([layer_out, *layer_parts], token_parts, space="window")
    return (layer_out, grad_tokens, grad_w_in, grad_w_out)


def collective(tokens, cotangent, w_in, w_out):
    token_full = lax.all_gather(tokens, "col", axis=0, tiled=True)
    cot_full = lax.all_gather(cotangent, "col", axis=0, tiled=True)

    def over(value, axis):
        return lax.psum_scatter(value.astype(BF16), axis, scatter_dimension=0, tiled=True)

    hidden = over(dot(token_full, w_in, 1, 0), "row").astype(F32)
    grad_act = over(dot(cot_full, w_out, 1, 1), "row").astype(F32)
    act = lax.all_gather(gelu_fn(hidden).astype(BF16), "row", axis=0, tiled=True)
    grad_hidden = lax.all_gather(gelu_back(hidden, grad_act), "row", axis=0, tiled=True)
    layer_out = over(dot(act, w_out, 1, 0), "col")
    grad_tokens = over(dot(grad_hidden, w_in, 1, 1), "col")
    grad_w_in = dot(token_full, grad_hidden, 0, 0).astype(BF16)
    grad_w_out = dot(act, cot_full, 0, 0).astype(BF16)
    return (layer_out, grad_tokens, grad_w_in, grad_w_out)


def solution(mesh):
    rows, cols = mesh.shape["row"], mesh.shape["col"]

    def shards(tokens, cotangent, w_in, w_out):
        powers = rows & (rows - 1) == 0 and cols & (cols - 1) == 0
        if powers and rows == 8 and cols > 2 and w_in.shape[1] % (rows * 128) == 0:
            return blocked(rows, cols, tokens, cotangent, w_in, w_out)
        return collective(tokens, cotangent, w_in, w_out)

    return jax.shard_map(
        shards,
        mesh=mesh,
        in_specs=(P("col", "row"), P("col", "row"), P("row", "col"), P("col", "row")),
        out_specs=(P("col", "row"), P("col", "row"), P("row", "col"), P("col", "row")),
        check_vma=False,
    )
```

```python
import functools

import jax
import jax.numpy as jnp
from jax import lax
from jax.experimental import pallas as pl
from jax.experimental.pallas import tpu as pltpu
from jax.sharding import PartitionSpec as P

BF16 = jnp.bfloat16
F32 = jnp.float32
VMEM_LIMIT = 10 * 1024 * 1024
WRITES = 6
READ_CUTS, WRITE_CUTS = 4, 3
PART_COST = 6 * 10**9


def gelu_fn(value):
    return jax.nn.gelu(value, approximate=True)


def gelu_back(hidden, grad_act):
    unused, pullback = jax.vjp(gelu_fn, hidden)
    return pullback(grad_act)[0].astype(BF16)


def swap(value, axis, flip, count):
    return lax.ppermute(value, axis, [(i, i ^ flip) for i in range(count)])


def reverse(p, bits):
    return sum(((p >> j) & 1) << (bits - 1 - j) for j in range(bits))


def across(value, step, rows):
    bits = rows.bit_length() - 2
    flips = [2 << (bits - 1 - step if i & 1 else step) for i in range(rows)]
    return lax.ppermute(value, "row", [(i, i ^ flips[i]) for i in range(rows)])


def dot(left, right, left_dim, right_dim):
    return lax.dot_general(
        left, right, (((left_dim,), (right_dim,)), ((), ())), preferred_element_type=F32
    )


LAST = []


def call(kernel, arrays, outs, flops, moved, after=(), scratch=(), in_place=False):
    unread, count = [*LAST, *after], len(arrays)

    def body(*refs):
        kernel(*refs[:count], *refs[count + len(unread) :])

    specs = {
        "smem": pl.BlockSpec(memory_space=pltpu.SMEM),
        "vmem": pl.BlockSpec(memory_space=pltpu.VMEM),
        "hbm": pl.BlockSpec(memory_space=pl.ANY),
        "window": pl.BlockSpec(),
    }
    operands = []
    for space, value in arrays:
        if space != "smem":
            value = pltpu.with_memory_space_constraint(
                value, pltpu.HBM if space == "hbm" else pltpu.VMEM
            )
        operands.append(value)
    results = pl.pallas_call(
        body,
        in_specs=[specs[space] for space, value in arrays]
        + [pl.BlockSpec(memory_space=pl.ANY)] * len(unread),
        out_specs=[specs[space] for space, value in outs],
        scratch_shapes=list(scratch),
        input_output_aliases={count - 1: len(outs) - 1} if in_place else {},
        out_shape=[
            pltpu.VMEM(shape, dtype) if space == "vmem" else jax.ShapeDtypeStruct(shape, dtype)
            for space, (shape, dtype) in outs
        ],
        compiler_params=pltpu.CompilerParams(vmem_limit_bytes=VMEM_LIMIT),
        cost_estimate=pl.CostEstimate(flops=flops, bytes_accessed=moved, transcendentals=0),
    )(*operands, *unread)
    last = results[-1]
    if outs[-1][0] != "vmem":
        last = pltpu.with_memory_space_constraint(last, pltpu.HBM)
    LAST[:] = [last]
    return results


def in_vmem(values):
    return [("vmem", value) for value in values]


def join(pieces, out):
    at = 0
    for piece in pieces:
        out[at : at + piece.shape[0], :] = piece[...]
        at += piece.shape[0]


def place(pieces, order, out):
    size, order = pieces[0].shape[0], list(order)
    for piece in pieces:
        for at in range(0, piece.shape[0], size):
            to = order.pop(0) * size
            out[to : to + size, :] = piece[at : at + size, :]


def joined(pieces, after=(), flops=0):
    rows = sum(piece.shape[0] for piece in pieces)

    def kernel(*refs):
        join(refs[: len(pieces)], refs[-1])

    return call(
        kernel, in_vmem(pieces), [("vmem", ((rows, pieces[0].shape[1]), BF16))], flops, 0, after
    )[0]


class Weight:
    def __init__(self, me, value, rows, by_rows):
        self.me, self.value, self.by_rows = me, value, by_rows
        self.bits = rows.bit_length() - 2
        self.block = value.shape[0 if by_rows else 1] // rows
        self.width = value.shape[1 if by_rows else 0]
        self.shape = (self.block, self.width) if by_rows else (self.width, self.block)
        self.held = {}

    def part(self, ref, me, key):
        p, odd = key
        chip = p + (me & 1) * (reverse(p, self.bits) - p)
        at = (me ^ (2 * chip + odd)) * self.block
        at = pl.ds(pl.multiple_of(at, 128), self.block)
        return ref.at[at, :] if self.by_rows else ref.at[:, at]


def cut(ref, i, cuts):
    size = ref.shape[0] // cuts
    return ref.at[i * size : (i + 1) * size, :]


class Coming:
    def __init__(self, blocks):
        self.blocks = blocks
        self.weights = list(dict.fromkeys(weight for weight, key in blocks))
        self.count = len(blocks) * READ_CUTS
        self.inputs = [("hbm", weight.value) for weight in self.weights]
        self.outs = [("vmem", (weight.shape, BF16)) for weight, key in blocks]
        self.scratch = [pltpu.SemaphoreType.DMA((self.count,))] if blocks else []

    def copies(self, sources, helds, arrived, me):
        return [
            pltpu.make_async_copy(
                cut(weight.part(sources[self.weights.index(weight)], me, key), i, READ_CUTS),
                cut(held, i, READ_CUTS),
                arrived.at[n * READ_CUTS + i],
            )
            for n, ((weight, key), held) in enumerate(zip(self.blocks, helds))
            for i in range(READ_CUTS)
        ]

    def arrive(self, helds):
        for (weight, key), held in zip(self.blocks, helds):
            weight.held[key] = held


def load(blocks, after=()):
    coming = Coming(blocks)
    n = len(coming.inputs)

    def kernel(me_ref, *refs):
        copies = coming.copies(refs[:n], refs[n:-1], refs[-1], me_ref[0])
        for copy in copies:
            copy.start()
        for copy in copies:
            copy.wait()

    me = blocks[0][0].me
    coming.arrive(
        call(kernel, [("smem", me), *coming.inputs], coming.outs, 0, 0, after, coming.scratch)
    )


def project(weight, shards, positions, blocks, after=()):
    pieces, order = shards
    coming = Coming(blocks)
    tokens, n = sum(piece.shape[0] for piece in pieces), len(positions)
    block, by_rows = weight.block, weight.by_rows
    keys = [(reverse(p, weight.bits), 1) for p in positions] + [(p, 0) for p in positions]

    def kernel(me_ref, *refs):
        piece_refs, refs = refs[: len(pieces)], refs[len(pieces) :]
        parts, refs = refs[: 2 * n], refs[2 * n :]
        sources, refs = refs[: len(coming.inputs)], refs[len(coming.inputs) :]
        keep, send, refs = refs[0], refs[1], refs[2:]
        left, copies = refs[len(blocks)], []
        if blocks:
            copies = coming.copies(sources, refs[: len(blocks)], refs[-1], me_ref[0])
        for copy in copies:
            copy.start()

        @pl.when(me_ref[0] >= 0)
        def _():
            place(piece_refs, order, left)
            for i, part in enumerate(parts):
                out = dot(left[...], part[...], 1, 1 if by_rows else 0).astype(BF16)
                (send if i < n else keep)[i % n] = out

        for copy in copies:
            copy.wait()

    keep, send, *helds = call(
        kernel,
        [("smem", weight.me)]
        + in_vmem(pieces)
        + in_vmem([weight.held[key] for key in keys])
        + coming.inputs,
        [("vmem", ((n, tokens, block), BF16))] * 2 + coming.outs,
        0,
        0,
        after,
        [pltpu.VMEM((tokens, weight.width), BF16)] + coming.scratch,
    )
    coming.arrive(helds)
    return keep, send


def block_sum(weight, stacks, odds, cols, groups, so_far=()):
    width, by_rows, block = weight.width, weight.by_rows, weight.block
    chips = len(weight.held) // 2
    tokens = stacks[0].shape[0] // chips
    n, size = len(stacks), tokens // cols
    parts = [
        weight.held[(reverse(p, weight.bits) if odd else p, odd)]
        for odd in odds
        for p in range(chips)
    ]

    def kernel(*refs):
        stack_refs, part_refs, refs = refs[:n], refs[n : n + len(parts)], refs[n + len(parts) :]
        before, outs, total = refs[: len(so_far)], refs[len(so_far) : -1], refs[-1]
        for ref in before:
            total[...] = ref[...]
        for i, part in enumerate(part_refs):
            p = i % chips
            value = stack_refs[i // chips][p * tokens : (p + 1) * tokens, :]
            term = dot(value, part[...], 1, 0 if by_rows else 1)
            total[...] = total[...] + term if i or before else term
        if not groups:
            outs[0][...] = total[...]
        for group, out in zip(groups, outs):
            for i, q in enumerate(group):
                out[i * size : (i + 1) * size, :] = total[q * size : (q + 1) * size, :].astype(BF16)

    return call(
        kernel,
        in_vmem(stacks) + in_vmem(parts) + in_vmem(so_far),
        [("vmem", ((len(group) * size, width), BF16)) for group in groups]
        or [("vmem", ((tokens, width), F32))],
        2 * tokens * width * block * chips * n,
        2 * width * block * chips * n,
        (),
        [pltpu.VMEM((tokens, width), F32)],
    )


def block_keys(weight):
    chips = len(weight.held) // 2
    return [(reverse(p, weight.bits) if odd else p, odd) for odd in range(2) for p in range(chips)]


def weight_grad(weight, stacks, shards, odds=(0, 1), cols=1, groups=(), into=None):
    pieces, order = shards
    width, by_rows, block = weight.width, weight.by_rows, weight.block
    chips, n = len(weight.held) // 2, len(stacks)
    tokens = stacks[0].shape[0] // chips
    halves = 2
    size = (block if by_rows else width) // halves
    keys = block_keys(weight)
    order_of = [odd * chips + p for p in range(chips) for odd in odds]
    parts = [weight.held[key] for key in keys] if groups else []

    def kernel(me_ref, *refs):
        stack_refs, refs = refs[:n], refs[n:]
        piece_refs, refs = refs[: len(pieces)], refs[len(pieces) :]
        part_refs, refs = refs[: len(parts)], refs[len(parts) + (into is not None) :]
        sums, (grad, other, turned, ready, sent, total) = refs[: len(groups)], refs[len(groups) :]
        place(piece_refs, order, other)
        if not by_rows:
            turned[...] = other[...].T
        me = me_ref[0]

        def value(i):
            return stack_refs[i // chips], slice(i % chips * tokens, (i % chips + 1) * tokens)

        def writes(step):
            to = weight.part(grad, me, keys[order_of[step // halves]])
            at = step % halves * size
            to = to.at[at : at + size, :]
            slot = step % WRITES
            return [
                pltpu.make_async_copy(
                    cut(ready.at[slot], i, WRITE_CUTS), cut(to, i, WRITE_CUTS), sent.at[slot, i]
                )
                for i in range(WRITE_CUTS)
            ]

        def product(step):
            stack, of = value(order_of[step // halves])
            at = slice(step % halves * size, (step % halves + 1) * size)
            if by_rows:
                out = dot(stack[of, at], other[...], 0, 0)
            else:
                out = dot(turned[at, :], stack[of, :], 1, 0)
            ready[step % WRITES] = out.astype(BF16)

        steps = len(order_of) * halves
        for step in range(steps):
            if step >= WRITES:
                for write in writes(step - WRITES):
                    write.wait()
            if by_rows:
                product(step)
            else:
                pl.when(me >= 0)(functools.partial(product, step))
            for write in writes(step):
                write.start()

        @pl.when(me >= 0)
        def _():
            for i, part in enumerate(part_refs):
                stack, of = value(i)
                term = dot(stack[of, :], part[...], 1, 0)
                total[...] = term if i == 0 else total[...] + term
            rows = tokens // cols
            for group, out in zip(groups, sums):
                for i, q in enumerate(group):
                    out[i * rows : (i + 1) * rows, :] = total[q * rows : (q + 1) * rows, :].astype(BF16)

        for step in range(max(0, steps - WRITES), steps):
            for write in writes(step):
                write.wait()

    return call(
        kernel,
        [("smem", weight.me)]
        + in_vmem(stacks)
        + in_vmem(pieces)
        + in_vmem(parts)
        + ([("hbm", into)] if into is not None else []),
        [("vmem", ((len(group) * tokens // cols, width), BF16)) for group in groups]
        + [("hbm", (weight.value.shape, BF16))],
        2 * tokens * width * block * len(order_of) if 1 in odds else 0,
        2 * width * block * len(order_of) if 1 in odds else 0,
        (),
        [
            pltpu.VMEM((tokens, width), BF16),
            pltpu.VMEM((width, tokens), BF16),
            pltpu.VMEM((WRITES, size, width if by_rows else block), BF16),
            pltpu.SemaphoreType.DMA((WRITES, WRITE_CUTS)),
            pltpu.VMEM((tokens, width), F32),
        ],
        into is not None,
    )


def summed_half(keep, got, count, after=()):
    size = keep.shape[0] // count

    def kernel(keep_ref, got_ref, *outs):
        for i, out in enumerate(outs):
            at = slice(i * size, (i + 1) * size)
            total = keep_ref[at, :].astype(F32) + got_ref[at, :].astype(F32)
            out[...] = total.astype(out.dtype)

    shape = (size, keep.shape[1])
    outs = [("vmem", (shape, F32))] + [("vmem", (shape, BF16))] * (count - 1)
    return call(kernel, in_vmem([keep, got]), outs, 0, 0, after)


def added(*sums, space="vmem"):
    def kernel(*refs):
        refs, outs = refs[: -len(sums)], refs[-len(sums) :]
        for terms, out in zip(sums, outs):
            out[...] = sum(ref[...].astype(F32) for ref in refs[: len(terms)]).astype(BF16)
            refs = refs[len(terms) :]

    arrays = in_vmem([term for terms in sums for term in terms])
    return call(kernel, arrays, [(space, (terms[0].shape, BF16)) for terms in sums], 0, 0)


def block_of(terms):
    def total(refs):
        return sum(ref[block].astype(F32) for ref, (array, block) in zip(refs, terms))

    return total


def one_block(terms, dtype=BF16, flops=0):
    def kernel(*refs):
        refs[-1][0] = block_of(terms)(refs).astype(dtype)

    shape = (1, *terms[0][0].shape[1:])
    arrays = in_vmem([array for array, block in terms])
    return call(kernel, arrays, [("vmem", (shape, dtype))], flops, 0)[0]


def activate(terms):
    def kernel(*refs):
        total = block_of(terms)(refs)
        refs[-2][...] = total
        refs[-1][...] = gelu_fn(total).astype(BF16)

    shape = terms[0][0].shape[1:]
    outs = [("vmem", (shape, F32)), ("vmem", (shape, BF16))]
    return call(kernel, in_vmem([array for array, block in terms]), outs, PART_COST, 0)


def activate_back(hidden, terms):
    def kernel(hidden_ref, *refs):
        refs[-1][...] = gelu_back(hidden_ref[...], block_of(terms)(refs))

    arrays = [hidden] + [array for array, block in terms]
    return call(kernel, in_vmem(arrays), [("vmem", (hidden.shape, BF16))], PART_COST, 0)[0]


def exchange_col(parts, cols):
    return [parts[0]] + [swap(parts[q], "col", q, cols) for q in range(cols - 1, 0, -1)]


def blocked(rows, cols, tokens, cotangent, w_in, w_out):
    LAST.clear()
    me = lax.axis_index("row").astype(jnp.int32).reshape(1)
    w_in, w_out = Weight(me, w_in, rows, False), Weight(me, w_out, rows, True)
    first, second, own = [1, 3], [2], [0]

    def keys(positions):
        return [(reverse(p, 2), 1) for p in positions] + [(p, 0) for p in positions]

    def other_core(value):
        return swap(value, "row", 1, rows)

    def doubled(stack, step, flops=0):
        return joined([stack, across(stack, step, rows)], (), flops)

    wanted = [(w, key) for w in (w_in, w_out) for part in (first, second, own) for key in keys(part)]

    flips = [1 << bit for bit in range(cols.bit_length() - 1)][::-1]
    token_pieces, cot_pieces, order = [tokens], [cotangent], [0]
    for hop, flip in enumerate(flips):
        sent = joined(token_pieces) if hop else tokens
        token_pieces.append(swap(sent, "col", flip, cols))
        if hop:
            sent = joined(cot_pieces, (token_pieces[hop],))
            cot_pieces.append(swap(sent, "col", flips[hop - 1], cols))
        if hop < 2:
            load(wanted[5 * hop : 5 + 3 * hop])
        order += [q ^ flip for q in order]
    token_shards = token_pieces, order
    cot_sent = joined(cot_pieces, (token_pieces[-1],))

    keep, sent = project(w_in, token_shards, first, wanted[8:10])
    got = other_core(sent)
    here, sent = project(w_in, token_shards, second + own, [])
    got_here, came = other_core(sent), across(added([keep, got])[0], 0, rows)
    cot_pieces.append(swap(joined([cot_sent]), "col", flips[-1], cols))
    cot_shards = cot_pieces, order
    load(wanted[10:12])
    sent = one_block([(here, 0), (got_here, 0), (came, 1)])
    terms = [(here, 1), (got_here, 1), (came, 0), (across(sent, 1, rows), 0)]

    keep, sent = project(w_out, cot_shards, first, wanted[12:14])
    got = other_core(sent)
    hidden, act = activate(terms)
    came = across(added([keep, got])[0], 0, rows)
    keep, sent = project(w_out, cot_shards, second, wanted[14:])
    got = other_core(sent)
    own_keep, sent = project(w_out, cot_shards, own, [])
    own_got = other_core(sent)
    sent = one_block([(keep, 0), (got, 0), (came, 1)])
    last = across(sent, 1, rows)
    stack = doubled(act, 0)
    grad_hidden = activate_back(hidden, [(own_keep, 0), (own_got, 0), (came, 0), (last, 0)])
    stack = doubled(stack, 1)
    act = stack, other_core(stack)
    back_stack = doubled(grad_hidden, 0, PART_COST)

    even, odd = range(0, cols, 2), range(1, cols, 2)
    keep, sent, grad_w_out = weight_grad(w_out, act, cot_shards, (0, 1), cols, (even, odd))
    got = swap(sent, "col", 1, cols)
    back_stack = doubled(back_stack, 1)
    grad_hidden = back_stack, other_core(back_stack)
    so_far = block_sum(w_in, grad_hidden[:1], (0,), cols, [])
    token_parts = block_sum(w_in, grad_hidden[1:], (1,), cols, [[q] for q in range(cols)], so_far)
    layer_out, *sums = summed_half(keep, got, len(even))
    layer_parts = [swap(part, "col", q, cols) for part, q in zip(sums, even[1:])]
    token_parts = exchange_col(token_parts, cols)
    (grad_w_in,) = weight_grad(w_in, grad_hidden, token_shards)
    layer_out, grad_tokens = added([layer_out, *layer_parts], token_parts, space="window")
    return (layer_out, grad_tokens, grad_w_in, grad_w_out)


def collective(tokens, cotangent, w_in, w_out):
    token_full = lax.all_gather(tokens, "col", axis=0, tiled=True)
    cot_full = lax.all_gather(cotangent, "col", axis=0, tiled=True)

    def over(value, axis):
        return lax.psum_scatter(value.astype(BF16), axis, scatter_dimension=0, tiled=True)

    hidden = over(dot(token_full, w_in, 1, 0), "row").astype(F32)
    grad_act = over(dot(cot_full, w_out, 1, 1), "row").astype(F32)
    act = lax.all_gather(gelu_fn(hidden).astype(BF16), "row", axis=0, tiled=True)
    grad_hidden = lax.all_gather(gelu_back(hidden, grad_act), "row", axis=0, tiled=True)
    layer_out = over(dot(act, w_out, 1, 0), "col")
    grad_tokens = over(dot(grad_hidden, w_in, 1, 1), "col")
    grad_w_in = dot(token_full, grad_hidden, 0, 0).astype(BF16)
    grad_w_out = dot(act, cot_full, 0, 0).astype(BF16)
    return (layer_out, grad_tokens, grad_w_in, grad_w_out)


def solution(mesh):
    rows, cols = mesh.shape["row"], mesh.shape["col"]

    def shards(tokens, cotangent, w_in, w_out):
        powers = rows & (rows - 1) == 0 and cols & (cols - 1) == 0
        if powers and rows == 8 and cols > 2 and w_in.shape[1] % (rows * 128) == 0:
            return blocked(rows, cols, tokens, cotangent, w_in, w_out)
        return collective(tokens, cotangent, w_in, w_out)

    return jax.shard_map(
        shards,
        mesh=mesh,
        in_specs=(P("col", "row"), P("col", "row"), P("row", "col"), P("col", "row")),
        out_specs=(P("col", "row"), P("col", "row"), P("row", "col"), P("col", "row")),
        check_vma=False,
    )
```

```python
import functools

import jax
import jax.numpy as jnp
from jax import lax
from jax.experimental import pallas as pl
from jax.experimental.pallas import tpu as pltpu
from jax.sharding import PartitionSpec as P

BF16 = jnp.bfloat16
F32 = jnp.float32
VMEM_LIMIT = 10 * 1024 * 1024
WRITES = 6
READ_CUTS, WRITE_CUTS = 4, 3
PART_COST = 6 * 10**9
BACK_COST = 6 * 10**9


def gelu_fn(value):
    return jax.nn.gelu(value, approximate=True)


def gelu_back(hidden, grad_act):
    unused, pullback = jax.vjp(gelu_fn, hidden)
    return pullback(grad_act)[0].astype(BF16)


def swap(value, axis, flip, count):
    return lax.ppermute(value, axis, [(i, i ^ flip) for i in range(count)])


def reverse(p, bits):
    return sum(((p >> j) & 1) << (bits - 1 - j) for j in range(bits))


def across(value, step, rows):
    bits = rows.bit_length() - 2
    flips = [2 << (bits - 1 - step if i & 1 else step) for i in range(rows)]
    return lax.ppermute(value, "row", [(i, i ^ flips[i]) for i in range(rows)])


def dot(left, right, left_dim, right_dim):
    return lax.dot_general(
        left, right, (((left_dim,), (right_dim,)), ((), ())), preferred_element_type=F32
    )


LAST = []


def call(kernel, arrays, outs, flops, moved, after=(), scratch=(), in_place=False):
    unread, count = [*LAST, *after], len(arrays)

    def body(*refs):
        kernel(*refs[:count], *refs[count + len(unread) :])

    specs = {
        "smem": pl.BlockSpec(memory_space=pltpu.SMEM),
        "vmem": pl.BlockSpec(memory_space=pltpu.VMEM),
        "hbm": pl.BlockSpec(memory_space=pl.ANY),
        "window": pl.BlockSpec(),
    }
    operands = []
    for space, value in arrays:
        if space != "smem":
            value = pltpu.with_memory_space_constraint(
                value, pltpu.HBM if space == "hbm" else pltpu.VMEM
            )
        operands.append(value)
    results = pl.pallas_call(
        body,
        in_specs=[specs[space] for space, value in arrays]
        + [pl.BlockSpec(memory_space=pl.ANY)] * len(unread),
        out_specs=[specs[space] for space, value in outs],
        scratch_shapes=list(scratch),
        input_output_aliases={count - 1: len(outs) - 1} if in_place else {},
        out_shape=[
            pltpu.VMEM(shape, dtype) if space == "vmem" else jax.ShapeDtypeStruct(shape, dtype)
            for space, (shape, dtype) in outs
        ],
        compiler_params=pltpu.CompilerParams(vmem_limit_bytes=VMEM_LIMIT),
        cost_estimate=pl.CostEstimate(flops=flops, bytes_accessed=moved, transcendentals=0),
    )(*operands, *unread)
    last = results[-1]
    if outs[-1][0] != "vmem":
        last = pltpu.with_memory_space_constraint(last, pltpu.HBM)
    LAST[:] = [last]
    return results


def in_vmem(values):
    return [("vmem", value) for value in values]


def join(pieces, out):
    at = 0
    for piece in pieces:
        out[at : at + piece.shape[0], :] = piece[...]
        at += piece.shape[0]


def place(pieces, order, out):
    size, order = pieces[0].shape[0], list(order)
    for piece in pieces:
        for at in range(0, piece.shape[0], size):
            to = order.pop(0) * size
            out[to : to + size, :] = piece[at : at + size, :]


def joined(pieces, after=(), flops=0):
    rows = sum(piece.shape[0] for piece in pieces)

    def kernel(*refs):
        join(refs[: len(pieces)], refs[-1])

    return call(
        kernel, in_vmem(pieces), [("vmem", ((rows, pieces[0].shape[1]), BF16))], flops, 0, after
    )[0]


class Weight:
    def __init__(self, me, value, rows, by_rows):
        self.me, self.value, self.by_rows = me, value, by_rows
        self.bits = rows.bit_length() - 2
        self.block = value.shape[0 if by_rows else 1] // rows
        self.width = value.shape[1 if by_rows else 0]
        self.shape = (self.block, self.width) if by_rows else (self.width, self.block)
        self.held = {}

    def part(self, ref, me, key):
        p, odd = key
        chip = p + (me & 1) * (reverse(p, self.bits) - p)
        at = (me ^ (2 * chip + odd)) * self.block
        at = pl.ds(pl.multiple_of(at, 128), self.block)
        return ref.at[at, :] if self.by_rows else ref.at[:, at]


def cut(ref, i, cuts):
    size = ref.shape[0] // cuts
    return ref.at[i * size : (i + 1) * size, :]


class Coming:
    def __init__(self, blocks):
        self.blocks = blocks
        self.weights = list(dict.fromkeys(weight for weight, key in blocks))
        self.count = len(blocks) * READ_CUTS
        self.inputs = [("hbm", weight.value) for weight in self.weights]
        self.outs = [("vmem", (weight.shape, BF16)) for weight, key in blocks]
        self.scratch = [pltpu.SemaphoreType.DMA((self.count,))] if blocks else []

    def copies(self, sources, helds, arrived, me):
        return [
            pltpu.make_async_copy(
                cut(weight.part(sources[self.weights.index(weight)], me, key), i, READ_CUTS),
                cut(held, i, READ_CUTS),
                arrived.at[n * READ_CUTS + i],
            )
            for n, ((weight, key), held) in enumerate(zip(self.blocks, helds))
            for i in range(READ_CUTS)
        ]

    def arrive(self, helds):
        for (weight, key), held in zip(self.blocks, helds):
            weight.held[key] = held


def load(blocks, after=()):
    coming = Coming(blocks)
    n = len(coming.inputs)

    def kernel(me_ref, *refs):
        copies = coming.copies(refs[:n], refs[n:-1], refs[-1], me_ref[0])
        for copy in copies:
            copy.start()
        for copy in copies:
            copy.wait()

    me = blocks[0][0].me
    coming.arrive(
        call(kernel, [("smem", me), *coming.inputs], coming.outs, 0, 0, after, coming.scratch)
    )


def project(weight, shards, positions, blocks, after=()):
    pieces, order = shards
    coming = Coming(blocks)
    tokens, n = sum(piece.shape[0] for piece in pieces), len(positions)
    block, by_rows = weight.block, weight.by_rows
    keys = [(reverse(p, weight.bits), 1) for p in positions] + [(p, 0) for p in positions]

    def kernel(me_ref, *refs):
        piece_refs, refs = refs[: len(pieces)], refs[len(pieces) :]
        parts, refs = refs[: 2 * n], refs[2 * n :]
        sources, refs = refs[: len(coming.inputs)], refs[len(coming.inputs) :]
        keep, send, refs = refs[0], refs[1], refs[2:]
        left, copies = refs[len(blocks)], []
        if blocks:
            copies = coming.copies(sources, refs[: len(blocks)], refs[-1], me_ref[0])
        for copy in copies:
            copy.start()

        @pl.when(me_ref[0] >= 0)
        def _():
            place(piece_refs, order, left)
            for i, part in enumerate(parts):
                out = dot(left[...], part[...], 1, 1 if by_rows else 0).astype(BF16)
                (send if i < n else keep)[i % n] = out

        for copy in copies:
            copy.wait()

    keep, send, *helds = call(
        kernel,
        [("smem", weight.me)]
        + in_vmem(pieces)
        + in_vmem([weight.held[key] for key in keys])
        + coming.inputs,
        [("vmem", ((n, tokens, block), BF16))] * 2 + coming.outs,
        0,
        0,
        after,
        [pltpu.VMEM((tokens, weight.width), BF16)] + coming.scratch,
    )
    coming.arrive(helds)
    return keep, send


def block_sum(weight, stacks, odds, cols, groups, so_far=()):
    width, by_rows, block = weight.width, weight.by_rows, weight.block
    chips = len(weight.held) // 2
    tokens = stacks[0].shape[0] // chips
    n, size = len(stacks), tokens // cols
    parts = [
        weight.held[(reverse(p, weight.bits) if odd else p, odd)]
        for odd in odds
        for p in range(chips)
    ]

    def kernel(*refs):
        stack_refs, part_refs, refs = refs[:n], refs[n : n + len(parts)], refs[n + len(parts) :]
        before, outs, total = refs[: len(so_far)], refs[len(so_far) : -1], refs[-1]
        for ref in before:
            total[...] = ref[...]
        for i, part in enumerate(part_refs):
            p = i % chips
            value = stack_refs[i // chips][p * tokens : (p + 1) * tokens, :]
            term = dot(value, part[...], 1, 0 if by_rows else 1)
            total[...] = total[...] + term if i or before else term
        if not groups:
            outs[0][...] = total[...]
        for group, out in zip(groups, outs):
            for i, q in enumerate(group):
                out[i * size : (i + 1) * size, :] = total[q * size : (q + 1) * size, :].astype(BF16)

    return call(
        kernel,
        in_vmem(stacks) + in_vmem(parts) + in_vmem(so_far),
        [("vmem", ((len(group) * size, width), BF16)) for group in groups]
        or [("vmem", ((tokens, width), F32))],
        2 * tokens * width * block * chips * n,
        2 * width * block * chips * n,
        (),
        [pltpu.VMEM((tokens, width), F32)],
    )


def block_keys(weight):
    chips = len(weight.held) // 2
    return [(reverse(p, weight.bits) if odd else p, odd) for odd in range(2) for p in range(chips)]


def weight_grad(weight, stacks, shards, odds=(0, 1), cols=1, groups=(), into=None):
    pieces, order = shards
    width, by_rows, block = weight.width, weight.by_rows, weight.block
    chips, n = len(weight.held) // 2, len(stacks)
    tokens = stacks[0].shape[0] // chips
    halves = 2
    size = (block if by_rows else width) // halves
    keys = block_keys(weight)
    order_of = [odd * chips + p for p in range(chips) for odd in odds]
    parts = [weight.held[key] for key in keys] if groups else []

    def kernel(me_ref, *refs):
        stack_refs, refs = refs[:n], refs[n:]
        piece_refs, refs = refs[: len(pieces)], refs[len(pieces) :]
        part_refs, refs = refs[: len(parts)], refs[len(parts) + (into is not None) :]
        sums, (grad, other, turned, ready, sent, total) = refs[: len(groups)], refs[len(groups) :]
        place(piece_refs, order, other)
        if not by_rows:
            turned[...] = other[...].T
        me = me_ref[0]

        def value(i):
            return stack_refs[i // chips], slice(i % chips * tokens, (i % chips + 1) * tokens)

        def writes(step):
            to = weight.part(grad, me, keys[order_of[step // halves]])
            at = step % halves * size
            to = to.at[at : at + size, :]
            slot = step % WRITES
            return [
                pltpu.make_async_copy(
                    cut(ready.at[slot], i, WRITE_CUTS), cut(to, i, WRITE_CUTS), sent.at[slot, i]
                )
                for i in range(WRITE_CUTS)
            ]

        def product(step):
            stack, of = value(order_of[step // halves])
            at = slice(step % halves * size, (step % halves + 1) * size)
            if by_rows:
                out = dot(stack[of, at], other[...], 0, 0)
            else:
                out = dot(turned[at, :], stack[of, :], 1, 0)
            ready[step % WRITES] = out.astype(BF16)

        steps = len(order_of) * halves
        for step in range(steps):
            if step >= WRITES:
                for write in writes(step - WRITES):
                    write.wait()
            if by_rows:
                product(step)
            else:
                pl.when(me >= 0)(functools.partial(product, step))
            for write in writes(step):
                write.start()

        @pl.when(me >= 0)
        def _():
            for i, part in enumerate(part_refs):
                stack, of = value(i)
                term = dot(stack[of, :], part[...], 1, 0)
                total[...] = term if i == 0 else total[...] + term
            rows = tokens // cols
            for group, out in zip(groups, sums):
                for i, q in enumerate(group):
                    out[i * rows : (i + 1) * rows, :] = total[q * rows : (q + 1) * rows, :].astype(BF16)

        for step in range(max(0, steps - WRITES), steps):
            for write in writes(step):
                write.wait()

    return call(
        kernel,
        [("smem", weight.me)]
        + in_vmem(stacks)
        + in_vmem(pieces)
        + in_vmem(parts)
        + ([("hbm", into)] if into is not None else []),
        [("vmem", ((len(group) * tokens // cols, width), BF16)) for group in groups]
        + [("hbm", (weight.value.shape, BF16))],
        2 * tokens * width * block * len(order_of) if 1 in odds else 0,
        2 * width * block * len(order_of) if 1 in odds else 0,
        (),
        [
            pltpu.VMEM((tokens, width), BF16),
            pltpu.VMEM((width, tokens), BF16),
            pltpu.VMEM((WRITES, size, width if by_rows else block), BF16),
            pltpu.SemaphoreType.DMA((WRITES, WRITE_CUTS)),
            pltpu.VMEM((tokens, width), F32),
        ],
        into is not None,
    )


def summed_half(keep, got, count, after=()):
    size = keep.shape[0] // count

    def kernel(keep_ref, got_ref, *outs):
        for i, out in enumerate(outs):
            at = slice(i * size, (i + 1) * size)
            total = keep_ref[at, :].astype(F32) + got_ref[at, :].astype(F32)
            out[...] = total.astype(out.dtype)

    shape = (size, keep.shape[1])
    outs = [("vmem", (shape, F32))] + [("vmem", (shape, BF16))] * (count - 1)
    return call(kernel, in_vmem([keep, got]), outs, 0, 0, after)


def added(*sums, space="vmem"):
    def kernel(*refs):
        refs, outs = refs[: -len(sums)], refs[-len(sums) :]
        for terms, out in zip(sums, outs):
            out[...] = sum(ref[...].astype(F32) for ref in refs[: len(terms)]).astype(BF16)
            refs = refs[len(terms) :]

    arrays = in_vmem([term for terms in sums for term in terms])
    return call(kernel, arrays, [(space, (terms[0].shape, BF16)) for terms in sums], 0, 0)


def block_of(terms):
    def total(refs):
        return sum(ref[block].astype(F32) for ref, (array, block) in zip(refs, terms))

    return total


def one_block(terms, dtype=BF16, flops=0):
    def kernel(*refs):
        refs[-1][0] = block_of(terms)(refs).astype(dtype)

    shape = (1, *terms[0][0].shape[1:])
    arrays = in_vmem([array for array, block in terms])
    return call(kernel, arrays, [("vmem", (shape, dtype))], flops, 0)[0]


def activate(terms):
    def kernel(*refs):
        total = block_of(terms)(refs)
        refs[-2][...] = total
        refs[-1][...] = gelu_fn(total).astype(BF16)

    shape = terms[0][0].shape[1:]
    outs = [("vmem", (shape, F32)), ("vmem", (shape, BF16))]
    return call(kernel, in_vmem([array for array, block in terms]), outs, PART_COST, 0)


def activate_back(hidden, terms):
    def kernel(hidden_ref, *refs):
        refs[-1][...] = gelu_back(hidden_ref[...], block_of(terms)(refs))

    arrays = [hidden] + [array for array, block in terms]
    return call(kernel, in_vmem(arrays), [("vmem", (hidden.shape, BF16))], BACK_COST, 0)[0]


def exchange_col(parts, cols):
    return [parts[0]] + [swap(parts[q], "col", q, cols) for q in range(cols - 1, 0, -1)]


def blocked(rows, cols, tokens, cotangent, w_in, w_out):
    LAST.clear()
    me = lax.axis_index("row").astype(jnp.int32).reshape(1)
    w_in, w_out = Weight(me, w_in, rows, False), Weight(me, w_out, rows, True)
    first, second, own = [1, 3], [2], [0]

    def keys(positions):
        return [(reverse(p, 2), 1) for p in positions] + [(p, 0) for p in positions]

    def other_core(value):
        return swap(value, "row", 1, rows)

    def doubled(stack, step, flops=0):
        return joined([stack, across(stack, step, rows)], (), flops)

    wanted = [(w, key) for w in (w_in, w_out) for part in (first, second, own) for key in keys(part)]

    flips = [1 << bit for bit in range(cols.bit_length() - 1)][::-1]
    token_pieces, cot_pieces, order = [tokens], [cotangent], [0]
    for hop, flip in enumerate(flips):
        sent = joined(token_pieces) if hop else tokens
        token_pieces.append(swap(sent, "col", flip, cols))
        if hop:
            sent = joined(cot_pieces, (token_pieces[hop],))
            cot_pieces.append(swap(sent, "col", flips[hop - 1], cols))
        if hop < 2:
            load(wanted[5 * hop : 5 + 3 * hop])
        order += [q ^ flip for q in order]
    token_shards = token_pieces, order
    cot_sent = joined(cot_pieces, (token_pieces[-1],))

    keep, sent = project(w_in, token_shards, first, wanted[8:10])
    got = other_core(sent)
    here, sent = project(w_in, token_shards, second + own, [])
    got_here, came = other_core(sent), across(added([keep, got])[0], 0, rows)
    cot_pieces.append(swap(joined([cot_sent]), "col", flips[-1], cols))
    cot_shards = cot_pieces, order
    load(wanted[10:12])
    sent = one_block([(here, 0), (got_here, 0), (came, 1)])
    terms = [(here, 1), (got_here, 1), (came, 0), (across(sent, 1, rows), 0)]

    keep, sent = project(w_out, cot_shards, first, wanted[12:14])
    got = other_core(sent)
    hidden, act = activate(terms)
    came = across(added([keep, got])[0], 0, rows)
    keep, sent = project(w_out, cot_shards, second, wanted[14:])
    got = other_core(sent)
    stack = doubled(act, 0, PART_COST)
    own_keep, sent = project(w_out, cot_shards, own, [])
    own_got = other_core(sent)
    sent = one_block([(keep, 0), (got, 0), (came, 1)])
    last = across(sent, 1, rows)
    grad_hidden = activate_back(hidden, [(own_keep, 0), (own_got, 0), (came, 0), (last, 0)])
    stack = doubled(stack, 1)
    act = stack, other_core(stack)
    (grad_w_out,) = weight_grad(w_out, act[:1], cot_shards, (0,))
    back_stack = doubled(grad_hidden, 0)

    even, odd = range(0, cols, 2), range(1, cols, 2)
    keep, sent, grad_w_out = weight_grad(
        w_out, act, cot_shards, (1,), cols, (even, odd), grad_w_out
    )
    got = swap(sent, "col", 1, cols)
    back_stack = doubled(back_stack, 1)
    grad_hidden = back_stack, other_core(back_stack)
    so_far = block_sum(w_in, grad_hidden[:1], (0,), cols, [])
    token_parts = block_sum(w_in, grad_hidden[1:], (1,), cols, [[q] for q in range(cols)], so_far)
    layer_out, *sums = summed_half(keep, got, len(even))
    layer_parts = [swap(part, "col", q, cols) for part, q in zip(sums, even[1:])]
    token_parts = exchange_col(token_parts, cols)
    (grad_w_in,) = weight_grad(w_in, grad_hidden, token_shards)
    layer_out, grad_tokens = added([layer_out, *layer_parts], token_parts, space="window")
    return (layer_out, grad_tokens, grad_w_in, grad_w_out)


def collective(tokens, cotangent, w_in, w_out):
    token_full = lax.all_gather(tokens, "col", axis=0, tiled=True)
    cot_full = lax.all_gather(cotangent, "col", axis=0, tiled=True)

    def over(value, axis):
        return lax.psum_scatter(value.astype(BF16), axis, scatter_dimension=0, tiled=True)

    hidden = over(dot(token_full, w_in, 1, 0), "row").astype(F32)
    grad_act = over(dot(cot_full, w_out, 1, 1), "row").astype(F32)
    act = lax.all_gather(gelu_fn(hidden).astype(BF16), "row", axis=0, tiled=True)
    grad_hidden = lax.all_gather(gelu_back(hidden, grad_act), "row", axis=0, tiled=True)
    layer_out = over(dot(act, w_out, 1, 0), "col")
    grad_tokens = over(dot(grad_hidden, w_in, 1, 1), "col")
    grad_w_in = dot(token_full, grad_hidden, 0, 0).astype(BF16)
    grad_w_out = dot(act, cot_full, 0, 0).astype(BF16)
    return (layer_out, grad_tokens, grad_w_in, grad_w_out)


def solution(mesh):
    rows, cols = mesh.shape["row"], mesh.shape["col"]

    def shards(tokens, cotangent, w_in, w_out):
        powers = rows & (rows - 1) == 0 and cols & (cols - 1) == 0
        if powers and rows == 8 and cols > 2 and w_in.shape[1] % (rows * 128) == 0:
            return blocked(rows, cols, tokens, cotangent, w_in, w_out)
        return collective(tokens, cotangent, w_in, w_out)

    return jax.shard_map(
        shards,
        mesh=mesh,
        in_specs=(P("col", "row"), P("col", "row"), P("row", "col"), P("col", "row")),
        out_specs=(P("col", "row"), P("col", "row"), P("row", "col"), P("col", "row")),
        check_vma=False,
    )
```

```python
import functools

import jax
import jax.numpy as jnp
from jax import lax
from jax.experimental import pallas as pl
from jax.experimental.pallas import tpu as pltpu
from jax.sharding import PartitionSpec as P

BF16 = jnp.bfloat16
F32 = jnp.float32
VMEM_LIMIT = 10 * 1024 * 1024
WRITES = 6
READ_CUTS, WRITE_CUTS = 4, 3
PART_COST = 6 * 10**9
BACK_COST = 6 * 10**9


def gelu_fn(value):
    return jax.nn.gelu(value, approximate=True)


def gelu_back(hidden, grad_act):
    unused, pullback = jax.vjp(gelu_fn, hidden)
    return pullback(grad_act)[0].astype(BF16)


def swap(value, axis, flip, count):
    return lax.ppermute(value, axis, [(i, i ^ flip) for i in range(count)])


def reverse(p, bits):
    return sum(((p >> j) & 1) << (bits - 1 - j) for j in range(bits))


def across(value, step, rows):
    bits = rows.bit_length() - 2
    flips = [2 << (bits - 1 - step if i & 1 else step) for i in range(rows)]
    return lax.ppermute(value, "row", [(i, i ^ flips[i]) for i in range(rows)])


def dot(left, right, left_dim, right_dim):
    return lax.dot_general(
        left, right, (((left_dim,), (right_dim,)), ((), ())), preferred_element_type=F32
    )


LAST = []


def call(kernel, arrays, outs, flops, moved, after=(), scratch=(), in_place=False):
    unread, count = [*LAST, *after], len(arrays)

    def body(*refs):
        kernel(*refs[:count], *refs[count + len(unread) :])

    specs = {
        "smem": pl.BlockSpec(memory_space=pltpu.SMEM),
        "vmem": pl.BlockSpec(memory_space=pltpu.VMEM),
        "hbm": pl.BlockSpec(memory_space=pl.ANY),
        "window": pl.BlockSpec(),
    }
    operands = []
    for space, value in arrays:
        if space != "smem":
            value = pltpu.with_memory_space_constraint(
                value, pltpu.HBM if space == "hbm" else pltpu.VMEM
            )
        operands.append(value)
    results = pl.pallas_call(
        body,
        in_specs=[specs[space] for space, value in arrays]
        + [pl.BlockSpec(memory_space=pl.ANY)] * len(unread),
        out_specs=[specs[space] for space, value in outs],
        scratch_shapes=list(scratch),
        input_output_aliases={count - 1: len(outs) - 1} if in_place else {},
        out_shape=[
            pltpu.VMEM(shape, dtype) if space == "vmem" else jax.ShapeDtypeStruct(shape, dtype)
            for space, (shape, dtype) in outs
        ],
        compiler_params=pltpu.CompilerParams(vmem_limit_bytes=VMEM_LIMIT),
        cost_estimate=pl.CostEstimate(flops=flops, bytes_accessed=moved, transcendentals=0),
    )(*operands, *unread)
    last = results[-1]
    if outs[-1][0] != "vmem":
        last = pltpu.with_memory_space_constraint(last, pltpu.HBM)
    LAST[:] = [last]
    return results


def in_vmem(values):
    return [("vmem", value) for value in values]


def join(pieces, out):
    at = 0
    for piece in pieces:
        out[at : at + piece.shape[0], :] = piece[...]
        at += piece.shape[0]


def place(pieces, order, out):
    size, order = pieces[0].shape[0], list(order)
    for piece in pieces:
        for at in range(0, piece.shape[0], size):
            to = order.pop(0) * size
            out[to : to + size, :] = piece[at : at + size, :]


def joined(pieces, after=(), flops=0):
    rows = sum(piece.shape[0] for piece in pieces)

    def kernel(*refs):
        join(refs[: len(pieces)], refs[-1])

    return call(
        kernel, in_vmem(pieces), [("vmem", ((rows, pieces[0].shape[1]), BF16))], flops, 0, after
    )[0]


class Weight:
    def __init__(self, me, value, rows, by_rows):
        self.me, self.value, self.by_rows = me, value, by_rows
        self.bits = rows.bit_length() - 2
        self.block = value.shape[0 if by_rows else 1] // rows
        self.width = value.shape[1 if by_rows else 0]
        self.shape = (self.block, self.width) if by_rows else (self.width, self.block)
        self.held = {}

    def part(self, ref, me, key):
        p, odd = key
        chip = p + (me & 1) * (reverse(p, self.bits) - p)
        at = (me ^ (2 * chip + odd)) * self.block
        at = pl.ds(pl.multiple_of(at, 128), self.block)
        return ref.at[at, :] if self.by_rows else ref.at[:, at]


def cut(ref, i, cuts):
    size = ref.shape[0] // cuts
    return ref.at[i * size : (i + 1) * size, :]


class Coming:
    def __init__(self, blocks):
        self.blocks = blocks
        self.weights = list(dict.fromkeys(weight for weight, key in blocks))
        self.count = len(blocks) * READ_CUTS
        self.inputs = [("hbm", weight.value) for weight in self.weights]
        self.outs = [("vmem", (weight.shape, BF16)) for weight, key in blocks]
        self.scratch = [pltpu.SemaphoreType.DMA((self.count,))] if blocks else []

    def copies(self, sources, helds, arrived, me):
        return [
            pltpu.make_async_copy(
                cut(weight.part(sources[self.weights.index(weight)], me, key), i, READ_CUTS),
                cut(held, i, READ_CUTS),
                arrived.at[n * READ_CUTS + i],
            )
            for n, ((weight, key), held) in enumerate(zip(self.blocks, helds))
            for i in range(READ_CUTS)
        ]

    def arrive(self, helds):
        for (weight, key), held in zip(self.blocks, helds):
            weight.held[key] = held


def load(blocks, after=()):
    coming = Coming(blocks)
    n = len(coming.inputs)

    def kernel(me_ref, *refs):
        copies = coming.copies(refs[:n], refs[n:-1], refs[-1], me_ref[0])
        for copy in copies:
            copy.start()
        for copy in copies:
            copy.wait()

    me = blocks[0][0].me
    coming.arrive(
        call(kernel, [("smem", me), *coming.inputs], coming.outs, 0, 0, after, coming.scratch)
    )


def project(weight, shards, positions, blocks, after=(), flops=0):
    pieces, order = shards
    coming = Coming(blocks)
    tokens, n = sum(piece.shape[0] for piece in pieces), len(positions)
    block, by_rows = weight.block, weight.by_rows
    keys = [(reverse(p, weight.bits), 1) for p in positions] + [(p, 0) for p in positions]

    def kernel(me_ref, *refs):
        piece_refs, refs = refs[: len(pieces)], refs[len(pieces) :]
        parts, refs = refs[: 2 * n], refs[2 * n :]
        sources, refs = refs[: len(coming.inputs)], refs[len(coming.inputs) :]
        keep, send, refs = refs[0], refs[1], refs[2:]
        left, copies = refs[len(blocks)], []
        if blocks:
            copies = coming.copies(sources, refs[: len(blocks)], refs[-1], me_ref[0])
        for copy in copies:
            copy.start()

        @pl.when(me_ref[0] >= 0)
        def _():
            place(piece_refs, order, left)
            for i, part in enumerate(parts):
                out = dot(left[...], part[...], 1, 1 if by_rows else 0).astype(BF16)
                (send if i < n else keep)[i % n] = out

        for copy in copies:
            copy.wait()

    keep, send, *helds = call(
        kernel,
        [("smem", weight.me)]
        + in_vmem(pieces)
        + in_vmem([weight.held[key] for key in keys])
        + coming.inputs,
        [("vmem", ((n, tokens, block), BF16))] * 2 + coming.outs,
        flops,
        0,
        after,
        [pltpu.VMEM((tokens, weight.width), BF16)] + coming.scratch,
    )
    coming.arrive(helds)
    return keep, send


def block_sum(weight, stacks, odds, cols, groups, so_far=()):
    width, by_rows, block = weight.width, weight.by_rows, weight.block
    chips = len(weight.held) // 2
    tokens = stacks[0].shape[0] // chips
    n, size = len(stacks), tokens // cols
    parts = [
        weight.held[(reverse(p, weight.bits) if odd else p, odd)]
        for odd in odds
        for p in range(chips)
    ]

    def kernel(*refs):
        stack_refs, part_refs, refs = refs[:n], refs[n : n + len(parts)], refs[n + len(parts) :]
        before, outs, total = refs[: len(so_far)], refs[len(so_far) : -1], refs[-1]
        for ref in before:
            total[...] = ref[...]
        for i, part in enumerate(part_refs):
            p = i % chips
            value = stack_refs[i // chips][p * tokens : (p + 1) * tokens, :]
            term = dot(value, part[...], 1, 0 if by_rows else 1)
            total[...] = total[...] + term if i or before else term
        if not groups:
            outs[0][...] = total[...]
        for group, out in zip(groups, outs):
            for i, q in enumerate(group):
                out[i * size : (i + 1) * size, :] = total[q * size : (q + 1) * size, :].astype(BF16)

    return call(
        kernel,
        in_vmem(stacks) + in_vmem(parts) + in_vmem(so_far),
        [("vmem", ((len(group) * size, width), BF16)) for group in groups]
        or [("vmem", ((tokens, width), F32))],
        2 * tokens * width * block * chips * n,
        2 * width * block * chips * n,
        (),
        [pltpu.VMEM((tokens, width), F32)],
    )


def block_keys(weight):
    chips = len(weight.held) // 2
    return [(reverse(p, weight.bits) if odd else p, odd) for odd in range(2) for p in range(chips)]


def weight_grad(weight, stacks, shards, odds=(0, 1), cols=1, groups=(), into=None):
    pieces, order = shards
    width, by_rows, block = weight.width, weight.by_rows, weight.block
    chips, n = len(weight.held) // 2, len(stacks)
    tokens = stacks[0].shape[0] // chips
    halves = 2
    size = (block if by_rows else width) // halves
    keys = block_keys(weight)
    order_of = [odd * chips + p for p in range(chips) for odd in odds]
    parts = [weight.held[key] for key in keys] if groups else []

    def kernel(me_ref, *refs):
        stack_refs, refs = refs[:n], refs[n:]
        piece_refs, refs = refs[: len(pieces)], refs[len(pieces) :]
        part_refs, refs = refs[: len(parts)], refs[len(parts) + (into is not None) :]
        sums, (grad, other, turned, ready, sent, total) = refs[: len(groups)], refs[len(groups) :]
        place(piece_refs, order, other)
        if not by_rows:
            turned[...] = other[...].T
        me = me_ref[0]

        def value(i):
            return stack_refs[i // chips], slice(i % chips * tokens, (i % chips + 1) * tokens)

        def writes(step):
            to = weight.part(grad, me, keys[order_of[step // halves]])
            at = step % halves * size
            to = to.at[at : at + size, :]
            slot = step % WRITES
            return [
                pltpu.make_async_copy(
                    cut(ready.at[slot], i, WRITE_CUTS), cut(to, i, WRITE_CUTS), sent.at[slot, i]
                )
                for i in range(WRITE_CUTS)
            ]

        def product(step):
            stack, of = value(order_of[step // halves])
            at = slice(step % halves * size, (step % halves + 1) * size)
            if by_rows:
                out = dot(stack[of, at], other[...], 0, 0)
            else:
                out = dot(turned[at, :], stack[of, :], 1, 0)
            ready[step % WRITES] = out.astype(BF16)

        steps = len(order_of) * halves
        for step in range(steps):
            if step >= WRITES:
                for write in writes(step - WRITES):
                    write.wait()
            if by_rows:
                product(step)
            else:
                pl.when(me >= 0)(functools.partial(product, step))
            for write in writes(step):
                write.start()

        @pl.when(me >= 0)
        def _():
            for i, part in enumerate(part_refs):
                stack, of = value(i)
                term = dot(stack[of, :], part[...], 1, 0)
                total[...] = term if i == 0 else total[...] + term
            rows = tokens // cols
            for group, out in zip(groups, sums):
                for i, q in enumerate(group):
                    out[i * rows : (i + 1) * rows, :] = total[q * rows : (q + 1) * rows, :].astype(BF16)

        for step in range(max(0, steps - WRITES), steps):
            for write in writes(step):
                write.wait()

    return call(
        kernel,
        [("smem", weight.me)]
        + in_vmem(stacks)
        + in_vmem(pieces)
        + in_vmem(parts)
        + ([("hbm", into)] if into is not None else []),
        [("vmem", ((len(group) * tokens // cols, width), BF16)) for group in groups]
        + [("hbm", (weight.value.shape, BF16))],
        2 * tokens * width * block * len(order_of) if 1 in odds else 0,
        2 * width * block * len(order_of) if 1 in odds else 0,
        (),
        [
            pltpu.VMEM((tokens, width), BF16),
            pltpu.VMEM((width, tokens), BF16),
            pltpu.VMEM((WRITES, size, width if by_rows else block), BF16),
            pltpu.SemaphoreType.DMA((WRITES, WRITE_CUTS)),
            pltpu.VMEM((tokens, width), F32),
        ],
        into is not None,
    )


def summed_half(keep, got, count, after=()):
    size = keep.shape[0] // count

    def kernel(keep_ref, got_ref, *outs):
        for i, out in enumerate(outs):
            at = slice(i * size, (i + 1) * size)
            total = keep_ref[at, :].astype(F32) + got_ref[at, :].astype(F32)
            out[...] = total.astype(out.dtype)

    shape = (size, keep.shape[1])
    outs = [("vmem", (shape, F32))] + [("vmem", (shape, BF16))] * (count - 1)
    return call(kernel, in_vmem([keep, got]), outs, 0, 0, after)


def added(*sums, space="vmem"):
    def kernel(*refs):
        refs, outs = refs[: -len(sums)], refs[-len(sums) :]
        for terms, out in zip(sums, outs):
            out[...] = sum(ref[...].astype(F32) for ref in refs[: len(terms)]).astype(BF16)
            refs = refs[len(terms) :]

    arrays = in_vmem([term for terms in sums for term in terms])
    return call(kernel, arrays, [(space, (terms[0].shape, BF16)) for terms in sums], 0, 0)


def block_of(terms):
    def total(refs):
        return sum(ref[block].astype(F32) for ref, (array, block) in zip(refs, terms))

    return total


def one_block(terms, dtype=BF16, flops=0):
    def kernel(*refs):
        refs[-1][0] = block_of(terms)(refs).astype(dtype)

    shape = (1, *terms[0][0].shape[1:])
    arrays = in_vmem([array for array, block in terms])
    return call(kernel, arrays, [("vmem", (shape, dtype))], flops, 0)[0]


def activate(terms):
    def kernel(*refs):
        total = block_of(terms)(refs)
        refs[-2][...] = total
        refs[-1][...] = gelu_fn(total).astype(BF16)

    shape = terms[0][0].shape[1:]
    outs = [("vmem", (shape, F32)), ("vmem", (shape, BF16))]
    return call(kernel, in_vmem([array for array, block in terms]), outs, PART_COST, 0)


def activate_back(hidden, terms):
    def kernel(hidden_ref, *refs):
        refs[-1][...] = gelu_back(hidden_ref[...], block_of(terms)(refs))

    arrays = [hidden] + [array for array, block in terms]
    return call(kernel, in_vmem(arrays), [("vmem", (hidden.shape, BF16))], BACK_COST, 0)[0]


def exchange_col(parts, cols):
    return [parts[0]] + [swap(parts[q], "col", q, cols) for q in range(cols - 1, 0, -1)]


def blocked(rows, cols, tokens, cotangent, w_in, w_out):
    LAST.clear()
    me = lax.axis_index("row").astype(jnp.int32).reshape(1)
    w_in, w_out = Weight(me, w_in, rows, False), Weight(me, w_out, rows, True)
    first, second, own = [1, 3], [2], [0]

    def keys(positions):
        return [(reverse(p, 2), 1) for p in positions] + [(p, 0) for p in positions]

    def other_core(value):
        return swap(value, "row", 1, rows)

    def doubled(stack, step, flops=0):
        return joined([stack, across(stack, step, rows)], (), flops)

    wanted = [(w, key) for w in (w_in, w_out) for part in (first, second, own) for key in keys(part)]

    flips = [1 << bit for bit in range(cols.bit_length() - 1)][::-1]
    token_pieces, cot_pieces, order = [tokens], [cotangent], [0]
    for hop, flip in enumerate(flips):
        sent = joined(token_pieces) if hop else tokens
        token_pieces.append(swap(sent, "col", flip, cols))
        if hop:
            sent = joined(cot_pieces, (token_pieces[hop],))
            cot_pieces.append(swap(sent, "col", flips[hop - 1], cols))
        if hop < 2:
            load(wanted[5 * hop : 5 + 3 * hop])
        order += [q ^ flip for q in order]
    token_shards = token_pieces, order
    cot_sent = joined(cot_pieces, (token_pieces[-1],))

    keep, sent = project(w_in, token_shards, first, wanted[8:10])
    got = other_core(sent)
    here, sent = project(w_in, token_shards, second + own, [])
    got_here, came = other_core(sent), across(added([keep, got])[0], 0, rows)
    cot_pieces.append(swap(joined([cot_sent]), "col", flips[-1], cols))
    cot_shards = cot_pieces, order
    load(wanted[10:12])
    sent = one_block([(here, 0), (got_here, 0), (came, 1)])
    terms = [(here, 1), (got_here, 1), (came, 0), (across(sent, 1, rows), 0)]

    keep, sent = project(w_out, cot_shards, first, wanted[12:14], (), PART_COST)
    got = other_core(sent)
    hidden, act = activate(terms)
    came = across(added([keep, got])[0], 0, rows)
    keep, sent = project(w_out, cot_shards, second, wanted[14:])
    got = other_core(sent)
    stack = doubled(act, 0, PART_COST)
    own_keep, sent = project(w_out, cot_shards, own, [])
    own_got = other_core(sent)
    sent = one_block([(keep, 0), (got, 0), (came, 1)])
    last = across(sent, 1, rows)
    grad_hidden = activate_back(hidden, [(own_keep, 0), (own_got, 0), (came, 0), (last, 0)])
    stack = doubled(stack, 1)
    act = stack, other_core(stack)
    back_stack = doubled(grad_hidden, 0, PART_COST)

    even, odd = range(0, cols, 2), range(1, cols, 2)
    keep, sent, grad_w_out = weight_grad(w_out, act, cot_shards, (0, 1), cols, (even, odd))
    got = swap(sent, "col", 1, cols)
    back_stack = doubled(back_stack, 1)
    grad_hidden = back_stack, other_core(back_stack)
    so_far = block_sum(w_in, grad_hidden[:1], (0,), cols, [])
    token_parts = block_sum(w_in, grad_hidden[1:], (1,), cols, [[q] for q in range(cols)], so_far)
    layer_out, *sums = summed_half(keep, got, len(even))
    layer_parts = [swap(part, "col", q, cols) for part, q in zip(sums, even[1:])]
    token_parts = exchange_col(token_parts, cols)
    (grad_w_in,) = weight_grad(w_in, grad_hidden, token_shards)
    layer_out, grad_tokens = added([layer_out, *layer_parts], token_parts, space="window")
    return (layer_out, grad_tokens, grad_w_in, grad_w_out)


def collective(tokens, cotangent, w_in, w_out):
    token_full = lax.all_gather(tokens, "col", axis=0, tiled=True)
    cot_full = lax.all_gather(cotangent, "col", axis=0, tiled=True)

    def over(value, axis):
        return lax.psum_scatter(value.astype(BF16), axis, scatter_dimension=0, tiled=True)

    hidden = over(dot(token_full, w_in, 1, 0), "row").astype(F32)
    grad_act = over(dot(cot_full, w_out, 1, 1), "row").astype(F32)
    act = lax.all_gather(gelu_fn(hidden).astype(BF16), "row", axis=0, tiled=True)
    grad_hidden = lax.all_gather(gelu_back(hidden, grad_act), "row", axis=0, tiled=True)
    layer_out = over(dot(act, w_out, 1, 0), "col")
    grad_tokens = over(dot(grad_hidden, w_in, 1, 1), "col")
    grad_w_in = dot(token_full, grad_hidden, 0, 0).astype(BF16)
    grad_w_out = dot(act, cot_full, 0, 0).astype(BF16)
    return (layer_out, grad_tokens, grad_w_in, grad_w_out)


def solution(mesh):
    rows, cols = mesh.shape["row"], mesh.shape["col"]

    def shards(tokens, cotangent, w_in, w_out):
        powers = rows & (rows - 1) == 0 and cols & (cols - 1) == 0
        if powers and rows == 8 and cols > 2 and w_in.shape[1] % (rows * 128) == 0:
            return blocked(rows, cols, tokens, cotangent, w_in, w_out)
        return collective(tokens, cotangent, w_in, w_out)

    return jax.shard_map(
        shards,
        mesh=mesh,
        in_specs=(P("col", "row"), P("col", "row"), P("row", "col"), P("col", "row")),
        out_specs=(P("col", "row"), P("col", "row"), P("row", "col"), P("col", "row")),
        check_vma=False,
    )
```
